32 devices in a mesh: img: 8 (over z, y), ch: 4 (over x, core).
Axes of the slice: x: 2, y: 2, z: 4, core: 2. Of those that a mesh axis runs over, the one named last changes fastest.
Arguments:
- feats: bfloat16 [8, 24, 24, 512], P('img', None, None, 'ch'), may hold values from -6 to 6
- shared_w: bfloat16 [2, 2, 3, 3, 512, 512], P(None, None, None, None, None, 'ch'), may hold values from -0.09375 to 0.09375
- task_w: bfloat16 [2, 3, 3, 3, 512, 512], P(None, None, None, None, None, 'ch'), may hold values from -0.09375 to 0.09375
- down_w: bfloat16 [2, 3, 512, 128], P(None, None, 'ch'), may hold values from -0.25 to 0.25
- up_w: bfloat16 [2, 3, 128, 512], P(None, None, None, 'ch'), may hold values from -0.5 to 0.5
- norm_gain: float32 [2, 8, 512], P(None, None, 'ch'), may hold values from 0.1 to 1.9
- norm_shift: float32 [2, 8, 512], P(None, None, 'ch'), may hold values from -3 to 3
- bottle_gain: float32 [2, 3, 128], replicated, may hold values from 0.1 to 1.9
- bottle_shift: float32 [2, 3, 128], replicated, may hold values from -3 to 3
- seg_mask: int32 [8, 6, 6], P('img'), may hold values 0 or 1
- depth_mask: int32 [8, 6, 6], P('img'), may hold values 0 or 1
- shared_cot: bfloat16 [8, 6, 6, 512], P('img', None, None, 'ch'), may hold values from -6 to 6
- task_cot: bfloat16 [3, 8, 6, 6, 512], P(None, 'img', None, None, 'ch'), may hold values from -6 to 6
Outputs:
- shared_out: bfloat16 [8, 6, 6, 512], P('img', None, None, 'ch')
- task_out: bfloat16 [3, 8, 6, 6, 512], P(None, 'img', None, None, 'ch')
- feats_grad: float32 [8, 24, 24, 512], P('img', None, None, 'ch')
- shared_w_grad: float32 [2, 2, 3, 3, 512, 512], P(None, None, None, None, 'img', 'ch')
- task_w_grad: float32 [2, 3, 3, 3, 512, 512], P(None, None, None, None, 'img', 'ch')
- down_w_grad: float32 [2, 3, 512, 128], P(None, None, 'ch')
- up_w_grad: float32 [2, 3, 128, 512], P(None, None, None, 'ch')
- norm_gain_grad: float32 [2, 8, 512], P(None, None, 'ch')
- norm_shift_grad: float32 [2, 8, 512], P(None, None, 'ch')
- bottle_gain_grad: float32 [2, 3, 128], replicated
- bottle_shift_grad: float32 [2, 3, 128], replicated
The draws below stay inside these ranges and needn't reach their ends.
Inputs may be any that keep to these rules, and one draw needn't show every extreme that they name: `seg_mask`: a pixel's mask is 0 or 1. `depth_mask`: a pixel's mask is 0 or 1.
All inputs are finite; a program needn't handle non-finite values. No bound on the sum of `seg_mask` or of `depth_mask` on one device may be relied on, other than what follows from the above.
Results may differ from the reference program's by a relative error of at most 0.035.
Values may be sent and summed in bfloat16 or wider, within the bound.
No kernel may reach another device: no remote copies, remote signals or barrier semaphores. Data moves between devices by JAX's collectives and lax.ppermute only.
A program may use at most 192 MiB of HBM per device.

```python
import jax
import jax.numpy as jnp
from jax import lax

C = 512
BOT = 128
TASKS = 3
LAYERS = 2
H0 = 24
W0 = 24
IMAGES = 8
H2 = 6
W2 = 6


def with_ends(entries, stream_key, least, high):
    longest = entries.shape.index(max(entries.shape))
    spots = []
    for shift in (0, 1):
        where = [jax.random.randint(jax.random.fold_in(stream_key, axis), (), 0, length) for axis, length in enumerate(entries.shape)]
        where[longest] = (where[longest] + shift) % entries.shape[longest]
        spots.append(tuple(where))
    return entries.at[spots[0]].set(least).at[spots[1]].set(high)


def levels(own_key, dims, split, low, top_value):
    loudness = 1.0
    for dim, parts in split:
        heights = jax.random.uniform(jax.random.fold_in(jax.random.fold_in(own_key, 6), dim), (parts,), jnp.float32, low / len(split), top_value / len(split))
        loudness = loudness * jnp.repeat(jnp.exp(heights), dims[dim] // parts).reshape((-1,) + (1,) * (len(dims) - 1 - dim))
    return loudness


def centred(stream_key, extent, deviation, bound, shards=(), dtype=jnp.bfloat16):
    values = jax.random.normal(stream_key, extent, jnp.float32) * deviation
    if len(shards) > 0:
        values = levels(stream_key, extent, shards, -0.22, 0.18) * values
    return jnp.clip(values, min=-bound, max=bound).astype(dtype)


def setup_inputs(seed: int = 0) -> dict:
    streams_of = jax.random.split(jax.random.key(seed), 14)
    feats = centred(streams_of[0], (IMAGES, H0, W0, C), 1.0, 6.0, ((0, 8), (3, 4)))
    shared_w = centred(streams_of[1], (LAYERS, 2, 3, 3, C, C), (9 * C) ** -0.5, 0.09375, ((5, 4),))
    task_w = centred(streams_of[2], (LAYERS, TASKS, 3, 3, C, C), (9 * C) ** -0.5, 0.09375, ((5, 4),))
    down_w = centred(streams_of[3], (LAYERS, TASKS, C, BOT), C ** -0.5, 0.25, ((2, 4),))
    up_w = centred(streams_of[4], (LAYERS, TASKS, BOT, C), BOT ** -0.5, 0.5, ((3, 4),))
    norm_gain = jnp.clip(1.0 + 0.18 * jax.random.normal(streams_of[5], (LAYERS, 8, C), jnp.float32), 0.1, 1.9)
    norm_shift = centred(streams_of[6], (LAYERS, 8, C), 0.5, 3.0, ((2, 4),), jnp.float32)
    bottle_gain = jnp.clip(1.0 + 0.18 * jax.random.normal(streams_of[7], (LAYERS, TASKS, BOT), jnp.float32), 0.1, 1.9)
    bottle_shift = centred(streams_of[8], (LAYERS, TASKS, BOT), 0.5, 3.0, (), jnp.float32)
    seg_mask = with_ends((jax.random.randint(streams_of[9], (IMAGES, H2, W2), 0, 4) < 3).astype(jnp.int32), jax.random.fold_in(streams_of[9], 1), 0, 1)
    depth_mask = with_ends((jax.random.randint(streams_of[10], (IMAGES, H2, W2), 0, 5) < 4).astype(jnp.int32), jax.random.fold_in(streams_of[10], 1), 0, 1)
    shared_cot = centred(streams_of[11], (IMAGES, H2, W2, C), 1.0, 6.0, ((0, 8), (3, 4)))
    task_cot = centred(streams_of[12], (TASKS, IMAGES, H2, W2, C), 1.0, 6.0, ((1, 8), (4, 4)))
    return {"feats": feats, "shared_w": shared_w, "task_w": task_w, "down_w": down_w, "up_w": up_w, "norm_gain": norm_gain, "norm_shift": norm_shift, "bottle_gain": bottle_gain, "bottle_shift": bottle_shift, "seg_mask": seg_mask, "depth_mask": depth_mask, "shared_cot": shared_cot, "task_cot": task_cot}


EPSILON = 1e-05
exact_mode = lax.Precision.HIGHEST

@jax.custom_vjp
def low(v):
    return lax.optimization_barrier(v.astype(jnp.bfloat16)).astype(jnp.float32)

@jax.custom_vjp
def low_back(v):
    return v

def low_keep(v):
    return (low(v), None)

def low_pass(kept, grad):
    return (grad,)

def back_keep(v):
    return (v, None)

def back_low(kept, grad):
    return (low(grad),)
low.defvjp(low_keep, low_pass)
low_back.defvjp(back_keep, back_low)

def conv_same(inputs, kernel):
    return lax.conv_general_dilated(inputs, kernel, (1, 1), 'SAME', dimension_numbers=('NHWC', 'HWIO', 'NHWC'), precision=exact_mode)

def batch_norm(values, gain_rows, offset, norm_axes):
    center = lax.optimization_barrier(jnp.mean(values, axis=norm_axes, keepdims=True))
    spread = lax.optimization_barrier(jnp.mean(values * values, axis=norm_axes, keepdims=True)) - center * center
    return (values - center) * lax.rsqrt(spread + EPSILON) * gain_rows + offset

def pooled(values):
    dims_in = values.shape
    blocks = values.reshape(dims_in[:-3] + (dims_in[-3] // 2, 2, dims_in[-2] // 2, 2, dims_in[-1]))
    return lax.optimization_barrier(jnp.mean(blocks, axis=(-4, -2)))

def as_tasks(per_task):
    return per_task[:, None, None, None, :]

def encoder_layer(inputs, previous, shared_k, task_k, down_k, up_k, gain_rows, offset, bottle_g, bottle_s):
    first_in = low(inputs)
    act_one = jax.nn.silu(batch_norm(low_back(conv_same(first_in, shared_k[0])), gain_rows[0], offset[0], (0, 1, 2)))
    low_one = low(act_one)
    act_two = jax.nn.silu(batch_norm(low_back(conv_same(low_one, shared_k[1])), gain_rows[1], offset[1], (0, 1, 2)))
    if previous is None:
        bottle = jnp.einsum('nhwc,tcb->tnhwb', low_one, down_k, precision=exact_mode)
    else:
        attend = low(act_one[None] + previous)
        bottle = jnp.einsum('tnhwc,tcb->tnhwb', attend, down_k, precision=exact_mode)
    bottle = low_back(bottle)
    hidden = low(jax.nn.silu(batch_norm(bottle, as_tasks(bottle_g), as_tasks(bottle_s), (1, 2, 3))))
    expand = low_back(jnp.einsum('tnhwb,tbc->tnhwc', hidden, up_k, precision=exact_mode))
    gating = jax.nn.sigmoid(batch_norm(expand, as_tasks(gain_rows[5:8]), as_tasks(offset[5:8]), (1, 2, 3)))
    masked = low(gating * act_two[None])
    task_conv = low_back(jax.vmap(conv_same)(masked, task_k))
    task_act = jax.nn.silu(batch_norm(task_conv, as_tasks(gain_rows[2:5]), as_tasks(offset[2:5]), (1, 2, 3)))
    return (pooled(act_two), pooled(task_act))

def reference(feats, shared_w, task_w, down_w, up_w, norm_gain, norm_shift, bottle_gain, bottle_shift, seg_mask, depth_mask, shared_cot, task_cot):

    def forward(inputs, shared_all, task_all, down_all, up_all, gain_all, shift_all, bgain_all, bshift_all):
        previous = None
        for layer_no in range(LAYERS):
            inputs, previous = encoder_layer(inputs, previous, shared_all[layer_no], task_all[layer_no], down_all[layer_no], up_all[layer_no], gain_all[layer_no], shift_all[layer_no], bgain_all[layer_no], bshift_all[layer_no])
        return (inputs, previous)
    outputs, pullback = jax.vjp(forward, feats.astype(jnp.float32), shared_w.astype(jnp.float32), task_w.astype(jnp.float32), down_w.astype(jnp.float32), up_w.astype(jnp.float32), norm_gain, norm_shift, bottle_gain, bottle_shift)
    scales = jnp.stack([seg_mask, depth_mask, jnp.ones_like(seg_mask)]).astype(jnp.float32)
    gradients = pullback((shared_cot.astype(jnp.float32), task_cot.astype(jnp.float32) * scales[..., None]))
    return (outputs[0].astype(jnp.bfloat16), outputs[1].astype(jnp.bfloat16), gradients[0], gradients[1], gradients[2], gradients[3], gradients[4], gradients[5], gradients[6], gradients[7], gradients[8])
```

```python
import functools

import jax
import jax.numpy as jnp
from jax import lax
from jax.experimental import pallas as pl
from jax.experimental.pallas import tpu as pltpu
from jax.sharding import PartitionSpec as P

EPSILON = 1e-05
F32 = jnp.float32
LOW = jnp.bfloat16
VMEM_LIMIT = 56 * 2**20


def sigmoid(v):
    return 0.5 * jnp.tanh(0.5 * v) + 0.5


def silu_slope(v, s):
    return s * (1.0 + v * (1.0 - s))


def dot(a, b):
    return lax.dot_general(a, b, (((1,), (0,)), ((), ())), preferred_element_type=F32)


def dot_nt(a, b):
    return lax.dot_general(a, b, (((1,), (1,)), ((), ())), preferred_element_type=F32)


def dot_tn(a, b):
    return lax.dot_general(a, b, (((0,), (0,)), ((), ())), preferred_element_type=F32)


def sums(v):
    return jnp.sum(v, axis=0, keepdims=True)


def column_of(shape, width):
    place = lax.broadcasted_iota(jnp.int32, shape, 0)
    row = (place * (2731 if width == 24 else 5462)) >> 16
    return place - row * width


def move_columns(v, step, width):
    if step == 0:
        return v
    column = column_of(v.shape, width)
    keep = column < width - 1 if step == 1 else column > 0
    return jnp.where(keep, pltpu.roll(v, (-step) % v.shape[0], 0), 0.0)


def move_rows(v, step, width):
    if step == 0:
        return v
    size = v.shape[0]
    place = lax.broadcasted_iota(jnp.int32, v.shape, 0)
    keep = place < size - width if step == 1 else place >= width
    return jnp.where(keep, pltpu.roll(v, (-step * width) % size, 0), 0.0)


def centre(total, count):
    mean = total[0:1] / count
    spread = total[1:2] / count - mean * mean
    return mean, lax.rsqrt(spread + EPSILON)


def place_blocks(ch_ref, blocks, full_ref):
    own = ch_ref[0]
    for k, block in enumerate(blocks):
        start = pl.multiple_of((own ^ k) * 128, 128)
        full_ref[:, pl.ds(start, 128)] = block[...]


def conv(values, taps_ref, lead, width):
    total = None
    for col in range(3):
        kernel = jnp.concatenate([taps_ref[lead, 3 * row + col] for row in range(3)], 1)
        part = dot(values, kernel)
        line = part[:, 128:256]
        line = line + move_rows(part[:, 0:128], -1, width)
        line = line + move_rows(part[:, 256:384], 1, width)
        line = move_columns(line, col - 1, width)
        total = line if total is None else total + line
    return total


def spread_taps(grad, width, taps_out):
    for col in range(3):
        line = move_columns(grad, 1 - col, width)
        for row in range(3):
            tap = 3 * row + col
            taps_out[:, tap * 128 : tap * 128 + 128] = move_rows(line, 1 - row, width).astype(LOW)


def conv_back(taps_value, taps_ref, lead):
    kernel = jnp.concatenate([taps_ref[lead, tap] for tap in range(9)], 1)
    return dot_nt(taps_value, kernel)


def pool(v, scratch, width):
    size = v.shape[0]
    if width % 8 == 0:
        pairs = v.reshape(size // (2 * width), 2 * width, 128)
        rows = (pairs[:, :width] + pairs[:, width:]).reshape(size // 2, 128)
        scratch[0 : size // 2] = rows
        return 0.25 * (
            scratch[pl.ds(0, size // 4, stride=2)] + scratch[pl.ds(1, size // 4, stride=2)]
        )
    v = v + pltpu.roll(v, size - width, 0)
    v = v + pltpu.roll(v, size - 1, 0)
    scratch[...] = v
    half = scratch[pl.ds(0, size // 2, stride=2)]
    scratch[0 : size // 2] = half
    parts = [scratch[a * width : a * width + width // 2] for a in range(size // (2 * width))]
    return 0.25 * jnp.concatenate(parts, 0)


def unpool(v, scratch, width):
    size = 4 * v.shape[0]
    v = 0.25 * v
    scratch[pl.ds(0, size // 4, stride=2)] = v
    scratch[pl.ds(1, size // 4, stride=2)] = v
    rows = scratch[0 : size // 2]
    if width % 8 == 0:
        rows = rows.reshape(size // (2 * width), width, 128)
        return jnp.concatenate([rows, rows], 1).reshape(size, 128)
    parts = []
    for a in range(size // (2 * width)):
        part = rows[a * width : a * width + width]
        parts += [part, part]
    return jnp.concatenate(parts, 0)


def first_conv_body(width, ch, x0, x1, x2, x3, taps, full, y, stats):
    place_blocks(ch, (x0, x1, x2, x3), full)
    out = conv(full[...], taps, 0, width)
    y[...] = out
    stats[0:1] = sums(out)
    stats[1:2] = sums(out * out)


def plain_conv_body(width, x, taps, y, stats):
    out = conv(x[...], taps, 0, width)
    y[...] = out
    stats[0:1] = sums(out)
    stats[1:2] = sums(out * out)


def first_act_body(count, y, total, gain, shift, low):
    mean, inverse = centre(total[...], count)
    v = (y[...] - mean) * inverse * gain[...] + shift[...]
    low[...] = (v * sigmoid(v)).astype(LOW)


def second_conv_body(width, ch, x0, x1, x2, x3, taps, down, full, y, p, stats):
    place_blocks(ch, (x0, x1, x2, x3), full)
    values = full[...]
    out = conv(values, taps, 0, width)
    y[...] = out
    stats[0:1] = sums(out)
    stats[1:2] = sums(out * out)
    for t in range(3):
        part = dot(values, down[t])
        p[t] = part
        stats[2 + 2 * t : 3 + 2 * t] = sums(part)
        stats[3 + 2 * t : 4 + 2 * t] = sums(part * part)


def second_conv_only_body(width, ch, x0, x1, x2, x3, taps, full, y, stats):
    place_blocks(ch, (x0, x1, x2, x3), full)
    out = conv(full[...], taps, 0, width)
    y[...] = out
    stats[0:1] = sums(out)
    stats[1:2] = sums(out * out)


def hidden_body(count, width, y, p, total, gain, shift, bgain, bshift, up, s, u, pooled_u, zstats, scratch):
    mean, inverse = centre(total[0:2], count)
    v = (y[...] - mean) * inverse * gain[...] + shift[...]
    act = v * sigmoid(v)
    u[...] = act.astype(LOW)
    pooled_u[...] = pool(act, scratch, width).astype(LOW)
    for t in range(3):
        mean, inverse = centre(total[2 + 2 * t : 4 + 2 * t], count)
        v = (p[t] - mean) * inverse * bgain[t : t + 1] + bshift[t : t + 1]
        low = (v * sigmoid(v)).astype(LOW)
        s[t] = low
        z = dot(low, up[t])
        zstats[2 * t : 2 * t + 1] = sums(z)
        zstats[2 * t + 1 : 2 * t + 2] = sums(z * z)


def task_conv_body(count, width, ch, s, up, u0, u1, u2, u3, ztotal, gain, shift, taps, k, y, stats, full):
    @pl.when(pl.program_id(0) == 0)
    def _():
        place_blocks(ch, (u0, u1, u2, u3), full)

    mean, inverse = centre(ztotal[0], count)
    v = (dot(s[0], up[0]) - mean) * inverse * gain[0] + shift[0]
    k[0] = (sigmoid(v) * full[...].astype(F32)).astype(LOW)
    out = conv(k[0], taps, 0, width)
    y[0] = out
    stats[0, 0:1] = sums(out)
    stats[0, 1:2] = sums(out * out)


def task_act_body(count, width, y, total, gain, shift, q, scratch):
    for t in range(3):
        mean, inverse = centre(total[2 * t : 2 * t + 2], count)
        v = (y[t] - mean) * inverse * gain[t : t + 1] + shift[t : t + 1]
        q[t] = pool(v * sigmoid(v), scratch, width)


def attend_body(count, y, total, gain, shift, q, down, low, g, part):
    mean, inverse = centre(total[...], count)
    v = (y[...] - mean) * inverse * gain[...] + shift[...]
    act = v * sigmoid(v)
    low[...] = act.astype(LOW)
    for t in range(3):
        attend = (act + q[t]).astype(LOW)
        g[t] = attend
        part[t] = dot(attend, down[t]).astype(LOW)


def task_grad_body(width, count, y, total, gain, shift, dq, d, stats, scratch):
    for t in range(3):
        mean, inverse = centre(total[2 * t : 2 * t + 2], count)
        normal = (y[t] - mean) * inverse
        v = normal * gain[t : t + 1] + shift[t : t + 1]
        sg = sigmoid(v)
        grad = unpool(dq[t], scratch, width) * silu_slope(v, sg)
        d[t] = grad
        stats[2 * t : 2 * t + 1] = sums(grad)
        stats[2 * t + 1 : 2 * t + 2] = sums(grad * normal)


def task_last_body(count, width, y, total, gain, shift, dq, out, d, stats, scratch):
    for t in range(3):
        mean, inverse = centre(total[2 * t : 2 * t + 2], count)
        normal = (y[t] - mean) * inverse
        v = normal * gain[t : t + 1] + shift[t : t + 1]
        sg = sigmoid(v)
        out[t] = pool(v * sg, scratch, width).astype(LOW)
        grad = unpool(dq[t], scratch, width) * silu_slope(v, sg)
        d[t] = grad
        stats[2 * t : 2 * t + 1] = sums(grad)
        stats[2 * t + 1 : 2 * t + 2] = sums(grad * normal)


def norm_back(d, y, total, dtotal, gain, count):
    mean, inverse = centre(total, count)
    normal = (y - mean) * inverse
    return gain * inverse * (d - dtotal[0:1] / count - normal * (dtotal[1:2] / count))


def conv_grads(width, images, ch, im, dy, x_value, taps, send, keep, dk, cat, dv, dkf):
    spread_taps(dy, width, cat)
    values = cat[...]
    dv[...] = conv_back(values, taps, 0)
    own = ch[0]
    for place, k in ((send, 1), (keep, 0), (send, 3), (keep, 2)):
        start = pl.multiple_of((own ^ k) * 128, 128)
        block = dv[:, pl.ds(start, 128)]
        place[0, k // 2] = block.astype(place.dtype)
    dkf[...] = dot_tn(x_value, values)
    share = 512 // images

    def copy(r, carry):
        start = pl.multiple_of((im[0] ^ r) * share, share)
        for tap in range(9):
            dk[0, r, tap] = dkf[pl.ds(start, share), tap * 128 : tap * 128 + 128].astype(LOW)
        return carry

    lax.fori_loop(0, images, copy, 0)


def conv_back_body(count, width, images, ch, im, d, y, total, dtotal, gain, x, taps, send, keep, dk, cat, dv, dkf):
    dy = norm_back(d[0], y[0], total[0], dtotal[0], gain[0], count)
    conv_grads(width, images, ch, im, dy, x[0], taps, send, keep, dk, cat, dv, dkf)


def gate_grad_body(count, width, dr, s, up, ztotal, zgain, zshift, y, total, gain, shift, dx, d, d2, stats, scratch):
    mean, inverse = centre(total[...], count)
    normal = (y[...] - mean) * inverse
    v = normal * gain[...] + shift[...]
    sg = sigmoid(v)
    act = v * sg
    upstream = unpool(dx[...], scratch, width)
    for t in range(3):
        zmean, zinverse = centre(ztotal[2 * t : 2 * t + 2], count)
        znormal = (dot(s[t], up[t]) - zmean) * zinverse
        m = sigmoid(znormal * zgain[t : t + 1] + zshift[t : t + 1])
        through = dr[t] * m
        upstream = upstream + through
        grad = through * act * (1.0 - m)
        d[t] = grad
        stats[2 + 2 * t : 3 + 2 * t] = sums(grad)
        stats[3 + 2 * t : 4 + 2 * t] = sums(grad * znormal)
    grad = upstream * silu_slope(v, sg)
    d2[...] = grad
    stats[0:1] = sums(grad)
    stats[1:2] = sums(grad * normal)


def hidden_grad_body(count, d, s, up, ztotal, dztotal, zgain, ds, dup):
    for t in range(3):
        z = dot(s[t], up[t])
        rows = slice(2 * t, 2 * t + 2)
        dz = norm_back(d[t], z, ztotal[rows], dztotal[rows], zgain[t : t + 1], count).astype(LOW)
        dup[t] = dot_tn(s[t], dz)
        ds[t] = dot_nt(dz, up[t]).astype(LOW)


def bottle_grad_body(count, ds0, ds1, p, total, bgain, bshift, d, stats):
    for t in range(3):
        mean, inverse = centre(total[2 * t : 2 * t + 2], count)
        normal = (p[t] - mean) * inverse
        v = normal * bgain[t : t + 1] + bshift[t : t + 1]
        grad = (ds0[t].astype(F32) + ds1[t].astype(F32)) * silu_slope(v, sigmoid(v))
        d[t] = grad
        stats[2 * t : 2 * t + 1] = sums(grad)
        stats[2 * t + 1 : 2 * t + 2] = sums(grad * normal)


def attend_grad_body(count, separate, d, p, total, dtotal, bgain, g, down, dv, y, ytotal, gain, shift, ddown, d1, stats, dg=None):
    upstream = dv[...]
    for t in range(3):
        rows = slice(2 * t, 2 * t + 2)
        dp = norm_back(d[t], p[t], total[rows], dtotal[rows], bgain[t : t + 1], count).astype(LOW)
        ddown[t] = dot_tn(g[t] if separate else g[...], dp)
        grad = dot_nt(dp, down[t])
        if separate:
            dg[t] = grad
        upstream = upstream + grad
    mean, inverse = centre(ytotal[...], count)
    normal = (y[...] - mean) * inverse
    v = normal * gain[...] + shift[...]
    grad = upstream * silu_slope(v, sigmoid(v))
    d1[...] = grad
    stats[0:1] = sums(grad)
    stats[1:2] = sums(grad * normal)


def spec_of(value):
    if value.dtype == jnp.int32:
        return pl.BlockSpec(memory_space=pltpu.SMEM)
    return pl.BlockSpec(memory_space=pltpu.VMEM)


def shape_of(shape, dtype=F32):
    return jax.ShapeDtypeStruct(shape, dtype)


def run(body, args, outs, scratch=(), specs=None, name=None, flops=0):
    specs = specs or {}
    ins = [specs.get(place, spec_of(value)) for place, value in enumerate(args)]
    return pl.pallas_call(
        body,
        out_shape=outs,
        grid=(1,),
        in_specs=ins,
        out_specs=[pl.BlockSpec(memory_space=pltpu.VMEM)] * len(outs),
        scratch_shapes=list(scratch),
        compiler_params=pltpu.CompilerParams(vmem_limit_bytes=VMEM_LIMIT),
        cost_estimate=pl.CostEstimate(flops=flops, bytes_accessed=4 << 20, transcendentals=0),
        name=name,
    )(*args)


def taps_spec(index):
    return pl.BlockSpec((1, 9, 512, 128), lambda i: (index, 0, 0, 0))


def per_task(value, lead=0):
    rest = value.shape[1:]
    return pl.BlockSpec((1,) + rest, lambda t: (lead + t,) + (0,) * len(rest))


def fixed(value):
    if value.dtype == jnp.int32:
        return pl.BlockSpec(memory_space=pltpu.SMEM)
    return pl.BlockSpec(value.shape, lambda t: (0,) * value.ndim)


def run_tasks(body, tasks, args, specs, outs, scratch=(), name=None, flops=0):
    return pl.pallas_call(
        body,
        out_shape=outs,
        grid=(tasks,),
        in_specs=specs,
        out_specs=[per_task(out) for out in outs],
        scratch_shapes=list(scratch),
        compiler_params=pltpu.CompilerParams(vmem_limit_bytes=VMEM_LIMIT),
        cost_estimate=pl.CostEstimate(flops=flops, bytes_accessed=8 << 20, transcendentals=0),
        name=name,
    )(*args)


CORE = ((0, 1), (1, 0), (2, 3), (3, 2))
CHIP = ((0, 2), (2, 0), (1, 3), (3, 1))


def gather_ch(value):
    far = lax.ppermute(value, "ch", CHIP)
    near = lax.ppermute(value, "ch", CORE)
    return value, near, far, lax.ppermute(far, "ch", CORE)


def in_order(blocks, axis):
    own = lax.axis_index("ch")
    odd = (own & 1) == 1
    high = (own >> 1) == 1
    own_b, near, far, last = blocks
    pair = jnp.where(odd, jnp.stack([near, own_b]), jnp.stack([own_b, near]))
    other = jnp.where(odd, jnp.stack([last, far]), jnp.stack([far, last]))
    first = jnp.where(high, other, pair)
    second = jnp.where(high, pair, other)
    return jnp.concatenate([first[0], first[1], second[0], second[1]], axis)


def sum_img(value):
    count = lax.axis_size("img")
    copies = jnp.broadcast_to(value[None], (count,) + value.shape)
    return jnp.sum(lax.all_to_all(copies, "img", 0, 0), 0)


def sum_ch_halves(value):
    pair = value.astype(F32) + lax.ppermute(value, "ch", CORE).astype(F32)
    pair = pair.astype(LOW)
    return pair, lax.ppermute(pair, "ch", CHIP)


def scatter_ch(send, keep):
    got = lax.ppermute(send, "ch", CORE)
    both = keep + got.astype(F32)
    far = lax.ppermute(both[:, 1].astype(LOW), "ch", CHIP)
    return both[:, 0] + far.astype(F32)


def scatter_img(blocks):
    count = lax.axis_size("img")
    total = blocks
    step = 1
    while step < count:
        pairs = total.reshape((total.shape[0], -1, 2) + total.shape[2:])
        moves = [(i, i ^ step) for i in range(count)]
        got = lax.ppermute(pairs[:, :, 1], "img", moves)
        total = pairs[:, :, 0].astype(F32) + got.astype(F32)
        step *= 2
        if step < count:
            total = total.astype(LOW)
    return total[:, 0]


def sum_img_wide(value):
    count = lax.axis_size("img")
    step = 1
    total = value.astype(LOW)
    while step < count:
        got = lax.ppermute(total, "img", [(i, i ^ step) for i in range(count)])
        wide = total.astype(F32) + got.astype(F32)
        total = wide.astype(LOW)
        step *= 2
    return wide


class Layer:
    pass


def on_device(
    feats,
    shared_w,
    task_w,
    down_w,
    up_w,
    norm_gain,
    norm_shift,
    bottle_gain,
    bottle_shift,
    seg_mask,
    depth_mask,
    shared_cot,
    task_cot,
):
    images = lax.axis_size("img")
    tasks = task_w.shape[1]
    layers = shared_w.shape[0]
    own = lax.axis_index("ch").astype(jnp.int32).reshape(1)
    img = lax.axis_index("img").astype(jnp.int32).reshape(1)
    shared_taps = shared_w.reshape(2 * layers, 9, 512, 128)
    task_taps = task_w.reshape(tasks * layers, 9, 512, 128)
    widths = [feats.shape[2], feats.shape[2] // 2]
    sizes = [w * w for w in widths]
    counts = [float(images * n) for n in sizes]

    feats_blocks = gather_ch(feats.reshape(sizes[0], 128))
    pack = jnp.stack([down_w, up_w])
    pack, _ = lax.optimization_barrier((pack, feats_blocks[1]))
    packs = gather_ch(pack)
    down_all = in_order([b[0] for b in packs], 2)
    up_all = in_order([b[1] for b in packs], 3)
    gates = gather_ch(jnp.stack([norm_gain[:, 5:8], norm_shift[:, 5:8]]))
    gates = in_order(gates, 3)[:, :, :, None, :]

    kept = [Layer() for _ in range(layers)]

    def conv_cost(n):
        return 2 * n * 512 * 128 * 9

    def forward_shared(l, blocks=None, full=None):
        k, n, w = kept[l], sizes[l], widths[l]
        if blocks is not None:
            k.x, k.y1, stats = run(
                functools.partial(first_conv_body, w),
                (own, *blocks, shared_taps),
                [shape_of((n, 512), LOW), shape_of((n, 128)), shape_of((2, 128))],
                specs={5: taps_spec(2 * l)},
                name=f"conv1_{l}",
                flops=conv_cost(n),
            )
        else:
            k.x = full
            k.y1, stats = run(
                functools.partial(plain_conv_body, w),
                (full, shared_taps),
                [shape_of((n, 128)), shape_of((2, 128))],
                specs={1: taps_spec(2 * l)},
                name=f"conv1_{l}",
                flops=conv_cost(n),
            )
        return stats

    def gain_of(l, row):
        return norm_gain[l, row : row + 1], norm_shift[l, row : row + 1]

    def hidden(l):
        k, n, w = kept[l], sizes[l], widths[l]
        k.s, u, pooled_u, zstats = run(
            functools.partial(hidden_body, counts[l], w),
            (k.y2, k.p, k.total2, *gain_of(l, 1), bottle_gain[l], bottle_shift[l], up_all[l]),
            [
                shape_of((tasks, n, 128), LOW),
                shape_of((n, 128), LOW),
                shape_of((n // 4, 128), LOW),
                shape_of((2 * tasks, 512)),
            ],
            scratch=[pltpu.VMEM((n, 128), F32)],
            name=f"hidden_{l}",
            flops=2 * 3 * n * 128 * 512,
        )
        return u, pooled_u, zstats

    def task_convs(l, u_blocks):
        k, n, w = kept[l], sizes[l], widths[l]
        args = (
            own,
            k.s,
            up_all[l],
            *u_blocks,
            k.ztotal.reshape(tasks, 2, 512),
            gates[0, l],
            gates[1, l],
            task_taps,
        )
        specs = [
            fixed(own),
            per_task(k.s),
            per_task(args[2]),
            *[fixed(b) for b in u_blocks],
            per_task(args[7]),
            per_task(args[8]),
            per_task(args[9]),
            per_task(task_taps, tasks * l),
        ]
        k.k, k.yt, stats = run_tasks(
            functools.partial(task_conv_body, counts[l], w),
            tasks,
            args,
            specs,
            [shape_of((tasks, n, 512), LOW), shape_of((tasks, n, 128)), shape_of((tasks, 2, 128))],
            scratch=[pltpu.VMEM((n, 512), LOW)],
            name=f"taskconv_{l}",
            flops=3 * conv_cost(n),
        )
        return stats.reshape(2 * tasks, 128)

    k = kept[0]
    k.total1 = sum_img(forward_shared(0, blocks=feats_blocks))
    low = run(
        functools.partial(first_act_body, counts[0]),
        (k.y1, k.total1, *gain_of(0, 0)),
        [shape_of((sizes[0], 128), LOW)],
        name="act1_0",
    )[0]
    k.low = low
    low_blocks = gather_ch(low)
    k.x2, k.y2, k.p, stats = run(
        functools.partial(second_conv_body, widths[0]),
        (own, *low_blocks, shared_taps, down_all[0]),
        [
            shape_of((sizes[0], 512), LOW),
            shape_of((sizes[0], 128)),
            shape_of((tasks, sizes[0], 128)),
            shape_of((8, 128)),
        ],
        specs={5: taps_spec(1)},
        name="conv2_0",
        flops=conv_cost(sizes[0]),
    )
    k.total2 = sum_img(stats)
    u, pooled_u, zstats = hidden(0)
    u_blocks = gather_ch(jnp.concatenate([u, pooled_u], 0))
    k.ztotal = sum_img(zstats)
    n = sizes[0]
    next_x = in_order([b[n:] for b in u_blocks], 1)
    u_blocks = [b[:n] for b in u_blocks]
    stats_next = forward_shared(1, full=next_x)
    stats = task_convs(0, u_blocks)
    total = sum_img(jnp.concatenate([stats, stats_next], 0))
    k.ttotal = total[: 2 * tasks]
    kept[1].total1 = total[2 * tasks :]

    q = run(
        functools.partial(task_act_body, counts[0], widths[0]),
        (k.yt, k.ttotal, norm_gain[0, 2:5], norm_shift[0, 2:5]),
        [shape_of((tasks, sizes[1], 128))],
        scratch=[pltpu.VMEM((sizes[0], 128), F32)],
        name="taskact_0",
    )[0]
    k = kept[1]
    k.low, k.g, part = run(
        functools.partial(attend_body, counts[1]),
        (k.y1, k.total1, *gain_of(1, 0), q, down_w[1]),
        [
            shape_of((sizes[1], 128), LOW),
            shape_of((tasks, sizes[1], 128), LOW),
            shape_of((tasks, sizes[1], 128), LOW),
        ],
        name="attend_1",
    )
    low_blocks = gather_ch(k.low)
    near, far = sum_ch_halves(part)
    k.p = near.astype(F32) + far.astype(F32)
    k.x2, k.y2, stats2 = run(
        functools.partial(second_conv_only_body, widths[1]),
        (own, *low_blocks, shared_taps),
        [shape_of((sizes[1], 512), LOW), shape_of((sizes[1], 128)), shape_of((2, 128))],
        specs={5: taps_spec(3)},
        name="conv2_1",
        flops=conv_cost(sizes[1]),
    )
    pstats = jnp.stack([jnp.sum(k.p, 1), jnp.sum(k.p * k.p, 1)], 1).reshape(2 * tasks, 128)
    k.total2 = sum_img(jnp.concatenate([stats2, pstats], 0))
    u, pooled_u, zstats = hidden(1)
    shared_out = pooled_u
    u_blocks = gather_ch(u)
    k.ztotal = sum_img(zstats)
    k.ttotal = sum_img(task_convs(1, u_blocks))

    scales = jnp.stack([seg_mask, depth_mask, jnp.ones_like(seg_mask)]).astype(F32)
    dq = (task_cot.astype(F32) * scales[..., None]).reshape(tasks, sizes[1] // 4, 128)
    dx = shared_cot.astype(F32).reshape(sizes[1] // 4, 128)
    task_out, d, stats = run(
        functools.partial(task_last_body, counts[1], widths[1]),
        (k.yt, k.ttotal, norm_gain[1, 2:5], norm_shift[1, 2:5], dq),
        [
            shape_of((tasks, sizes[1] // 4, 128), LOW),
            shape_of((tasks, sizes[1], 128)),
            shape_of((2 * tasks, 128)),
        ],
        scratch=[pltpu.VMEM((sizes[1], 128), F32)],
        name="tasklast_1",
    )
    dttotal = sum_img(stats)

    def conv_grad(l, d, y, total, dtotal, gain, x, taps, lead, name):
        n, w = sizes[l], widths[l]
        count = d.shape[0]
        args = (own, img, d, y, total, dtotal, gain, x, taps)
        specs = [fixed(own), fixed(img)] + [per_task(a) for a in args[2:8]] + [per_task(taps, lead)]
        return run_tasks(
            functools.partial(conv_back_body, counts[l], w, images),
            count,
            args,
            specs,
            [
                shape_of((count, 2, n, 128), LOW),
                shape_of((count, 2, n, 128)),
                shape_of((count, images, 9, 512 // images, 128), LOW),
            ],
            scratch=[
                pltpu.VMEM((n, 1152), LOW),
                pltpu.VMEM((n, 512), F32),
                pltpu.VMEM((512, 1152), F32),
            ],
            name=name,
            flops=2 * count * conv_cost(n),
        )

    def send_blocks(send, keep):
        return scatter_ch(send, keep)

    grads = [None] * layers
    for l in range(layers - 1, -1, -1):
        k, n, w = kept[l], sizes[l], widths[l]
        g = Layer()
        grads[l] = g
        g.task = dttotal
        send, keep, dk = conv_grad(
            l,
            d,
            k.yt,
            k.ttotal.reshape(tasks, 2, 128),
            dttotal.reshape(tasks, 2, 128),
            norm_gain[l, 2:5][:, None],
            k.k,
            task_taps,
            tasks * l,
            f"taskgrad_{l}",
        )
        dr = send_blocks(send, keep)
        g.task_w = scatter_img(dk)
        own_rows = lax.dynamic_slice_in_dim(k.ztotal, own[0] * 128, 128, 1)
        d, d2, stats = run(
            functools.partial(gate_grad_body, counts[l], w),
            (
                dr,
                k.s,
                up_w[l],
                own_rows,
                norm_gain[l, 5:8],
                norm_shift[l, 5:8],
                k.y2,
                k.total2[0:2],
                *gain_of(l, 1),
                dx,
            ),
            [shape_of((tasks, n, 128)), shape_of((n, 128)), shape_of((2 * tasks + 2, 128))],
            scratch=[pltpu.VMEM((n, 128), F32)],
            name=f"gategrad_{l}",
        )
        total = sum_img(stats)
        g.second, g.gate = total[0:2], total[2:]
        ds, dup = run(
            functools.partial(hidden_grad_body, counts[l]),
            (d, k.s, up_w[l], own_rows, g.gate, norm_gain[l, 5:8]),
            [shape_of((tasks, n, 128), LOW), shape_of((tasks, 128, 128))],
            name=f"hiddengrad_{l}",
        )
        near, far = sum_ch_halves(ds)
        send, keep, dk2 = conv_grad(
            l,
            d2[None],
            k.y2[None],
            k.total2[None, 0:2],
            g.second[None],
            gain_of(l, 1)[0][None],
            k.x2[None],
            shared_taps,
            2 * l + 1,
            f"conv2grad_{l}",
        )
        dv = send_blocks(send, keep)[0]
        d, stats = run(
            functools.partial(bottle_grad_body, counts[l]),
            (near, far, k.p, k.total2[2:], bottle_gain[l], bottle_shift[l]),
            [shape_of((tasks, n, 128)), shape_of((2 * tasks, 128))],
            name=f"bottlegrad_{l}",
        )
        g.bottle = sum_img(stats)
        separate = l > 0
        outs = run(
            functools.partial(attend_grad_body, counts[l], separate),
            (
                d,
                k.p,
                k.total2[2:],
                g.bottle,
                bottle_gain[l],
                k.g if separate else k.low,
                down_w[l],
                dv,
                k.y1,
                k.total1,
                *gain_of(l, 0),
            ),
            [shape_of((tasks, 128, 128)), shape_of((n, 128)), shape_of((2, 128))]
            + ([shape_of((tasks, n, 128))] if separate else []),
            name=f"attendgrad_{l}",
        )
        ddown, d1, stats = outs[:3]
        if separate:
            b = kept[l - 1]
            d, task_stats = run(
                functools.partial(task_grad_body, widths[l - 1], counts[l - 1]),
                (b.yt, b.ttotal, norm_gain[l - 1, 2:5], norm_shift[l - 1, 2:5], outs[3]),
                [shape_of((tasks, sizes[l - 1], 128)), shape_of((2 * tasks, 128))],
                scratch=[pltpu.VMEM((sizes[l - 1], 128), F32)],
                name=f"taskdown_{l - 1}",
            )
            total = sum_img(jnp.concatenate([stats, task_stats], 0))
            g.first, dttotal = total[0:2], total[2:]
        else:
            g.first = sum_img(stats)
        send, keep, dk1 = conv_grad(
            l,
            d1[None],
            k.y1[None],
            k.total1[None],
            g.first[None],
            gain_of(l, 0)[0][None],
            k.x[None],
            shared_taps,
            2 * l,
            f"conv1grad_{l}",
        )
        dx = send_blocks(send, keep)[0]
        g.shared_w = jnp.concatenate([scatter_img(dk1), scatter_img(dk2)], 0)
        g.down, g.up = sum_img_wide(jnp.stack([ddown, dup]))

    def rows(g, part):
        pairs = jnp.concatenate([g.first, g.second, g.task, g.gate], 0).reshape(8, 2, 128)
        return pairs[:, part]

    share = 512 // images
    return (
        shared_out.reshape(1, widths[1] // 2, widths[1] // 2, 128),
        task_out.reshape(tasks, 1, widths[1] // 2, widths[1] // 2, 128),
        dx.reshape(1, widths[0], widths[0], 128),
        jnp.stack([g.shared_w for g in grads]).reshape(layers, 2, 3, 3, share, 128),
        jnp.stack([g.task_w for g in grads]).reshape(layers, tasks, 3, 3, share, 128),
        jnp.stack([g.down for g in grads]),
        jnp.stack([g.up for g in grads]),
        jnp.stack([rows(g, 1) for g in grads]),
        jnp.stack([rows(g, 0) for g in grads]),
        jnp.stack([g.bottle.reshape(tasks, 2, 128)[:, 1] for g in grads]),
        jnp.stack([g.bottle.reshape(tasks, 2, 128)[:, 0] for g in grads]),
    )


def solution(mesh):
    placed = (
        P("img", None, None, "ch"),
        P(None, None, None, None, None, "ch"),
        P(None, None, None, None, None, "ch"),
        P(None, None, "ch", None),
        P(None, None, None, "ch"),
        P(None, None, "ch"),
        P(None, None, "ch"),
        P(),
        P(),
        P("img", None, None),
        P("img", None, None),
        P("img", None, None, "ch"),
        P(None, "img", None, None, "ch"),
    )
    return jax.shard_map(
        on_device,
        mesh=mesh,
        in_specs=placed,
        out_specs=(
            P("img", None, None, "ch"),
            P(None, "img", None, None, "ch"),
            P("img", None, None, "ch"),
            P(None, None, None, None, "img", "ch"),
            P(None, None, None, None, "img", "ch"),
            P(None, None, "ch", None),
            P(None, None, None, "ch"),
            P(None, None, "ch"),
            P(None, None, "ch"),
            P(),
            P(),
        ),
        check_vma=False,
    )
```

```python
import functools

import jax
import jax.numpy as jnp
from jax import lax
from jax.experimental import pallas as pl
from jax.experimental.pallas import tpu as pltpu
from jax.sharding import PartitionSpec as P

EPSILON = 1e-05
F32 = jnp.float32
LOW = jnp.bfloat16
VMEM_LIMIT = 16 * 2**20


def sigmoid(v):
    return 0.5 * jnp.tanh(0.5 * v) + 0.5


def silu_slope(v, s):
    return s * (1.0 + v * (1.0 - s))


def dot(a, b):
    return lax.dot_general(a, b, (((1,), (0,)), ((), ())), preferred_element_type=F32)


def dot_nt(a, b):
    return lax.dot_general(a, b, (((1,), (1,)), ((), ())), preferred_element_type=F32)


def dot_tn(a, b):
    return lax.dot_general(a, b, (((0,), (0,)), ((), ())), preferred_element_type=F32)


def sums(v):
    return jnp.sum(v, axis=0, keepdims=True)


def column_of(shape, width):
    place = lax.broadcasted_iota(jnp.int32, shape, 0)
    row = (place * (2731 if width == 24 else 5462)) >> 16
    return place - row * width


def move_columns(v, step, width):
    if step == 0:
        return v
    column = column_of(v.shape, width)
    keep = column < width - 1 if step == 1 else column > 0
    return jnp.where(keep, pltpu.roll(v, (-step) % v.shape[0], 0), 0.0)


def move_rows(v, step, width):
    if step == 0:
        return v
    size = v.shape[0]
    place = lax.broadcasted_iota(jnp.int32, v.shape, 0)
    keep = place < size - width if step == 1 else place >= width
    return jnp.where(keep, pltpu.roll(v, (-step * width) % size, 0), 0.0)


def centre(total, count):
    mean = total[0:1] / count
    spread = total[1:2] / count - mean * mean
    return mean, lax.rsqrt(spread + EPSILON)


def place_blocks(ch_ref, blocks, full_ref):
    own = ch_ref[0]
    for k, block in enumerate(blocks):
        start = pl.multiple_of((own ^ k) * 128, 128)
        full_ref[:, pl.ds(start, 128)] = block[...]


def conv(values, taps_ref, lead, width):
    total = None
    for col in range(3):
        kernel = jnp.concatenate([taps_ref[lead, 3 * row + col] for row in range(3)], 1)
        part = dot(values, kernel)
        line = part[:, 128:256]
        line = line + move_rows(part[:, 0:128], -1, width)
        line = line + move_rows(part[:, 256:384], 1, width)
        line = move_columns(line, col - 1, width)
        total = line if total is None else total + line
    return total


def spread_taps(grad, width, taps_out):
    for col in range(3):
        line = move_columns(grad, 1 - col, width)
        for row in range(3):
            tap = 3 * row + col
            taps_out[:, tap * 128 : tap * 128 + 128] = move_rows(line, 1 - row, width).astype(LOW)


def conv_back(taps_value, taps_ref, lead):
    kernel = jnp.concatenate([taps_ref[lead, tap] for tap in range(9)], 1)
    return dot_nt(taps_value, kernel)


def pool(v, scratch, width):
    size = v.shape[0]
    if width % 8 == 0:
        pairs = v.reshape(size // (2 * width), 2 * width, 128)
        rows = (pairs[:, :width] + pairs[:, width:]).reshape(size // 2, 128)
        scratch[0 : size // 2] = rows
        return 0.25 * (
            scratch[pl.ds(0, size // 4, stride=2)] + scratch[pl.ds(1, size // 4, stride=2)]
        )
    v = v + pltpu.roll(v, size - width, 0)
    v = v + pltpu.roll(v, size - 1, 0)
    scratch[...] = v
    half = scratch[pl.ds(0, size // 2, stride=2)]
    scratch[0 : size // 2] = half
    parts = [scratch[a * width : a * width + width // 2] for a in range(size // (2 * width))]
    return 0.25 * jnp.concatenate(parts, 0)


def unpool(v, scratch, width):
    size = 4 * v.shape[0]
    v = 0.25 * v
    scratch[pl.ds(0, size // 4, stride=2)] = v
    scratch[pl.ds(1, size // 4, stride=2)] = v
    rows = scratch[0 : size // 2]
    if width % 8 == 0:
        rows = rows.reshape(size // (2 * width), width, 128)
        return jnp.concatenate([rows, rows], 1).reshape(size, 128)
    parts = []
    for a in range(size // (2 * width)):
        part = rows[a * width : a * width + width]
        parts += [part, part]
    return jnp.concatenate(parts, 0)

def bn_of(total, row, count):
    return centre(total[row : row + 2], count)


def spread_stats(out, rows):
    for place, row in enumerate(rows):
        out[place : place + 1] = row


def moments(v):
    return [sums(v), sums(v * v)]


def pack_body(down, up, gain, shift, wide, narrow, params):
    for l in range(down.shape[0]):
        wide[l, 0] = down[l]
        wide[l, 1] = up[l]
        narrow[l, 0:3] = gain[l, 5:8]
        narrow[l, 3:6] = shift[l, 5:8]
        params[l, 0:8] = gain[l, 0:8]
        params[l, 8:16] = shift[l, 0:8]


def unpack_body(ch, w0, w1, w2, w3, n0, n1, n2, n3, down, up, gates):
    own = ch[0]
    for k, (wide, narrow) in enumerate(((w0, n0), (w1, n1), (w2, n2), (w3, n3))):
        start = pl.ds(pl.multiple_of((own ^ k) * 128, 128), 128)
        for l in range(down.shape[0]):
            for t in range(3):
                down[l, t, start, :] = wide[l, 0, t]
                up[l, t, :, start] = wide[l, 1, t]
            gates[l, :, start] = narrow[l]


def first_conv_body(width, lead, ch, x0, x1, x2, x3, taps, full, y, stats):
    place_blocks(ch, (x0, x1, x2, x3), full)
    flush(full)
    out = conv(full[...], taps, lead, width)
    y[...] = out
    spread_stats(stats, moments(out))


def next_conv_body(width, lead, skip, ch, x0, x1, x2, x3, taps, full, y, stats):
    own = ch[0]
    for k, block in enumerate((x0, x1, x2, x3)):
        start = pl.multiple_of((own ^ k) * 128, 128)
        full[:, pl.ds(start, 128)] = block[skip:]
    flush(full)
    out = conv(full[...], taps, lead, width)
    y[...] = out
    for place, row in enumerate(moments(out)):
        stats[place : place + 1] = row


def first_act_body(count, y, raw, gain, shift, low, again):
    mean, inverse = bn_of(raw, 0, count)
    v = (y[...] - mean) * inverse * gain[0, 0:1] + shift[0, 0:1]
    act = (v * sigmoid(v)).astype(LOW)
    low[...] = act
    again[...] = act


def second_conv_body(width, lead, ch, x0, x1, x2, x3, taps, down, full, y, p, stats):
    place_blocks(ch, (x0, x1, x2, x3), full)
    flush(full)
    values = full[...]
    out = conv(values, taps, lead, width)
    y[...] = out
    rows = moments(out)
    for t in range(3):
        part = dot(values, down[0, t])
        p[t] = part
        rows += moments(part)
    spread_stats(stats, rows)


def second_conv_next_body(width, lead, ch, x0, x1, x2, x3, taps, near, far, full, y, p, stats):
    place_blocks(ch, (x0, x1, x2, x3), full)
    flush(full)
    out = conv(full[...], taps, lead, width)
    y[...] = out
    rows = moments(out)
    for t in range(3):
        part = near[t].astype(F32) + far[t].astype(F32)
        p[t] = part
        rows += moments(part)
    spread_stats(stats, rows)


def hidden_body(l, count, width, y, p, raw, gain, shift, bgain, bshift, up, s, u, pooled_u, zstats, scratch):
    mean, inverse = bn_of(raw, 0, count)
    v = (y[...] - mean) * inverse * gain[l, 1:2] + shift[l, 1:2]
    act = v * sigmoid(v)
    size = y.shape[0]
    u[0:size] = act.astype(LOW)
    pooled = pool(act, scratch, width).astype(LOW)
    if pooled_u is None:
        u[size:] = pooled
    else:
        pooled_u[...] = pooled
    rows = []
    for t in range(3):
        mean, inverse = bn_of(raw, 2 + 2 * t, count)
        v = (p[t] - mean) * inverse * bgain[l, t : t + 1] + bshift[l, t : t + 1]
        low = (v * sigmoid(v)).astype(LOW)
        s[t] = low
        rows += moments(dot(low, up[l, t]))
    spread_stats(zstats, rows)


def task_conv_body(l, count, width, ch, s, up, u0, u1, u2, u3, zraw, gates, taps, more, k, y, stats, full, acc):
    size = s.shape[1]
    own = ch[0]
    for i, block in enumerate((u0, u1, u2, u3)):
        start = pl.multiple_of((own ^ i) * 128, 128)
        full[:, pl.ds(start, 128)] = block[0:size]
    ztotal = zraw[...]
    for t in range(3):
        mean, inverse = centre(ztotal[2 * t : 2 * t + 2], count)
        scale = inverse * gates[l, t : t + 1]
        v = dot(s[t], up[l, t]) * scale + (gates[l, 3 + t : 4 + t] - mean * scale)
        k[t] = (sigmoid(v) * full[...].astype(F32)).astype(LOW)
    flush(k)
    ready(taps)

    def one(t, carry):
        out = conv(k[t], taps, t, width)
        y[t] = out
        rows = moments(out)
        acc[t, 0:1] = rows[0]
        acc[t, 1:2] = rows[1]
        return carry

    lax.fori_loop(0, 3, one, 0)
    rows = [acc[t, i : i + 1] for t in range(3) for i in range(2)]
    if more is not None:
        rows += [more[0:1], more[1:2]]
    spread_stats(stats, rows)


def attend_body(count, count_next, width, yt, y, raw, gain, shift, down, low, g, part, scratch):
    mean, inverse = bn_of(raw, 6, count_next)
    v = (y[...] - mean) * inverse * gain[1, 0:1] + shift[1, 0:1]
    act = v * sigmoid(v)
    low[...] = act.astype(LOW)
    for t in range(3):
        mean, inverse = bn_of(raw, 2 * t, count)
        v = (yt[t] - mean) * inverse * gain[0, 2 + t : 3 + t] + shift[0, 2 + t : 3 + t]
        attend = (act + pool(v * sigmoid(v), scratch, width)).astype(LOW)
        g[t] = attend
        part[t] = dot(attend, down[1, t]).astype(LOW)


def pair_body(a, b, out):
    out[...] = (a[...].astype(F32) + b[...].astype(F32)).astype(LOW)


def pair_second_body(keep, far, got, out, part):
    out[...] = (far[...] + got[1].astype(F32)).astype(LOW)
    part[...] = keep[...] + got[0].astype(F32)


def mixed_body(a, b, out):
    out[...] = a[...] + b[...].astype(F32)


def stack_body(a, b, out):
    out[0] = a[...]
    out[1] = b[...]


def add_body(a, b, out):
    out[...] = (a[...].astype(F32) + b[...].astype(F32)).astype(out.dtype)


def sum_body(*refs):
    parts = [ref[...] for ref in refs[:-1]]
    while len(parts) > 1:
        parts = [a + b for a, b in zip(parts[::2], parts[1::2])]
    refs[-1][...] = parts[0]


def task_last_body(l, count, width, y, raw, gain, shift, dq, out, d, stats, scratch):
    rows = []
    for t in range(3):
        mean, inverse = bn_of(raw, 2 * t, count)
        normal = (y[t] - mean) * inverse
        v = normal * gain[l, 2 + t : 3 + t] + shift[l, 2 + t : 3 + t]
        sg = sigmoid(v)
        out[t] = pool(v * sg, scratch, width).astype(LOW)
        grad = unpool(dq[t], scratch, width) * silu_slope(v, sg)
        d[t] = grad
        rows += [sums(grad), sums(grad * normal)]
    spread_stats(stats, rows)


def norm_back(d, y, bn, dtotal, gain, count):
    mean, inverse = bn
    scale = gain * inverse
    normal = (y - mean) * inverse
    return scale * (d - dtotal[0:1] / count - normal * (dtotal[1:2] / count))


def input_grads(width, ch, dy, taps, lead, outs, cat, dv):
    spread_taps(dy, width, cat)
    dv[...] = conv_back(cat[...], taps, lead)
    own = ch[0]
    blocks = []
    for k in range(4):
        start = pl.multiple_of((own ^ k) * 128, 128)
        blocks.append(dv[:, pl.ds(start, 128)])
    return blocks


def task_back_body(l, count, width, row0, ch, d, y, raw, draw, gain, taps, dys, send, keep, far, cat, dv):
    total = raw[...]
    dtotal = draw[...]
    for t in range(3):
        bn = centre(total[2 * t : 2 * t + 2], count)
        dts = dtotal[row0 + 2 * t : row0 + 2 * t + 2]
        dy = norm_back(d[t], y[t], bn, dts, gain[l, 2 + t : 3 + t], count)
        dys[t] = dy.astype(LOW)
    ready(taps)

    def one(t, carry):
        blocks = input_grads(width, ch, dys[t].astype(F32), taps, t, None, cat, dv)
        send[0, t] = blocks[1].astype(LOW)
        send[1, t] = blocks[3].astype(LOW)
        keep[t] = blocks[0]
        far[t] = blocks[2]
        return carry

    lax.fori_loop(0, 3, one, 0)


def conv_back_body(l, k, count, width, ch, d, y, raw, rawrow, draw, gain, taps, dys, send, keep, far, cat, dv):
    dtotal = draw[0:2]
    dy = norm_back(d[...], y[...], bn_of(raw, rawrow, count), dtotal, gain[l, k : k + 1], count)
    dys[...] = dy.astype(LOW)
    blocks = input_grads(width, ch, dy, taps, 0, None, cat, dv)
    send[0] = blocks[1].astype(LOW)
    send[1] = blocks[3].astype(LOW)
    keep[...] = blocks[0]
    far[...] = blocks[2]


def weight_body(width, many, im, x, dys, dk, cat, dkf):
    images = dk.shape[0]
    share = 512 // images
    ready(x)
    ready(dys)

    def one(t, carry):
        dy = dys[t] if many else dys[...]
        spread_taps(dy.astype(F32), width, cat)
        dkf[...] = dot_tn(x[t] if many else x[...], cat[...])

        def copy(r, carry):
            rows = pl.ds(pl.multiple_of(r * share, share), share)
            for tap in range(9):
                dk[r, t, tap] = dkf[rows, tap * 128 : tap * 128 + 128].astype(LOW)
            return carry

        return lax.fori_loop(0, images, copy, carry)

    lax.fori_loop(0, dk.shape[1], one, 0)


def split_body(bit, im, x, out):
    low = (im[0] >> bit) & 1
    ready(x)
    for i in range(2):
        start = pl.multiple_of((2 * i + 1 - low) * 128, 128)
        out[i] = x.ref[0, :, pl.ds(start, 128)]


def pair_weight_body(width, bit, rest, im, x, other_x, dy, other_dy, stay, leave, cat, total):
    low = (im[0] >> bit) & 1
    ready(x)
    ready(dy)
    mine = [x.ref[0, :, pl.ds(pl.multiple_of((2 * i + low) * 128, 128), 128)] for i in range(2)]
    spread_taps(dy[0].astype(F32), width, cat)
    total[...] = dot_tn(jnp.concatenate(mine, 1), cat[...])
    spread_taps(other_dy[...].astype(F32), width, cat)
    total[...] += dot_tn(jnp.concatenate([other_x[0], other_x[1]], 1), cat[...])
    half = stay.shape[0]
    share = stay.shape[2]
    for e in range(2 * half):
        mask = 0
        for s, b in enumerate(rest):
            mask |= ((e >> (len(rest) - 1 - s)) & 1) << b
        block = im[0] ^ mask
        row = ((block >> (bit + 1)) & 1) * 128 + (block & ((1 << bit) - 1)) * share
        rows = pl.ds(pl.multiple_of(row, share), share)
        target = stay if e < half else leave
        for tap in range(9):
            target[e % half, tap] = total[rows, tap * 128 : tap * 128 + 128].astype(LOW)


def halve_body(a, b, stay, leave):
    half = stay.shape[0]
    for i in range(half):
        stay[i] = a[i].astype(F32) + b[i].astype(F32)
        leave[i] = (a[half + i].astype(F32) + b[half + i].astype(F32)).astype(LOW)


def gate_grad_body(l, count, width, ch, part, far, s, up, zraw, y, raw, gain, shift, dx, d, d2, stats, scratch):
    mean, inverse = bn_of(raw, 0, count)
    normal = (y[...] - mean) * inverse
    v = normal * gain[l, 1:2] + shift[l, 1:2]
    sg = sigmoid(v)
    act = v * sg
    own = pl.ds(pl.multiple_of(ch[0] * 128, 128), 128)
    ztotal = zraw[:, own]
    upstream = unpool(dx[...], scratch, width)
    rows = []
    for t in range(3):
        zmean, zinverse = centre(ztotal[2 * t : 2 * t + 2], count)
        znormal = (dot(s[t], up[l, t]) - zmean) * zinverse
        m = sigmoid(znormal * gain[l, 5 + t : 6 + t] + shift[l, 5 + t : 6 + t])
        dr = part[t] + far[t].astype(F32)
        through = dr * m
        upstream = upstream + through
        grad = through * act * (1.0 - m)
        d[t] = grad
        rows += [sums(grad), sums(grad * znormal)]
    grad = upstream * silu_slope(v, sg)
    d2[...] = grad
    spread_stats(stats, [sums(grad), sums(grad * normal)] + rows)


def hidden_grad_body(l, count, ch, d, s, up, zraw, draw, gain, ds, dup):
    own = pl.ds(pl.multiple_of(ch[0] * 128, 128), 128)
    ztotal = zraw[:, own]
    dtotal = draw[2:8]
    for t in range(3):
        z = dot(s[t], up[l, t])
        rows = slice(2 * t, 2 * t + 2)
        bn = centre(ztotal[rows], count)
        dz = norm_back(d[t], z, bn, dtotal[rows], gain[l, 5 + t : 6 + t], count).astype(LOW)
        dup[t] = dot_tn(s[t], dz).astype(LOW)
        ds[t] = dot_nt(dz, up[l, t]).astype(LOW)


def bottle_grad_body(l, count, ds0, ds1, p, raw, bgain, bshift, d, stats):
    rows = []
    for t in range(3):
        mean, inverse = bn_of(raw, 2 + 2 * t, count)
        normal = (p[t] - mean) * inverse
        v = normal * bgain[l, t : t + 1] + bshift[l, t : t + 1]
        grad = (ds0[t].astype(F32) + ds1[t].astype(F32)) * silu_slope(v, sigmoid(v))
        d[t] = grad
        rows += [sums(grad), sums(grad * normal)]
    spread_stats(stats, rows)


def attend_grad_body(l, count, rawrow, d, p, raw, draw, bgain, g, down, part, far, y, raw1, gain, shift, more, ddown, d1, stats, more_out):
    upstream = part[...] + far[...].astype(F32)
    dtotal = draw[...]
    rows = []
    for t in range(3):
        bn = bn_of(raw, 2 + 2 * t, count)
        dp = norm_back(d[t], p[t], bn, dtotal[2 * t : 2 * t + 2], bgain[l, t : t + 1], count).astype(LOW)
        ddown[t] = dot_tn(g[...] if more is None else g[t], dp).astype(LOW)
        grad = dot_nt(dp, down[l, t])
        upstream = upstream + grad
        if more is not None:
            yt, traw, tcount, twidth, scratch = more
            mean, inverse = bn_of(traw, 2 * t, tcount)
            normal = (yt[t] - mean) * inverse
            v = normal * gain[l - 1, 2 + t : 3 + t] + shift[l - 1, 2 + t : 3 + t]
            grad = unpool(grad, scratch, twidth) * silu_slope(v, sigmoid(v))
            more_out[t] = grad
            rows += [sums(grad), sums(grad * normal)]
    mean, inverse = bn_of(raw1, rawrow, count)
    normal = (y[...] - mean) * inverse
    v = normal * gain[l, 0:1] + shift[l, 0:1]
    grad = upstream * silu_slope(v, sigmoid(v))
    d1[...] = grad
    spread_stats(stats, [sums(grad), sums(grad * normal)] + rows)


def attend_grad_last_body(l, count, rawrow, d, p, raw, draw, bgain, g, down, part, far, y, raw1, gain, shift, ddown, d1, stats):
    attend_grad_body(l, count, rawrow, d, p, raw, draw, bgain, g, down, part, far, y, raw1, gain, shift, None, ddown, d1, stats, None)


def attend_grad_first_body(l, count, rawrow, tcount, twidth, d, p, raw, draw, bgain, g, down, part, far, y, raw1, gain, shift, yt, traw, ddown, d1, stats, dt, scratch):
    more = (yt, traw, tcount, twidth, scratch)
    attend_grad_body(l, count, rawrow, d, p, raw, draw, bgain, g, down, part, far, y, raw1, gain, shift, more, ddown, d1, stats, dt)


def finish_body(order, refs_in, gain, shift, bgain, bshift):
    for l in range(gain.shape[0]):
        for row, (place, start) in enumerate(order[l]):
            total = refs_in[place][start : start + 2]
            if row < 8:
                shift[l, row : row + 1] = total[0:1]
                gain[l, row : row + 1] = total[1:2]
            else:
                bshift[l, row - 8 : row - 7] = total[0:1]
                bgain[l, row - 8 : row - 7] = total[1:2]


def shape_of(shape, dtype=F32):
    return jax.ShapeDtypeStruct(tuple(shape), dtype)


class Long:
    def __init__(self, near, home=None):
        self.near, self.home = near, home
        some = home if near is None else near
        self.shape, self.dtype = some.shape, some.dtype


class Taps:
    def __init__(self, home, first, count):
        self.home, self.first, self.shape = home, first, (count,) + home.shape[1:]
        self.dtype = home.dtype


class Rows:
    def __init__(self, whole, first, last):
        self.whole, self.first, self.last = whole, first, last


class Coming:
    def __init__(self, ref, copy):
        self.ref, self.copy, self.shape, self.dtype = ref, copy, ref.shape, ref.dtype

    def ready(self):
        if self.copy is not None:
            self.copy.wait()
            self.copy = None

    def __getitem__(self, place):
        self.ready()
        return self.ref[place]


class Going:
    def __init__(self, ref, copy):
        self.ref, self.copy, self.shape, self.dtype = ref, copy, ref.shape, ref.dtype
        self.started = False

    def flush(self):
        if not self.started:
            self.copy.start()
            self.started = True

    def __getitem__(self, place):
        return self.ref[place]

    def __setitem__(self, place, value):
        self.ref[place] = value


class SomeRows:
    def __init__(self, ref, first):
        self.ref, self.first = ref, first

    def __getitem__(self, place):
        layer, rows = place
        return self.ref[layer, self.first + rows.start : self.first + rows.stop]


def ready(ref):
    if isinstance(ref, Coming):
        ref.ready()


def flush(ref):
    if isinstance(ref, Going):
        ref.flush()


TURN = []


def run(body, args, outs, scratch=(), name=None, keep=(), away=(), save=(), after=()):
    values, picks = [], []
    for v in list(args) + list(save):
        whole = v.whole if isinstance(v, Rows) else v
        place = next((i for i, other in enumerate(values) if other is whole), None)
        if place is None:
            place = len(values)
            values.append(whole)
        picks.append((place, v))
    picks = picks[: len(args)]
    count = len(values)
    far = [
        isinstance(v, Taps) or (isinstance(v, Long) and v.near is None) for v in values
    ]
    saved = [i for i, v in enumerate(values) if isinstance(v, Long) and v.home is None]
    hbm, vmem = pl.BlockSpec(memory_space=pltpu.HBM), pl.BlockSpec(memory_space=pltpu.VMEM)
    operands, specs = [], []
    for v, apart in zip(values, far):
        if apart:
            operands.append(pltpu.with_memory_space_constraint(v.home, pltpu.HBM))
            specs.append(hbm)
        else:
            operands.append(v.near if isinstance(v, Long) else v)
            specs.append(spec_of(operands[-1]))
    after = list(after) + TURN
    TURN.clear()
    outs = list(outs) + [shape_of((8, 128))]
    stage = [pltpu.VMEM(v.shape, v.dtype) for v, apart in zip(values, far) if apart]
    leave = [pltpu.VMEM(outs[i].shape, outs[i].dtype) for i in away]
    moves = len(stage) + len(leave) + len(saved)

    def kernel(*refs):
        ins = list(refs[:count])
        results = list(refs[count + len(after) : count + len(after) + len(outs)])
        homes = refs[count + len(after) + len(outs) :][: len(saved)]
        rest = refs[count + len(after) + len(outs) + len(saved) :]
        own, rest = rest[: len(scratch)], rest[len(scratch) :]
        sems = rest[-1] if moves else None
        wait = []
        slot = 0
        for i in range(count):
            if not far[i]:
                continue
            source = ins[i]
            if isinstance(values[i], Taps):
                source = source.at[values[i].first : values[i].first + values[i].shape[0]]
            copy = pltpu.make_async_copy(source, rest[slot], sems.at[slot])
            copy.start()
            ins[i] = Coming(rest[slot], copy)
            wait.append(ins[i])
            slot += 1
        end = []
        for i, home in zip(saved, homes):
            copy = pltpu.make_async_copy(ins[i], home, sems.at[slot])
            copy.start()
            end.append(copy)
            slot += 1
        for n, i in enumerate(away):
            ref = rest[len(stage) + n]
            copy = pltpu.make_async_copy(ref, results[i], sems.at[slot])
            results[i] = Going(ref, copy)
            end.append(results[i])
            slot += 1
        turn = results.pop()
        turn[...] = jnp.zeros_like(turn)
        views = [SomeRows(ins[i], v.first) if isinstance(v, Rows) else ins[i] for i, v in picks]
        body(*views, *results, *own)
        for item in wait:
            item.ready()
        for item in end:
            if isinstance(item, Going):
                item.flush()
        for item in end:
            (item.copy if isinstance(item, Going) else item).wait()

    out_shape = []
    for i, v in enumerate(outs):
        kind = pltpu.HBM if i in away else pltpu.VMEM
        out_shape.append(kind(v.shape, v.dtype))
    out_shape += [pltpu.HBM(values[i].shape, values[i].dtype) for i in saved]
    results = pl.pallas_call(
        kernel,
        out_shape=out_shape,
        in_specs=specs + [vmem] * len(after),
        out_specs=[hbm if i in away else vmem for i in range(len(outs))] + [hbm] * len(saved),
        scratch_shapes=list(scratch)
        + stage
        + leave
        + ([pltpu.SemaphoreType.DMA((moves,))] if moves else []),
        compiler_params=pltpu.CompilerParams(vmem_limit_bytes=VMEM_LIMIT),
        cost_estimate=pl.CostEstimate(flops=0, bytes_accessed=1, transcendentals=0),
        name=name,
    )(*operands, *after)
    answer = list(results[: len(outs)])
    TURN.append(answer.pop())
    for i, home in zip(saved, results[len(outs) :]):
        values[i].home, values[i].near = home, None
    for i in keep:
        answer[i] = Long(answer[i])
    for i in away:
        answer[i] = Long(None, answer[i])
    return answer


def spec_of(value):
    return pl.BlockSpec(memory_space=pltpu.SMEM if value.dtype == jnp.int32 else pltpu.VMEM)


CORE = ((0, 1), (1, 0), (2, 3), (3, 2))
CHIP = ((0, 2), (2, 0), (1, 3), (3, 1))


def near_and_far(value):
    far = lax.ppermute(value, "ch", CHIP)
    return [value, lax.ppermute(value, "ch", CORE), far]


def add_last(blocks, after=None):
    far = blocks[2] if after is None else hold(blocks[2], after)
    blocks.append(lax.ppermute(far, "ch", CORE))


def gather_ch(value):
    blocks = near_and_far(value)
    add_last(blocks)
    return blocks


def hold(value, after):
    return lax.optimization_barrier((value, after))[0]


def swap_img(copies):
    return lax.all_to_all(copies, "img", 0, 0)


class Layer:
    pass


def on_device(
    feats,
    shared_w,
    task_w,
    down_w,
    up_w,
    norm_gain,
    norm_shift,
    bottle_gain,
    bottle_shift,
    seg_mask,
    depth_mask,
    shared_cot,
    task_cot,
):
    images = lax.axis_size("img")
    tasks = task_w.shape[1]
    layers = shared_w.shape[0]
    share = 512 // images
    own = lax.axis_index("ch").astype(jnp.int32).reshape(1)
    img = lax.axis_index("img").astype(jnp.int32).reshape(1)
    shared_taps = shared_w.reshape(2 * layers, 9, 512, 128)
    task_taps = task_w.reshape(tasks * layers, 9, 512, 128)
    widths = [feats.shape[2], feats.shape[2] // 2]
    sizes = [w * w for w in widths]
    counts = [float(images * n) for n in sizes]
    n0, n1 = sizes

    def stats_of(rows, lanes=128):
        return shape_of((rows, lanes))

    one, two = Layer(), Layer()
    kept = [one, two]

    TURN.clear()
    pending, held = [], []

    def total_of(rows, name, first=(), second=(), mid=()):
        if pending:
            rows = hold(rows, list(pending))
            pending.clear()
        low = min(1, bits - 1)
        groups = [range(low, bits), range(low)] if bits <= 3 else [[b] for b in range(bits)]
        for place, group in enumerate(groups):
            shifts = [0]
            for bit in group:
                shifts += [s | 1 << bit for s in shifts]
            parts = [rows] + [
                lax.ppermute(rows, "img", [(i, i ^ s) for i in range(images)]) for s in shifts[1:]
            ]
            last = place == len(groups) - 1
            if place == 0:
                for step in first:
                    step()
            if last:
                for step in second:
                    step()
            rows = run(
                sum_body,
                parts,
                [shape_of(rows.shape)],
                name=f"{name}_{place}",
                keep=(0,) if last else (),
            )[0]
            for blocks in mid if place == 0 else ():
                add_last(blocks, rows.near if last else rows)
        for make in held:
            make(rows.near)
        held.clear()
        return rows

    def gap(steps):
        for step in steps:
            step()
        for make in held:
            make(None)
        held.clear()

    def send_img(value, bit):
        got = lax.ppermute(value, "img", [(i, i ^ (1 << bit)) for i in range(images)])
        pending.append(got)
        return got

    bits = images.bit_length() - 1
    pair_bit = 7 - (share.bit_length() - 1)
    rest = [b for b in range(bits) if b != pair_bit]

    class Weights:
        def __init__(self, l, name):
            self.l, self.name, self.step, self.done = l, name, 0, None

        def take(self, x, place):
            self.x = Taps(x.home.reshape((-1,) + x.shape[-2:]), place, 1)

        def split(self):
            out = run(
                functools.partial(split_body, pair_bit),
                (img, self.x),
                [shape_of((2, sizes[self.l], 128), LOW)],
                name=f"split{self.name}",
            )[0]
            self.later(out, pair_bit, "other_x")

        def later(self, value, bit, name):
            def make(total):
                setattr(self, name, send_img(value if total is None else hold(value, total), bit))

            held.append(make)

        def meet(self, dys, place, other):
            self.dy = Taps(dys.home.reshape((-1,) + dys.shape[-2:]), place, 1)
            self.other_dy = other

        def weigh(self):
            n, half = sizes[self.l], images // 4
            stay, leave = run(
                functools.partial(pair_weight_body, widths[self.l], pair_bit, rest),
                (img, self.x, self.other_x, self.dy, self.other_dy),
                [shape_of((half, 9, share, 128), LOW)] * 2,
                scratch=[pltpu.VMEM((n, 1152), LOW), pltpu.VMEM((256, 1152), F32)],
                name=f"weigh{self.name}",
                away=(0,),
            )
            self.stay, self.step = stay, 1
            self.later(leave, rest[0], "got")

        def halve(self):
            half = self.stay.shape[0] // 2
            stay, leave = run(
                halve_body,
                (self.stay, self.got),
                [shape_of((half, 9, share, 128)), shape_of((half, 9, share, 128), LOW)],
                name=f"halve{self.name}_{self.step}",
                away=(0,),
            )
            self.stay = stay
            self.later(leave, rest[self.step], "got")
            self.step += 1

    class Shared(Weights):
        def __init__(self, name):
            self.name, self.step, self.got = name, 0, None

        def add(self):
            if self.step > 0:
                self.value = run(
                    add_body,
                    (self.value, self.got),
                    [shape_of(self.value.shape, LOW)],
                    name=f"{self.name}_{self.step}",
                    )[0]
            else:
                self.value = self.value.home
            self.later(self.value, self.step, "got")
            self.step += 1

    jobs = {
        name: Weights(int(name[-1]), name)
        for name in ["t0_0", "t1_0", "t2_0", "t0_1", "t1_1", "t2_1", "a_0", "b_0", "a_1", "b_1"]
    }
    for name in ["up_0", "up_1", "down_0", "down_1"]:
        jobs[name] = Shared(name)

    def tasks_of(l):
        return [jobs[f"t{t}_{l}"] for t in range(tasks)]

    def meet(names, dys):
        got = send_img(dys.home, pair_bit)
        if len(names) == 1:
            jobs[names[0]].meet(dys, 0, got)
        else:
            for t, name in enumerate(names):
                jobs[name].meet(dys, t, got[t])

    blocks = near_and_far(feats.reshape(n0, 128))
    add_last(blocks)
    down_w, up_w = Long(None, down_w), Long(None, up_w)
    wide, narrow, params = run(
        pack_body,
        (down_w, up_w, Long(None, norm_gain), Long(None, norm_shift)),
        [
            shape_of((layers, 2, tasks, 128, 128), LOW),
            shape_of((layers, 6, 128)),
            shape_of((layers, 16, 128)),
        ],
        name="pack",
        away=(2,),
    )
    gains = Rows(params, 0, 8)
    norms = (gains, Rows(params, 8, 16))
    bottles = (Long(None, bottle_gain), Long(None, bottle_shift))
    one.x, one.y1, stats = run(
        functools.partial(first_conv_body, widths[0], 0),
        (own, *blocks, Taps(shared_taps, 0, 1)),
        [shape_of((n0, 512), LOW), shape_of((n0, 128)), stats_of(2)],
        name="conv1_0",
        keep=(1,),
        away=(0,),
    )
    wides, narrows = near_and_far(hold(wide, stats)), near_and_far(hold(narrow, stats))
    scales = jnp.stack([seg_mask, depth_mask, jnp.ones_like(seg_mask)]).astype(F32)
    dq = (task_cot.astype(F32) * scales[..., None]).reshape(tasks, n1 // 4, 128)
    dq, dx = Long(dq), Long(shared_cot.astype(F32).reshape(n1 // 4, 128))
    jobs["a_0"].take(one.x, 0)
    one.raw1 = total_of(stats, "total1_0", [jobs["a_0"].split], mid=(wides, narrows))
    one.row1 = 0
    low, one.g = run(
        functools.partial(first_act_body, counts[0]),
        (one.y1, one.raw1, *norms),
        [shape_of((n0, 128), LOW)] * 2,
        name="act1_0",
        away=(1,),
    )
    blocks = gather_ch(low)
    down_all, up_all, gates = run(
        unpack_body,
        (own, *wides, *narrows),
        [
            shape_of((layers, tasks, 512, 128), LOW),
            shape_of((layers, tasks, 128, 512), LOW),
            shape_of((layers, 6, 512)),
        ],
        name="unpack",
        keep=(0,),
        away=(1, 2),
        save=(dq, dx),
    )
    one.x2, one.y2, one.p, stats = run(
        functools.partial(second_conv_body, widths[0], 0),
        (own, *blocks, Taps(shared_taps, 1, 1), down_all),
        [shape_of((n0, 512), LOW), shape_of((n0, 128)), shape_of((tasks, n0, 128)), stats_of(8)],
        name="conv2_0",
        keep=(1, 2),
        away=(0,),
    )
    one.raw2 = total_of(stats, "total2_0")

    def hidden(l):
        k, n = kept[l], sizes[l]
        body = functools.partial(hidden_body, l, counts[l], widths[l])
        outs = [shape_of((tasks, n, 128), LOW)]
        if l == 0:

            def inner(y, p, raw, gain, shift, bgain, bshift, up, s, u, zstats, scratch):
                body(y, p, raw, gain, shift, bgain, bshift, up, s, u, None, zstats, scratch)

            outs += [shape_of((n + n // 4, 128), LOW), stats_of(6, 512)]
        else:
            inner = body
            outs += [shape_of((n, 128), LOW), shape_of((n // 4, 128), LOW), stats_of(6, 512)]
        return run(
            inner,
            (k.y2, k.p, k.raw2, *norms, *bottles, up_all),
            outs,
            scratch=[pltpu.VMEM((n, 128), F32)],
            name=f"hidden_{l}",
            keep=(0,),
        )

    def task_convs(l, u_blocks, taps, more=None):
        k, n = kept[l], sizes[l]
        body = functools.partial(task_conv_body, l, counts[l], widths[l])
        args = (own, k.s, up_all, *u_blocks, k.zraw, gates, taps)
        if more is None:

            def inner(ch, s, up, u0, u1, u2, u3, zraw, gt, taps, kk, y, stats, full, acc):
                body(ch, s, up, u0, u1, u2, u3, zraw, gt, taps, None, kk, y, stats, full, acc)

        else:
            inner = body
            args += (more,)
        return run(
            inner,
            args,
            [
                shape_of((tasks, n, 512), LOW),
                shape_of((tasks, n, 128)),
                stats_of(6 if more is None else 8),
            ],
            scratch=[pltpu.VMEM((n, 512), LOW), pltpu.VMEM((tasks, 2, 128), F32)],
            name=f"taskconv_{l}",
            keep=(1,),
            away=(0,),
        )

    one.s, u, zstats = hidden(0)
    u_blocks = near_and_far(u)

    def next_conv():
        two.x, two.y1, two.more = run(
            functools.partial(next_conv_body, widths[1], 0, n0),
            (own, *u_blocks, Taps(shared_taps, 2, 1)),
            [shape_of((n1, 512), LOW), shape_of((n1, 128)), shape_of((2, 128))],
            name="conv1_1",
            away=(0, 1),
        )

    jobs["b_0"].take(one.x2, 0)
    one.zraw = total_of(zstats, "totalz_0", [jobs["b_0"].split], [next_conv], mid=(u_blocks,))
    one.k, one.yt, stats = task_convs(0, u_blocks, Taps(task_taps, 0, tasks), two.more)
    for t, job in enumerate(tasks_of(0)):
        job.take(one.k, t)
    one.traw = total_of(stats, "totalt_0", *[[job.split] for job in tasks_of(0)[:2]])
    two.raw1, two.row1 = one.traw, 6

    low, two.g, part = run(
        functools.partial(attend_body, counts[0], counts[1], widths[0]),
        (one.yt, two.y1, one.traw, *norms, down_w),
        [
            shape_of((n1, 128), LOW),
            shape_of((tasks, n1, 128), LOW),
            shape_of((tasks, n1, 128), LOW),
        ],
        scratch=[pltpu.VMEM((n0, 128), F32)],
        name="attend_1",
        away=(1,),
    )

    def sum_ch(value, name):
        got = lax.ppermute(value, "ch", CORE)
        near = run(pair_body, (value, got), [shape_of(value.shape, LOW)], name=name)[0]
        return near, lax.ppermute(near, "ch", CHIP)

    blocks = gather_ch(low)
    halves = sum_ch(part, "pairp_1")
    two.x2, two.y2, two.p, stats = run(
        functools.partial(second_conv_next_body, widths[1], 0),
        (own, *blocks, Taps(shared_taps, 3, 1), *halves),
        [shape_of((n1, 512), LOW), shape_of((n1, 128)), shape_of((tasks, n1, 128)), stats_of(8)],
        name="conv2_1",
        keep=(1, 2),
        away=(0,),
    )
    two.raw2 = total_of(stats, "total2_1")
    jobs["a_1"].take(two.x, 0)
    jobs["b_1"].take(two.x2, 0)
    two.s, u, shared_out, zstats = hidden(1)
    u_blocks = near_and_far(u)
    two.zraw = total_of(zstats, "totalz_1", mid=(u_blocks,))
    two.k, two.yt, stats = task_convs(1, u_blocks, Taps(task_taps, tasks, tasks))
    for t, job in enumerate(tasks_of(1)):
        job.take(two.k, t)
    two.traw = total_of(stats, "totalt_1")

    task_out, d, stats = run(
        functools.partial(task_last_body, 1, counts[1], widths[1]),
        (two.yt, two.traw, *norms, dq),
        [shape_of((tasks, n1 // 4, 128), LOW), shape_of((tasks, n1, 128)), stats_of(6)],
        scratch=[pltpu.VMEM((n1, 128), F32)],
        name="tasklast_1",
    )
    splits = [job.split for job in tasks_of(1)]
    two.dtraw = total_of(stats, "dtotalt_1", splits[:2], splits[2:])
    two.dtrow = 0

    def back_outs(n, lead=()):
        return [
            shape_of(lead + (n, 128), LOW),
            shape_of((2,) + lead + (n, 128), LOW),
            shape_of(lead + (n, 128)),
            shape_of(lead + (n, 128)),
        ]

    def back_scratch(n):
        return [pltpu.VMEM((n, 1152), LOW), pltpu.VMEM((n, 512), F32)]

    def scatter_ch(send, keep, far, name, away=()):
        near, part = run(
            pair_second_body,
            (keep, far, lax.ppermute(send, "ch", CORE)),
            [shape_of(far.shape, LOW), shape_of(far.shape)],
            name=name,
            away=away,
        )
        return (part, lax.ppermute(near, "ch", CHIP))

    def steps(weigh="", halve="", add="", split=""):
        return (
            [jobs[name].weigh for name in weigh.split()]
            + [jobs[name].halve for name in halve.split()]
            + [jobs[name].add for name in add.split()]
            + [jobs[name].split for name in split.split()]
        )

    plan = {
        "gate_1": (steps("t0_1", "", "", "t2_0"), steps("t1_1", "", "", "b_1")),
        "bottle_1": (steps("t2_1", "", "", "a_1"), steps()),
        "first_1": (steps("b_1", "t0_1"), steps("", "t1_1")),
        "gate_0": (steps("t0_0"), steps("", "t2_1")),
        "hidden_0": steps("a_1 t1_0", "b_1", "up_1 down_1"),
        "bottle_0": (steps("t2_0"), steps("", "t0_0", "up_1 down_1")),
        "first_0": (steps("b_0"), steps("", "t1_0 a_1", "up_0")),
    }
    unfinished = None

    for l in range(layers - 1, -1, -1):
        k, n, w, count = kept[l], sizes[l], widths[l], counts[l]
        dys, send, keep, far = run(
            functools.partial(task_back_body, l, count, w, k.dtrow),
            (own, d, k.yt, k.traw, k.dtraw, gains, Taps(task_taps, tasks * l, tasks)),
            back_outs(n, (tasks,)),
            scratch=back_scratch(n),
            name=f"taskback_{l}",
            away=(0,),
        )
        meet([f"t{t}_{l}" for t in range(tasks)], dys)
        if unfinished is not None:
            parts_before = unfinished()
        parts = scatter_ch(send, keep, far, f"pairr_{l}")
        gap(plan.get(f"task_{l}", ()))
        if unfinished is not None:
            dx = run(mixed_body, parts_before, [shape_of((sizes[l + 1], 128))], name=f"dx_{l + 1}")[0]
        d, d2, stats = run(
            functools.partial(gate_grad_body, l, count, w),
            (own, *parts, k.s, up_w, k.zraw, k.y2, k.raw2, *norms, dx),
            [shape_of((tasks, n, 128)), shape_of((n, 128)), stats_of(8)],
            scratch=[pltpu.VMEM((n, 128), F32)],
            name=f"gategrad_{l}",
        )
        k.draw2 = total_of(stats, f"dtotal2_{l}", *plan[f"gate_{l}"])
        d2 = Long(d2)
        ds, dup = run(
            functools.partial(hidden_grad_body, l, count),
            (own, d, k.s, up_w, k.zraw, k.draw2, gains),
            [shape_of((tasks, n, 128), LOW), shape_of((tasks, 128, 128), LOW)],
            name=f"hiddengrad_{l}",
            away=(1,),
            save=(d2,),
        )
        jobs[f"up_{l}"].value = dup
        got = lax.ppermute(ds, "ch", CORE)
        near = run(pair_body, (ds, got), [shape_of(ds.shape, LOW)], name=f"pairs_{l}")[0]
        halves = near, lax.ppermute(near, "ch", CHIP)

        def conv2_back(ch, d, y, raw, draw, gain, taps, *rest, l=l, count=count, w=w):
            conv_back_body(l, 1, count, w, ch, d, y, raw, 0, draw, gain, taps, *rest)

        dys, send, keep, far = run(
            conv2_back,
            (own, d2, k.y2, k.raw2, k.draw2, gains, Taps(shared_taps, 2 * l + 1, 1)),
            back_outs(n),
            scratch=back_scratch(n),
            name=f"conv2back_{l}",
            away=(0,),
        )
        meet([f"b_{l}"], dys)
        parts = scatter_ch(send, keep, far, f"pairv_{l}", (1,))
        gap(plan.get(f"hidden_{l}", ()))
        d, stats = run(
            functools.partial(bottle_grad_body, l, count),
            (*halves, k.p, k.raw2, *bottles),
            [shape_of((tasks, n, 128)), stats_of(6)],
            name=f"bottlegrad_{l}",
        )
        k.draw3 = total_of(stats, f"dtotal3_{l}", *plan[f"bottle_{l}"])
        args = (d, k.p, k.raw2, k.draw3, bottles[0], k.g, down_w, *parts, k.y1, k.raw1, *norms)
        outs = [shape_of((tasks, 128, 128), LOW), shape_of((n, 128))]
        if l > 0:
            ddown, d1, stats, d = run(
                functools.partial(
                    attend_grad_first_body, l, count, k.row1, counts[l - 1], widths[l - 1]
                ),
                args + (kept[l - 1].yt, kept[l - 1].traw),
                outs + [stats_of(8), shape_of((tasks, sizes[l - 1], 128))],
                scratch=[pltpu.VMEM((sizes[l - 1], 128), F32)],
                name=f"attendgrad_{l}",
                away=(0,),
            )
        else:
            ddown, d1, stats = run(
                functools.partial(attend_grad_last_body, l, count, k.row1),
                args,
                outs + [stats_of(2)],
                name=f"attendgrad_{l}",
                away=(0,),
            )
        jobs[f"down_{l}"].value = ddown
        k.draw1 = total_of(stats, f"dtotal1_{l}", *plan[f"first_{l}"])
        if l > 0:
            kept[l - 1].dtraw, kept[l - 1].dtrow = k.draw1, 2
            d1 = Long(d1)

        def conv1_back(ch, d, y, raw, draw, gain, taps, *rest, l=l, count=count, w=w, row=k.row1):
            conv_back_body(l, 0, count, w, ch, d, y, raw, row, draw, gain, taps, *rest)

        dys, send, keep, far = run(
            conv1_back,
            (own, d1, k.y1, k.raw1, k.draw1, gains, Taps(shared_taps, 2 * l, 1)),
            back_outs(n),
            scratch=back_scratch(n),
            name=f"conv1back_{l}",
            away=(0,),
        )
        meet([f"a_{l}"], dys)

        def unfinished(l=l, send=send, keep=keep, far=far):
            return scatter_ch(send, keep, far, f"pairx_{l}")

    parts = unfinished()
    rows_of = [k.draw1, k.draw2, k.dtraw, k.draw3]
    gap(steps("", "t2_0", "down_0 up_0"))
    dx = run(mixed_body, parts, [shape_of((n0, 128))], name="dx_0", away=(0,))[0].home
    gap(steps("a_0", "b_0"))
    order, places = [], []
    for k in kept:
        base = len(places)
        places += [k.draw1, k.draw2, k.dtraw, k.draw3]
        rows = [(base, 0), (base + 1, 0)]
        rows += [(base + 2, k.dtrow + 2 * t) for t in range(3)]
        rows += [(base + 1, 2 + 2 * t) for t in range(3)]
        rows += [(base + 3, 2 * t) for t in range(3)]
        order.append(rows)

    def norms_body(*refs):
        finish_body(order, refs[: len(places)], *refs[len(places) :])

    gains = run(
        norms_body,
        places,
        [shape_of((layers, 8, 128))] * 2 + [shape_of((layers, tasks, 128))] * 2,
        name="norms",
    )
    gap(steps("", "", "down_0 up_0"))
    gap(steps("", "a_0", "down_0"))
    while any(job.step < (bits if isinstance(job, Shared) else len(rest)) for job in jobs.values()):
        for job in jobs.values():
            if job.step < (bits if isinstance(job, Shared) else len(rest)):
                gap([job.add if isinstance(job, Shared) else job.halve])

    names = ["b_0", "a_1", "b_1"]
    names += [f"t{t}_{l}" for l in range(layers) for t in range(tasks)]
    sums = ["up_0", "up_1", "down_0", "down_1"]
    pieces = []
    for name in names:
        pieces += [jobs[name].stay, jobs[name].got]
    for name in sums:
        pieces += [jobs[name].value, jobs[name].got]

    def finish(*refs):
        sw, tw, down, up = refs[len(pieces) :]
        for i in range(len(names)):
            value = refs[2 * i][0].astype(F32) + refs[2 * i + 1][0].astype(F32)
            if i < 3:
                sw[i + 1] = value
            else:
                tw[i - 3] = value
        flush(tw)
        flush(sw)
        for i in range(len(sums)):
            first, second = refs[2 * (len(names) + i)], refs[2 * (len(names) + i) + 1]
            value = first[...].astype(F32) + second[...].astype(F32)
            (up if i < layers else down)[i % layers] = value

    sw, tw, down, up = run(
        finish,
        pieces,
        [
            shape_of((2 * layers, 9, share, 128)),
            shape_of((tasks * layers, 9, share, 128)),
            shape_of((layers, tasks, 128, 128)),
            shape_of((layers, tasks, 128, 128)),
        ],
        name="finish",
        away=range(4),
    )
    tw, down, up = tw.home, down.home, up.home

    def put_body(buffer, stay, got, turn, out, total, sem):
        total[...] = stay[0].astype(F32) + got[0].astype(F32)
        copy = pltpu.make_async_copy(total, out.at[0], sem)
        copy.start()
        copy.wait()

    job = jobs["a_0"]
    hbm, vmem = pl.BlockSpec(memory_space=pltpu.HBM), pl.BlockSpec(memory_space=pltpu.VMEM)
    sw = pl.pallas_call(
        put_body,
        out_shape=pltpu.HBM(sw.shape, F32),
        in_specs=[hbm, vmem, vmem, vmem],
        out_specs=hbm,
        input_output_aliases={0: 0},
        scratch_shapes=[pltpu.VMEM((9, share, 128), F32), pltpu.SemaphoreType.DMA],
        compiler_params=pltpu.CompilerParams(vmem_limit_bytes=VMEM_LIMIT),
        name="put",
    )(pltpu.with_memory_space_constraint(sw.home, pltpu.HBM), job.stay.home, job.got, TURN.pop())
    return (
        shared_out.reshape(1, widths[1] // 2, widths[1] // 2, 128),
        task_out.reshape(tasks, 1, widths[1] // 2, widths[1] // 2, 128),
        dx.reshape(1, widths[0], widths[0], 128),
        sw.reshape(layers, 2, 3, 3, share, 128),
        tw.reshape(layers, tasks, 3, 3, share, 128),
        down,
        up,
        *gains,
    )


def solution(mesh):
    placed = (
        P("img", None, None, "ch"),
        P(None, None, None, None, None, "ch"),
        P(None, None, None, None, None, "ch"),
        P(None, None, "ch", None),
        P(None, None, None, "ch"),
        P(None, None, "ch"),
        P(None, None, "ch"),
        P(),
        P(),
        P("img", None, None),
        P("img", None, None),
        P("img", None, None, "ch"),
        P(None, "img", None, None, "ch"),
    )
    return jax.shard_map(
        on_device,
        mesh=mesh,
        in_specs=placed,
        out_specs=(
            P("img", None, None, "ch"),
            P(None, "img", None, None, "ch"),
            P("img", None, None, "ch"),
            P(None, None, None, None, "img", "ch"),
            P(None, None, None, None, "img", "ch"),
            P(None, None, "ch", None),
            P(None, None, None, "ch"),
            P(None, None, "ch"),
            P(None, None, "ch"),
            P(),
            P(),
        ),
        check_vma=False,
    )
```

```python
import functools

import jax
import jax.numpy as jnp
from jax import lax
from jax.experimental import pallas as pl
from jax.experimental.pallas import tpu as pltpu
from jax.sharding import PartitionSpec as P

EPSILON = 1e-05
F32 = jnp.float32
LOW = jnp.bfloat16
VMEM_LIMIT = 16 * 2**20


def sigmoid(v):
    return 0.5 * jnp.tanh(0.5 * v) + 0.5


def silu_slope(v, s):
    return s * (1.0 + v * (1.0 - s))


def dot(a, b):
    return lax.dot_general(a, b, (((1,), (0,)), ((), ())), preferred_element_type=F32)


def dot_nt(a, b):
    return lax.dot_general(a, b, (((1,), (1,)), ((), ())), preferred_element_type=F32)


def dot_tn(a, b):
    return lax.dot_general(a, b, (((0,), (0,)), ((), ())), preferred_element_type=F32)


def sums(v):
    return jnp.sum(v, axis=0, keepdims=True)


def column_of(shape, width):
    place = lax.broadcasted_iota(jnp.int32, shape, 0)
    row = (place * (2731 if width == 24 else 5462)) >> 16
    return place - row * width


def move_columns(v, step, width):
    if step == 0:
        return v
    column = column_of(v.shape, width)
    keep = column < width - 1 if step == 1 else column > 0
    return jnp.where(keep, pltpu.roll(v, (-step) % v.shape[0], 0), 0.0)


def move_rows(v, step, width):
    if step == 0:
        return v
    size = v.shape[0]
    place = lax.broadcasted_iota(jnp.int32, v.shape, 0)
    keep = place < size - width if step == 1 else place >= width
    return jnp.where(keep, pltpu.roll(v, (-step * width) % size, 0), 0.0)


def centre(total, count):
    mean = total[0:1] / count
    spread = total[1:2] / count - mean * mean
    return mean, lax.rsqrt(spread + EPSILON)


def place_blocks(ch_ref, blocks, full_ref):
    own = ch_ref[0]
    for k, block in enumerate(blocks):
        start = pl.multiple_of((own ^ k) * 128, 128)
        full_ref[:, pl.ds(start, 128)] = block[...]


def conv(values, taps_ref, lead, width):
    total = None
    for col in range(3):
        kernel = jnp.concatenate([taps_ref[lead, 3 * row + col] for row in range(3)], 1)
        part = dot(values, kernel)
        line = part[:, 128:256]
        line = line + move_rows(part[:, 0:128], -1, width)
        line = line + move_rows(part[:, 256:384], 1, width)
        line = move_columns(line, col - 1, width)
        total = line if total is None else total + line
    return total


def spread_taps(grad, width, taps_out):
    for col in range(3):
        line = move_columns(grad, 1 - col, width)
        for row in range(3):
            tap = 3 * row + col
            taps_out[:, tap * 128 : tap * 128 + 128] = move_rows(line, 1 - row, width).astype(LOW)


def conv_back(taps_value, taps_ref, lead):
    kernel = jnp.concatenate([taps_ref[lead, tap] for tap in range(9)], 1)
    return dot_nt(taps_value, kernel)


def pool(v, scratch, width):
    size = v.shape[0]
    if width % 8 == 0:
        pairs = v.reshape(size // (2 * width), 2 * width, 128)
        rows = (pairs[:, :width] + pairs[:, width:]).reshape(size // 2, 128)
        scratch[0 : size // 2] = rows
        return 0.25 * (
            scratch[pl.ds(0, size // 4, stride=2)] + scratch[pl.ds(1, size // 4, stride=2)]
        )
    v = v + pltpu.roll(v, size - width, 0)
    v = v + pltpu.roll(v, size - 1, 0)
    scratch[...] = v
    half = scratch[pl.ds(0, size // 2, stride=2)]
    scratch[0 : size // 2] = half
    parts = [scratch[a * width : a * width + width // 2] for a in range(size // (2 * width))]
    return 0.25 * jnp.concatenate(parts, 0)


def unpool(v, scratch, width):
    size = 4 * v.shape[0]
    v = 0.25 * v
    scratch[pl.ds(0, size // 4, stride=2)] = v
    scratch[pl.ds(1, size // 4, stride=2)] = v
    rows = scratch[0 : size // 2]
    if width % 8 == 0:
        rows = rows.reshape(size // (2 * width), width, 128)
        return jnp.concatenate([rows, rows], 1).reshape(size, 128)
    parts = []
    for a in range(size // (2 * width)):
        part = rows[a * width : a * width + width]
        parts += [part, part]
    return jnp.concatenate(parts, 0)

def bn_of(total, row, count):
    return centre(total[row : row + 2], count)


def spread_stats(out, rows):
    for place, row in enumerate(rows):
        if len(out.shape) == 2:
            out[place : place + 1] = row
        else:
            out[:, place : place + 1] = jnp.broadcast_to(row[None], (out.shape[0],) + row.shape)


def moments(v):
    return [sums(v), sums(v * v)]


def pack_body(down, up, gain, shift, wide, narrow, params):
    for l in range(down.shape[0]):
        wide[l, 0] = down[l]
        wide[l, 1] = up[l]
        narrow[l, 0:3] = gain[l, 5:8]
        narrow[l, 3:6] = shift[l, 5:8]
        params[l, 0:8] = gain[l, 0:8]
        params[l, 8:16] = shift[l, 0:8]


def unpack_body(ch, w0, w1, w2, w3, n0, n1, n2, n3, down, up, gates):
    own = ch[0]
    for k, (wide, narrow) in enumerate(((w0, n0), (w1, n1), (w2, n2), (w3, n3))):
        start = pl.ds(pl.multiple_of((own ^ k) * 128, 128), 128)
        for l in range(down.shape[0]):
            for t in range(3):
                down[l, t, start, :] = wide[l, 0, t]
                up[l, t, :, start] = wide[l, 1, t]
            gates[l, :, start] = narrow[l]


def first_conv_body(width, lead, ch, x0, x1, x2, x3, taps, full, y, stats):
    place_blocks(ch, (x0, x1, x2, x3), full)
    flush(full)
    out = conv(full[...], taps, lead, width)
    y[...] = out
    spread_stats(stats, moments(out))


def next_conv_body(width, lead, skip, ch, x0, x1, x2, x3, taps, full, y, stats):
    own = ch[0]
    for k, block in enumerate((x0, x1, x2, x3)):
        start = pl.multiple_of((own ^ k) * 128, 128)
        full[:, pl.ds(start, 128)] = block[skip:]
    flush(full)
    out = conv(full[...], taps, lead, width)
    y[...] = out
    for place, row in enumerate(moments(out)):
        stats[place : place + 1] = row


def first_act_body(count, y, raw, gain, shift, low, again):
    mean, inverse = bn_of(raw, 0, count)
    v = (y[...] - mean) * inverse * gain[0, 0:1] + shift[0, 0:1]
    act = (v * sigmoid(v)).astype(LOW)
    low[...] = act
    again[...] = act


def second_conv_body(width, lead, ch, x0, x1, x2, x3, taps, down, full, y, p, stats):
    place_blocks(ch, (x0, x1, x2, x3), full)
    flush(full)
    values = full[...]
    out = conv(values, taps, lead, width)
    y[...] = out
    rows = moments(out)
    for t in range(3):
        part = dot(values, down[0, t])
        p[t] = part
        rows += moments(part)
    spread_stats(stats, rows)


def second_conv_next_body(width, lead, ch, x0, x1, x2, x3, taps, near, far, full, y, p, stats):
    place_blocks(ch, (x0, x1, x2, x3), full)
    flush(full)
    out = conv(full[...], taps, lead, width)
    y[...] = out
    rows = moments(out)
    for t in range(3):
        part = near[t].astype(F32) + far[t].astype(F32)
        p[t] = part
        rows += moments(part)
    spread_stats(stats, rows)


def hidden_body(l, count, width, y, p, raw, gain, shift, bgain, bshift, up, s, u, pooled_u, zstats, scratch):
    mean, inverse = bn_of(raw, 0, count)
    v = (y[...] - mean) * inverse * gain[l, 1:2] + shift[l, 1:2]
    act = v * sigmoid(v)
    size = y.shape[0]
    u[0:size] = act.astype(LOW)
    pooled = pool(act, scratch, width).astype(LOW)
    if pooled_u is None:
        u[size:] = pooled
    else:
        pooled_u[...] = pooled
    rows = []
    for t in range(3):
        mean, inverse = bn_of(raw, 2 + 2 * t, count)
        v = (p[t] - mean) * inverse * bgain[l, t : t + 1] + bshift[l, t : t + 1]
        low = (v * sigmoid(v)).astype(LOW)
        s[t] = low
        rows += moments(dot(low, up[l, t]))
    spread_stats(zstats, rows)


def task_conv_body(l, count, width, ch, s, up, u0, u1, u2, u3, zraw, gates, taps, more, k, y, stats, full, acc):
    size = s.shape[1]
    own = ch[0]
    for i, block in enumerate((u0, u1, u2, u3)):
        start = pl.multiple_of((own ^ i) * 128, 128)
        full[:, pl.ds(start, 128)] = block[0:size]
    ztotal = zraw[...]
    for t in range(3):
        mean, inverse = centre(ztotal[2 * t : 2 * t + 2], count)
        scale = inverse * gates[l, t : t + 1]
        v = dot(s[t], up[l, t]) * scale + (gates[l, 3 + t : 4 + t] - mean * scale)
        k[t] = (sigmoid(v) * full[...].astype(F32)).astype(LOW)
    flush(k)
    ready(taps)

    def one(t, carry):
        out = conv(k[t], taps, t, width)
        y[t] = out
        rows = moments(out)
        acc[t, 0:1] = rows[0]
        acc[t, 1:2] = rows[1]
        return carry

    lax.fori_loop(0, 3, one, 0)
    rows = [acc[t, i : i + 1] for t in range(3) for i in range(2)]
    if more is not None:
        rows += [more[0:1], more[1:2]]
    spread_stats(stats, rows)


def attend_body(count, count_next, width, yt, y, raw, gain, shift, down, low, g, part, scratch):
    mean, inverse = bn_of(raw, 6, count_next)
    v = (y[...] - mean) * inverse * gain[1, 0:1] + shift[1, 0:1]
    act = v * sigmoid(v)
    low[...] = act.astype(LOW)
    for t in range(3):
        mean, inverse = bn_of(raw, 2 * t, count)
        v = (yt[t] - mean) * inverse * gain[0, 2 + t : 3 + t] + shift[0, 2 + t : 3 + t]
        attend = (act + pool(v * sigmoid(v), scratch, width)).astype(LOW)
        g[t] = attend
        part[t] = dot(attend, down[1, t]).astype(LOW)


def pair_body(a, b, out):
    out[...] = (a[...].astype(F32) + b[...].astype(F32)).astype(LOW)


def pair_second_body(keep, far, got, out, part):
    out[...] = (far[...] + got[1].astype(F32)).astype(LOW)
    part[...] = keep[...] + got[0].astype(F32)


def pair_tasks_body(keep, far, got, keep_x, far_x, got_x, out, part, part_x):
    size = far.shape[1]
    for t in range(far.shape[0]):
        out[t * size : (t + 1) * size] = (far[t] + got[1, t].astype(F32)).astype(LOW)
        part[t] = keep[t] + got[0, t].astype(F32)
    out[far.shape[0] * size :] = (far_x[...] + got_x[1].astype(F32)).astype(LOW)
    part_x[...] = keep_x[...] + got_x[0].astype(F32)


def mixed_body(a, b, out):
    out[...] = a[...] + b[...].astype(F32)


def stack_body(a, b, out):
    out[0] = a[...]
    out[1] = b[...]


def add_body(a, b, out):
    out[...] = (a[...].astype(F32) + b[...].astype(F32)).astype(out.dtype)


def sum_body(copies, out):
    total = copies[0]
    for i in range(1, copies.shape[0]):
        total = total + copies[i]
    out[...] = total


def sum_all_body(*refs):
    parts = [ref[...] for ref in refs[:-1]]
    while len(parts) > 1:
        parts = [a + b for a, b in zip(parts[::2], parts[1::2])]
    refs[-1][...] = parts[0]


def mark_body(out):
    out[...] = jnp.zeros_like(out)


def task_last_body(l, count, width, y, raw, gain, shift, dq, out, d, stats, scratch):
    rows = []
    for t in range(3):
        mean, inverse = bn_of(raw, 2 * t, count)
        normal = (y[t] - mean) * inverse
        v = normal * gain[l, 2 + t : 3 + t] + shift[l, 2 + t : 3 + t]
        sg = sigmoid(v)
        out[t] = pool(v * sg, scratch, width).astype(LOW)
        grad = unpool(dq[t], scratch, width) * silu_slope(v, sg)
        d[t] = grad
        rows += [sums(grad), sums(grad * normal)]
    spread_stats(stats, rows)


def norm_back(d, y, bn, dtotal, gain, count):
    mean, inverse = bn
    scale = gain * inverse
    normal = (y - mean) * inverse
    return scale * (d - dtotal[0:1] / count - normal * (dtotal[1:2] / count))


def input_grads(width, ch, dy, taps, lead, outs, cat, dv):
    spread_taps(dy, width, cat)
    dv[...] = conv_back(cat[...], taps, lead)
    own = ch[0]
    blocks = []
    for k in range(4):
        start = pl.multiple_of((own ^ k) * 128, 128)
        blocks.append(dv[:, pl.ds(start, 128)])
    return blocks


def task_back_body(l, count, width, row0, ch, d, y, raw, draw, gain, taps, dys, send, keep, far, cat, dv):
    total = raw[...]
    dtotal = draw[...]
    for t in range(3):
        bn = centre(total[2 * t : 2 * t + 2], count)
        dts = dtotal[row0 + 2 * t : row0 + 2 * t + 2]
        dy = norm_back(d[t], y[t], bn, dts, gain[l, 2 + t : 3 + t], count)
        dys[t] = dy.astype(LOW)
    ready(taps)

    def one(t, carry):
        blocks = input_grads(width, ch, dys[t].astype(F32), taps, t, None, cat, dv)
        send[0, t] = blocks[1].astype(LOW)
        send[1, t] = blocks[3].astype(LOW)
        keep[t] = blocks[0]
        far[t] = blocks[2]
        return carry

    lax.fori_loop(0, 3, one, 0)


def conv_back_body(l, k, count, width, ch, d, y, raw, rawrow, draw, gain, taps, dys, send, keep, far, cat, dv):
    dtotal = draw[0:2]
    dy = norm_back(d[...], y[...], bn_of(raw, rawrow, count), dtotal, gain[l, k : k + 1], count)
    dys[...] = dy.astype(LOW)
    blocks = input_grads(width, ch, dy, taps, 0, None, cat, dv)
    send[0] = blocks[1].astype(LOW)
    send[1] = blocks[3].astype(LOW)
    keep[...] = blocks[0]
    far[...] = blocks[2]


def task_weights_body(width, x, dys, out, cat, total):
    ready(x)
    ready(dys)

    def one(t, carry):
        spread_taps(dys.ref[t].astype(F32), width, cat)
        total[...] = dot_tn(x.ref[t], cat[...])
        for tap in range(9):
            out.ref[t, tap] = total[:, tap * 128 : tap * 128 + 128].astype(LOW)
        return carry

    lax.fori_loop(0, 3, one, 0)


def widen_body(*refs):
    out = refs[-1]
    first = 0
    for ref in refs[:-1]:
        last = first + ref.shape[0]
        out[first:last] = ref[...].astype(F32)
        first = last


def split_body(bit, im, *refs):
    out = refs[-1]
    low = (im[0] >> bit) & 1
    for n, x in enumerate(refs[:-1]):
        ready(x)
        for i in range(2):
            start = pl.multiple_of((2 * i + 1 - low) * 128, 128)
            out[n, i] = x.ref[0, :, pl.ds(start, 128)]


def pair_weight_body(width, bit, rest, picks, im, *refs):
    stay, leave, cat, total = refs[-4:]
    low = (im[0] >> bit) & 1
    half = stay.shape[0]
    share = stay.shape[3]
    for n, (place_x, place_dy) in enumerate(picks):
        x, other_x, dy, other_dy = refs[4 * n : 4 * n + 4]
        ready(x)
        ready(dy)
        mine = [
            x.ref[0, :, pl.ds(pl.multiple_of((2 * i + low) * 128, 128), 128)] for i in range(2)
        ]
        spread_taps(dy[0].astype(F32), width, cat)
        total[...] = dot_tn(jnp.concatenate(mine, 1), cat[...])
        theirs = [other_x[place_x, i] for i in range(2)]
        grad = other_dy[...] if place_dy is None else other_dy[place_dy]
        spread_taps(grad.astype(F32), width, cat)
        total[...] += dot_tn(jnp.concatenate(theirs, 1), cat[...])
        for e in range(2 * half):
            mask = 0
            for s, b in enumerate(rest):
                mask |= ((e >> (len(rest) - 1 - s)) & 1) << b
            block = im[0] ^ mask
            row = ((block >> (bit + 1)) & 1) * 128 + (block & ((1 << bit) - 1)) * share
            rows = pl.ds(pl.multiple_of(row, share), share)
            target = stay if e < half else leave
            for tap in range(9):
                target[e % half, n, tap] = total[rows, tap * 128 : tap * 128 + 128].astype(LOW)


def halve_body(*refs):
    stay, leave = refs[-2:]
    half = stay.shape[0]
    first = 0
    for a, b in zip(refs[:-2:2], refs[1:-2:2]):
        last = first + a.shape[1]
        for i in range(half):
            stay[i, first:last] = a[i].astype(F32) + b[i].astype(F32)
            leave[i, first:last] = (a[half + i].astype(F32) + b[half + i].astype(F32)).astype(LOW)
        first = last


def flat_body(*refs):
    out = refs[-1]
    share = out.shape[1]
    rows = [ref[t] for ref in refs[:-1] for t in range(ref.shape[0])]
    whole = jnp.concatenate(rows, 0)
    for i in range(out.shape[0]):
        out[i] = whole[i * share : (i + 1) * share]


def spread_sum_body(copies, out):
    total = copies[0].astype(F32)
    for i in range(1, copies.shape[0]):
        total = total + copies[i].astype(F32)
    out[...] = jnp.broadcast_to(total.astype(LOW)[None], out.shape)


def gate_grad_body(l, count, width, ch, part, far, s, up, zraw, y, raw, gain, shift, dx, d, d2, stats, scratch):
    size = y.shape[0]
    if len(dx) == 1:
        grad = dx[0][...]
    else:
        grad = dx[0][...] + far[3 * size :].astype(F32)
    mean, inverse = bn_of(raw, 0, count)
    normal = (y[...] - mean) * inverse
    v = normal * gain[l, 1:2] + shift[l, 1:2]
    sg = sigmoid(v)
    act = v * sg
    own = pl.ds(pl.multiple_of(ch[0] * 128, 128), 128)
    ztotal = zraw[:, own]
    upstream = unpool(grad, scratch, width)
    rows = []
    for t in range(3):
        zmean, zinverse = centre(ztotal[2 * t : 2 * t + 2], count)
        znormal = (dot(s[t], up[l, t]) - zmean) * zinverse
        m = sigmoid(znormal * gain[l, 5 + t : 6 + t] + shift[l, 5 + t : 6 + t])
        dr = part[t] + (far[t] if len(dx) == 1 else far[t * size : (t + 1) * size]).astype(F32)
        through = dr * m
        upstream = upstream + through
        grad = through * act * (1.0 - m)
        d[t] = grad
        rows += [sums(grad), sums(grad * znormal)]
    grad = upstream * silu_slope(v, sg)
    d2[...] = grad
    spread_stats(stats, [sums(grad), sums(grad * normal)] + rows)


def hidden_grad_body(l, count, ch, d, s, up, zraw, draw, gain, ds, dup):
    own = pl.ds(pl.multiple_of(ch[0] * 128, 128), 128)
    ztotal = zraw[:, own]
    dtotal = draw[2:8]
    for t in range(3):
        z = dot(s[t], up[l, t])
        rows = slice(2 * t, 2 * t + 2)
        bn = centre(ztotal[rows], count)
        dz = norm_back(d[t], z, bn, dtotal[rows], gain[l, 5 + t : 6 + t], count).astype(LOW)
        dup[t] = dot_tn(s[t], dz).astype(LOW)
        ds[t] = dot_nt(dz, up[l, t]).astype(LOW)


def bottle_grad_body(l, count, ds0, ds1, p, raw, bgain, bshift, d, stats):
    rows = []
    for t in range(3):
        mean, inverse = bn_of(raw, 2 + 2 * t, count)
        normal = (p[t] - mean) * inverse
        v = normal * bgain[l, t : t + 1] + bshift[l, t : t + 1]
        grad = (ds0[t].astype(F32) + ds1[t].astype(F32)) * silu_slope(v, sigmoid(v))
        d[t] = grad
        rows += [sums(grad), sums(grad * normal)]
    spread_stats(stats, rows)


def attend_grad_body(l, count, rawrow, d, p, raw, draw, bgain, g, down, part, far, y, raw1, gain, shift, more, ddown, d1, stats, more_out):
    upstream = part[...] + far[...].astype(F32)
    dtotal = draw[...]
    rows = []
    for t in range(3):
        bn = bn_of(raw, 2 + 2 * t, count)
        dp = norm_back(d[t], p[t], bn, dtotal[2 * t : 2 * t + 2], bgain[l, t : t + 1], count).astype(LOW)
        ddown[t] = dot_tn(g[...] if more is None else g[t], dp).astype(LOW)
        grad = dot_nt(dp, down[l, t])
        upstream = upstream + grad
        if more is not None:
            yt, traw, tcount, twidth, scratch = more
            mean, inverse = bn_of(traw, 2 * t, tcount)
            normal = (yt[t] - mean) * inverse
            v = normal * gain[l - 1, 2 + t : 3 + t] + shift[l - 1, 2 + t : 3 + t]
            grad = unpool(grad, scratch, twidth) * silu_slope(v, sigmoid(v))
            more_out[t] = grad
            rows += [sums(grad), sums(grad * normal)]
    mean, inverse = bn_of(raw1, rawrow, count)
    normal = (y[...] - mean) * inverse
    v = normal * gain[l, 0:1] + shift[l, 0:1]
    grad = upstream * silu_slope(v, sigmoid(v))
    d1[...] = grad
    spread_stats(stats, [sums(grad), sums(grad * normal)] + rows)


def attend_grad_last_body(l, count, rawrow, d, p, raw, draw, bgain, g, down, part, far, y, raw1, gain, shift, ddown, d1, stats):
    attend_grad_body(l, count, rawrow, d, p, raw, draw, bgain, g, down, part, far, y, raw1, gain, shift, None, ddown, d1, stats, None)


def attend_grad_first_body(l, count, rawrow, tcount, twidth, d, p, raw, draw, bgain, g, down, part, far, y, raw1, gain, shift, yt, traw, ddown, d1, stats, dt, scratch):
    more = (yt, traw, tcount, twidth, scratch)
    attend_grad_body(l, count, rawrow, d, p, raw, draw, bgain, g, down, part, far, y, raw1, gain, shift, more, ddown, d1, stats, dt)


def finish_body(order, refs_in, gain, shift, bgain, bshift):
    for l in range(gain.shape[0]):
        for row, (place, start) in enumerate(order[l]):
            total = refs_in[place][start : start + 2]
            if row < 8:
                shift[l, row : row + 1] = total[0:1]
                gain[l, row : row + 1] = total[1:2]
            else:
                bshift[l, row - 8 : row - 7] = total[0:1]
                bgain[l, row - 8 : row - 7] = total[1:2]


def shape_of(shape, dtype=F32):
    return jax.ShapeDtypeStruct(tuple(shape), dtype)


class Long:
    def __init__(self, near, home=None):
        self.near, self.home = near, home
        some = home if near is None else near
        self.shape, self.dtype = some.shape, some.dtype


class Taps:
    def __init__(self, home, first, count):
        self.home, self.first, self.shape = home, first, (count,) + home.shape[1:]
        self.dtype, self.near = home.dtype, None


class Rows:
    def __init__(self, whole, first, last):
        self.whole, self.first, self.last = whole, first, last


class Coming:
    def __init__(self, ref, copy):
        self.ref, self.copy, self.shape, self.dtype = ref, copy, ref.shape, ref.dtype

    def ready(self):
        if self.copy is not None:
            self.copy.wait()
            self.copy = None

    def __getitem__(self, place):
        self.ready()
        return self.ref[place]


class Going:
    def __init__(self, ref, copy):
        self.ref, self.copy, self.shape, self.dtype = ref, copy, ref.shape, ref.dtype
        self.started = False

    def flush(self):
        if not self.started:
            self.copy.start()
            self.started = True

    def __getitem__(self, place):
        return self.ref[place]

    def __setitem__(self, place, value):
        self.ref[place] = value


class SomeRows:
    def __init__(self, ref, first):
        self.ref, self.first = ref, first

    def __getitem__(self, place):
        layer, rows = place
        return self.ref[layer, self.first + rows.start : self.first + rows.stop]


def ready(ref):
    if isinstance(ref, Coming):
        ref.ready()


def flush(ref):
    if isinstance(ref, Going):
        ref.flush()


TURN = []


def run(body, args, outs, scratch=(), name=None, keep=(), away=(), save=(), after=()):
    values, picks = [], []
    for v in list(args) + list(save):
        whole = v.whole if isinstance(v, Rows) else v
        place = next((i for i, other in enumerate(values) if other is whole), None)
        if place is None:
            place = len(values)
            values.append(whole)
        picks.append((place, v))
    picks = picks[: len(args)]
    count = len(values)
    far = [isinstance(v, (Taps, Long)) and v.near is None for v in values]
    saved = [i for i, v in enumerate(values) if isinstance(v, Long) and v.home is None]
    hbm, vmem = pl.BlockSpec(memory_space=pltpu.HBM), pl.BlockSpec(memory_space=pltpu.VMEM)
    operands, specs = [], []
    for v, apart in zip(values, far):
        if apart:
            operands.append(pltpu.with_memory_space_constraint(v.home, pltpu.HBM))
            specs.append(hbm)
        else:
            operands.append(v.near if isinstance(v, (Taps, Long)) else v)
            specs.append(spec_of(operands[-1]))
    after = list(after) + TURN
    TURN.clear()
    outs = list(outs) + [shape_of((8, 128))]
    stage = [pltpu.VMEM(v.shape, v.dtype) for v, apart in zip(values, far) if apart]
    leave = [pltpu.VMEM(outs[i].shape, outs[i].dtype) for i in away]
    moves = len(stage) + len(leave) + len(saved)

    def kernel(*refs):
        ins = list(refs[:count])
        results = list(refs[count + len(after) : count + len(after) + len(outs)])
        homes = refs[count + len(after) + len(outs) :][: len(saved)]
        rest = refs[count + len(after) + len(outs) + len(saved) :]
        own, rest = rest[: len(scratch)], rest[len(scratch) :]
        sems = rest[-1] if moves else None
        wait = []
        slot = 0
        for i in range(count):
            if not far[i]:
                continue
            source = ins[i]
            if isinstance(values[i], Taps):
                source = source.at[values[i].first : values[i].first + values[i].shape[0]]
            copy = pltpu.make_async_copy(source, rest[slot], sems.at[slot])
            copy.start()
            ins[i] = Coming(rest[slot], copy)
            wait.append(ins[i])
            slot += 1
        end = []
        for i, home in zip(saved, homes):
            copy = pltpu.make_async_copy(ins[i], home, sems.at[slot])
            copy.start()
            end.append(copy)
            slot += 1
        for n, i in enumerate(away):
            ref = rest[len(stage) + n]
            copy = pltpu.make_async_copy(ref, results[i], sems.at[slot])
            results[i] = Going(ref, copy)
            end.append(results[i])
            slot += 1
        turn = results.pop()
        turn[...] = jnp.zeros_like(turn)
        views = [SomeRows(ins[i], v.first) if isinstance(v, Rows) else ins[i] for i, v in picks]
        body(*views, *results, *own)
        for item in wait:
            item.ready()
        for item in end:
            if isinstance(item, Going):
                item.flush()
        for item in end:
            (item.copy if isinstance(item, Going) else item).wait()

    out_shape = []
    for i, v in enumerate(outs):
        kind = pltpu.HBM if i in away else pltpu.VMEM
        out_shape.append(kind(v.shape, v.dtype))
    out_shape += [pltpu.HBM(values[i].shape, values[i].dtype) for i in saved]
    results = pl.pallas_call(
        kernel,
        out_shape=out_shape,
        in_specs=specs + [vmem] * len(after),
        out_specs=[hbm if i in away else vmem for i in range(len(outs))] + [hbm] * len(saved),
        scratch_shapes=list(scratch)
        + stage
        + leave
        + ([pltpu.SemaphoreType.DMA((moves,))] if moves else []),
        compiler_params=pltpu.CompilerParams(vmem_limit_bytes=VMEM_LIMIT),
        cost_estimate=pl.CostEstimate(flops=0, bytes_accessed=1, transcendentals=0),
        name=name,
    )(*operands, *after)
    answer = list(results[: len(outs)])
    TURN.append(answer.pop())
    for i, home in zip(saved, results[len(outs) :]):
        values[i].home = home
    for v in values:
        if isinstance(v, (Taps, Long)):
            v.near = None
    for i in keep:
        answer[i] = Long(answer[i])
    for i in away:
        answer[i] = Long(None, answer[i])
    return answer


def bring(items, name):
    items = [v for v in items if v.near is None]
    if not items:
        return
    count = len(items)

    def body(*refs):
        turn, sems = refs[2 * count + 1], refs[-1]
        copies = []
        for i, item in enumerate(items):
            source = refs[i]
            if isinstance(item, Taps):
                source = source.at[item.first : item.first + item.shape[0]]
            copies.append(pltpu.make_async_copy(source, refs[count + 1 + i], sems.at[i]))
            copies[-1].start()
        turn[...] = jnp.zeros_like(turn)
        for copy in copies:
            copy.wait()

    hbm, vmem = pl.BlockSpec(memory_space=pltpu.HBM), pl.BlockSpec(memory_space=pltpu.VMEM)
    results = pl.pallas_call(
        body,
        out_shape=[pltpu.VMEM(v.shape, v.dtype) for v in items] + [pltpu.VMEM((8, 128), F32)],
        in_specs=[hbm] * count + [vmem],
        out_specs=[vmem] * (count + 1),
        scratch_shapes=[pltpu.SemaphoreType.DMA((count,))],
        compiler_params=pltpu.CompilerParams(vmem_limit_bytes=VMEM_LIMIT),
        cost_estimate=pl.CostEstimate(flops=0, bytes_accessed=1, transcendentals=0),
        name=name,
    )(*[pltpu.with_memory_space_constraint(v.home, pltpu.HBM) for v in items], TURN.pop())
    TURN.append(results[count])
    for v, near in zip(items, results):
        v.near = near


def spec_of(value):
    return pl.BlockSpec(memory_space=pltpu.SMEM if value.dtype == jnp.int32 else pltpu.VMEM)


CORE = ((0, 1), (1, 0), (2, 3), (3, 2))
CHIP = ((0, 2), (2, 0), (1, 3), (3, 1))


def near_and_far(value):
    far = lax.ppermute(value, "ch", CHIP)
    return [value, lax.ppermute(value, "ch", CORE), far]


def add_last(blocks, after=None):
    far = blocks[2] if after is None else hold(blocks[2], after)
    blocks.append(lax.ppermute(far, "ch", CORE))


def gather_ch(value):
    blocks = near_and_far(value)
    add_last(blocks)
    return blocks


def hold(value, after):
    return lax.optimization_barrier((value, after))[0]


def swap_img(copies):
    return lax.all_to_all(copies, "img", 0, 0)


class Layer:
    pass


def on_device(
    feats,
    shared_w,
    task_w,
    down_w,
    up_w,
    norm_gain,
    norm_shift,
    bottle_gain,
    bottle_shift,
    seg_mask,
    depth_mask,
    shared_cot,
    task_cot,
):
    images = lax.axis_size("img")
    tasks = task_w.shape[1]
    layers = shared_w.shape[0]
    share = 512 // images
    own = lax.axis_index("ch").astype(jnp.int32).reshape(1)
    img = lax.axis_index("img").astype(jnp.int32).reshape(1)
    shared_taps = shared_w.reshape(2 * layers, 9, 512, 128)
    task_taps = task_w.reshape(tasks * layers, 9, 512, 128)
    widths = [feats.shape[2], feats.shape[2] // 2]
    sizes = [w * w for w in widths]
    counts = [float(images * n) for n in sizes]
    n0, n1 = sizes

    def stats_of(rows, lanes=128):
        return shape_of((images, rows, lanes))

    one, two = Layer(), Layer()
    kept = [one, two]

    TURN.clear()
    pending, held = [], []

    def total_of(copies, name, steps=(), mid=(), ahead=()):
        if pending:
            copies = hold(copies, list(pending))
            pending.clear()
        got = swap_img(copies)
        if mid and not steps:
            run(mark_body, (), [shape_of((8, 128))], name="mark")
        for place, step in enumerate(steps):
            step()
            if place == 0:
                for blocks in mid:
                    add_last(blocks, TURN[0])
        if mid and not steps:
            for blocks in mid:
                add_last(blocks, TURN[0])
        bring(ahead, f"bring{name}")
        total = run(sum_body, (got,), [shape_of(copies.shape[1:])], name=name, keep=(0,))[0]
        for make in held:
            make(total.near)
        held.clear()
        return total

    def total_by_pairs(rows, name, first, second, mid, ahead=()):
        if pending:
            rows = hold(rows, list(pending))
            pending.clear()
        low = min(1, bits - 1)
        groups = [range(low, bits), range(low)] if bits <= 3 else [[b] for b in range(bits)]
        for place, group in enumerate(groups):
            shifts = [0]
            for bit in group:
                shifts += [s | 1 << bit for s in shifts]
            parts = [rows] + [
                lax.ppermute(rows, "img", [(i, i ^ s) for i in range(images)]) for s in shifts[1:]
            ]
            last = place == len(groups) - 1
            for step in (first if place == 0 else []) + (second if last else []):
                step()
            if place == 0:
                bring(ahead, f"bring{name}")
            rows = run(
                sum_all_body,
                parts,
                [shape_of(rows.shape)],
                name=f"{name}_{place}",
                keep=(0,) if last else (),
            )[0]
            for blocks in mid if place == 0 else ():
                add_last(blocks, rows.near if last else rows)
        for make in held:
            make(rows.near)
        held.clear()
        return rows

    def gap(steps):
        waiting = list(held)
        held.clear()
        for step in steps:
            step()
        for make in held:
            make(None)
        held[:] = waiting

    def send_img(value, bit):
        got = lax.ppermute(value, "img", [(i, i ^ (1 << bit)) for i in range(images)])
        pending.append(got)
        return got

    bits = images.bit_length() - 1
    pair_bit = 7 - (share.bit_length() - 1)
    rest = [b for b in range(bits) if b != pair_bit]

    def later(owner, field, value, bit):
        def make(total):
            setattr(owner, field, send_img(value if total is None else hold(value, total), bit))

        held.append(make)

    class Meeting:
        pass

    class Conv:
        def __init__(self, name):
            self.name, self.l = name, int(name[-1])

        def take(self, x, place):
            self.x = Taps(x.home.reshape((-1,) + x.shape[-2:]), place, 1)

    class Split:
        def __init__(self, names):
            self.names = names
            for place, name in enumerate(names):
                convs[name].split, convs[name].place_x = self, place

        def go(self):
            members = [convs[name] for name in self.names]
            out = run(
                functools.partial(split_body, pair_bit),
                (img, *[c.x for c in members]),
                [shape_of((len(members), 2, sizes[members[0].l], 128), LOW)],
                name="split" + "".join(self.names),
            )[0]
            later(self, "got", out, pair_bit)

    class Weights:
        def __init__(self, names):
            self.members, self.name, self.step = [convs[n] for n in names], "".join(names), 0
            self.parts, self.placed = [self], False

        def weigh(self):
            l = self.members[0].l
            args, picks = [], []
            for c in self.members:
                args += [c.x, c.split.got, c.dy, c.meeting.got]
                picks.append((c.place_x, c.place_dy))
            shape = shape_of((images // 4, len(picks), 9, share, 128), LOW)
            self.stay, leave = run(
                functools.partial(pair_weight_body, widths[l], pair_bit, rest, picks),
                (img, *args),
                [shape] * 2,
                scratch=[pltpu.VMEM((sizes[l], 1152), LOW), pltpu.VMEM((256, 1152), F32)],
                name=f"weigh{self.name}",
                away=(0,),
            )
            self.step = 1
            later(self, "got", leave, rest[0])

        def halve(self):
            args = []
            for part in self.parts:
                args += [part.stay, part.got]
            self.step = self.parts[0].step
            self.parts = [self]
            shape = (args[0].shape[0] // 2, len(self.members)) + args[0].shape[2:]
            self.stay, leave = run(
                halve_body,
                args,
                [shape_of(shape), shape_of(shape, LOW)],
                name=f"halve{self.name}_{self.step}",
                away=(0,),
            )
            later(self, "got", leave, rest[self.step])
            self.step += 1

        def put(self):
            self.placed = True
            places = [PLACES[c.name] for c in self.members]
            first = list(buffers)
            count = len(places)

            def body(*refs):
                stay, got, _, turn, out, value, other, sems = refs[len(first) :]
                load = pltpu.make_async_copy(stay.at[0], other, sems.at[count])
                load.start()
                turn[...] = jnp.zeros_like(turn)
                load.wait()
                copies = []
                for n, place in enumerate(places):
                    value[n] = other[n].astype(F32) + got[0, n].astype(F32)
                    copies.append(pltpu.make_async_copy(value.at[n], out.at[place], sems.at[n]))
                    copies[-1].start()
                for copy in copies:
                    copy.wait()

            stay = self.stay.home
            turn, *buffers[:] = pl.pallas_call(
                body,
                out_shape=[
                    pltpu.VMEM((8, 128), F32),
                    pltpu.HBM((2 * layers, 9, share, 128), F32),
                ],
                in_specs=[hbm] * len(first) + [hbm, vmem, vmem],
                out_specs=[vmem, hbm],
                input_output_aliases={i: i + 1 for i in range(len(first))},
                scratch_shapes=[
                    pltpu.VMEM((count, 9, share, 128), F32),
                    pltpu.VMEM((count, 9, share, 128), stay.dtype),
                    pltpu.SemaphoreType.DMA((count + 1,)),
                ],
                compiler_params=pltpu.CompilerParams(vmem_limit_bytes=VMEM_LIMIT),
                cost_estimate=pl.CostEstimate(flops=0, bytes_accessed=1, transcendentals=0),
                name=f"put{self.name}",
            )(
                *[pltpu.with_memory_space_constraint(v, pltpu.HBM) for v in first],
                pltpu.with_memory_space_constraint(stay, pltpu.HBM),
                self.got,
                TURN.pop(),
            )
            TURN.append(turn)

    hbm, vmem = pl.BlockSpec(memory_space=pltpu.HBM), pl.BlockSpec(memory_space=pltpu.VMEM)
    buffers = []
    PLACES = {"a_0": 0, "b_0": 1, "a_1": 2, "b_1": 3}
    convs = {name: Conv(name) for name in PLACES}

    jobs = {names: Weights(names.split()) for names in ["b_1", "a_1", "b_0", "a_0"]}
    splits = {names: Split(names.split()) for names in ["b_0", "a_0", "b_1 a_1"]}

    def task_weights(l):
        k = kept[l]
        out = run(
            functools.partial(task_weights_body, widths[l]),
            (k.k, k.dys),
            [shape_of((tasks, 9, 512, 128), LOW)],
            scratch=[pltpu.VMEM((sizes[l], 1152), LOW), pltpu.VMEM((512, 1152), F32)],
            name=f"weight_{l}",
            away=(0,),
        )[0]

        def make(total):
            value = out.home if total is None else hold(out.home, total)
            k.task_w = lax.psum_scatter(value, "img", scatter_dimension=2, tiled=True)

        held.append(make)

    def meet(names, dys, wait=False):
        for t, name in enumerate(names):
            c = convs[name]
            c.dy = Taps(dys.home.reshape((-1,) + dys.shape[-2:]), t, 1)
            c.meeting, c.place_dy = Meeting(), t if len(names) > 1 else None
        meeting = convs[names[0]].meeting
        for name in names:
            convs[name].meeting = meeting
        if wait:
            later(meeting, "got", dys.home, pair_bit)
        else:
            meeting.got = send_img(dys.home, pair_bit)

    blocks = near_and_far(feats.reshape(n0, 128))
    down_w, up_w = Long(None, down_w), Long(None, up_w)
    wide, narrow, params = run(
        pack_body,
        (down_w, up_w, Long(None, norm_gain), Long(None, norm_shift)),
        [
            shape_of((layers, 2, tasks, 128, 128), LOW),
            shape_of((layers, 6, 128)),
            shape_of((layers, 16, 128)),
        ],
        name="pack",
        away=(2,),
    )
    gains = Rows(params, 0, 8)
    norms = (gains, Rows(params, 8, 16))
    add_last(blocks, TURN[0])
    blocks[0] = Long(None, blocks[0])
    bottles = (Long(None, bottle_gain), Long(None, bottle_shift))
    one.x, one.y1, stats = run(
        functools.partial(first_conv_body, widths[0], 0),
        (own, *blocks, Taps(shared_taps, 0, 1)),
        [shape_of((n0, 512), LOW), shape_of((n0, 128)), stats_of(2)],
        name="conv1_0",
        keep=(1,),
        away=(0,),
    )
    wides, narrows = near_and_far(hold(wide, stats)), near_and_far(hold(narrow, stats))
    scales = jnp.stack([seg_mask, depth_mask, jnp.ones_like(seg_mask)]).astype(F32)
    dq = (task_cot.astype(F32) * scales[..., None]).reshape(tasks, n1 // 4, 128)
    dq, dx = Long(dq), Long(shared_cot.astype(F32).reshape(n1 // 4, 128))
    convs["a_0"].take(one.x, 0)
    one.raw1 = total_of(
        stats, "total1_0", [splits["a_0"].go], (wides, narrows), [params]
    )
    one.row1 = 0
    low, one.g = run(
        functools.partial(first_act_body, counts[0]),
        (one.y1, one.raw1, *norms),
        [shape_of((n0, 128), LOW)] * 2,
        name="act1_0",
        away=(1,),
    )
    blocks = gather_ch(low)
    down_all, up_all, gates = run(
        unpack_body,
        (own, *wides, *narrows),
        [
            shape_of((layers, tasks, 512, 128), LOW),
            shape_of((layers, tasks, 128, 512), LOW),
            shape_of((layers, 6, 512)),
        ],
        name="unpack",
        keep=(0,),
        away=(1, 2),
        save=(dq, dx),
    )
    one.x2, one.y2, one.p, stats = run(
        functools.partial(second_conv_body, widths[0], 0),
        (own, *blocks, Taps(shared_taps, 1, 1), down_all),
        [shape_of((n0, 512), LOW), shape_of((n0, 128)), shape_of((tasks, n0, 128)), stats_of(8)],
        name="conv2_0",
        keep=(1, 2),
        away=(0,),
    )
    one.raw2 = total_of(stats, "total2_0", ahead=[params, up_all, *bottles])

    def hidden(l):
        k, n = kept[l], sizes[l]
        body = functools.partial(hidden_body, l, counts[l], widths[l])
        outs = [shape_of((tasks, n, 128), LOW)]
        if l == 0:

            def inner(y, p, raw, gain, shift, bgain, bshift, up, s, u, zstats, scratch):
                body(y, p, raw, gain, shift, bgain, bshift, up, s, u, None, zstats, scratch)

            outs += [shape_of((n + n // 4, 128), LOW), shape_of((6, 512))]
        else:
            inner = body
            outs += [shape_of((n, 128), LOW), shape_of((n // 4, 128), LOW), stats_of(6, 512)]
        return run(
            inner,
            (k.y2, k.p, k.raw2, *norms, *bottles, up_all),
            outs,
            scratch=[pltpu.VMEM((n, 128), F32)],
            name=f"hidden_{l}",
            keep=(0,),
        )

    def task_convs(l, u_blocks, taps, more=None):
        k, n = kept[l], sizes[l]
        body = functools.partial(task_conv_body, l, counts[l], widths[l])
        args = (own, k.s, up_all, *u_blocks, k.zraw, gates, taps)
        if more is None:

            def inner(ch, s, up, u0, u1, u2, u3, zraw, gt, taps, kk, y, stats, full, acc):
                body(ch, s, up, u0, u1, u2, u3, zraw, gt, taps, None, kk, y, stats, full, acc)

        else:
            inner = body
            args += (more,)
        return run(
            inner,
            args,
            [
                shape_of((tasks, n, 512), LOW),
                shape_of((tasks, n, 128)),
                stats_of(6 if more is None else 8),
            ],
            scratch=[pltpu.VMEM((n, 512), LOW), pltpu.VMEM((tasks, 2, 128), F32)],
            name=f"taskconv_{l}",
            keep=(1,),
            away=(0,),
        )

    one.s, u, zstats = hidden(0)
    u_blocks = near_and_far(u)

    def next_conv():
        two.x, two.y1, two.more = run(
            functools.partial(next_conv_body, widths[1], 0, n0),
            (own, *u_blocks, Taps(shared_taps, 2, 1)),
            [shape_of((n1, 512), LOW), shape_of((n1, 128)), shape_of((2, 128))],
            name="conv1_1",
            away=(0, 1),
        )

    convs["b_0"].take(one.x2, 0)
    taps = Taps(task_taps, 0, tasks)
    one.zraw = total_by_pairs(
        zstats, "totalz_0", [], [next_conv], (u_blocks,), [up_all, gates, taps]
    )
    one.k, one.yt, stats = task_convs(0, u_blocks, taps, two.more)
    one.traw = total_of(
        stats, "totalt_0", [splits["b_0"].go], ahead=[params, down_w, two.y1]
    )
    two.raw1, two.row1 = one.traw, 6

    low, two.g, part = run(
        functools.partial(attend_body, counts[0], counts[1], widths[0]),
        (one.yt, two.y1, one.traw, *norms, down_w),
        [
            shape_of((n1, 128), LOW),
            shape_of((tasks, n1, 128), LOW),
            shape_of((tasks, n1, 128), LOW),
        ],
        scratch=[pltpu.VMEM((n0, 128), F32)],
        name="attend_1",
        away=(1,),
    )

    def sum_ch(value, name):
        got = lax.ppermute(value, "ch", CORE)
        near = run(pair_body, (value, got), [shape_of(value.shape, LOW)], name=name)[0]
        return near, lax.ppermute(near, "ch", CHIP)

    blocks = gather_ch(low)
    halves = sum_ch(part, "pairp_1")
    two.x2, two.y2, two.p, stats = run(
        functools.partial(second_conv_next_body, widths[1], 0),
        (own, *blocks, Taps(shared_taps, 3, 1), *halves),
        [shape_of((n1, 512), LOW), shape_of((n1, 128)), shape_of((tasks, n1, 128)), stats_of(8)],
        name="conv2_1",
        keep=(1, 2),
        away=(0,),
    )
    two.raw2 = total_of(stats, "total2_1", ahead=[params, up_all, *bottles])
    convs["a_1"].take(two.x, 0)
    convs["b_1"].take(two.x2, 0)
    two.s, u, shared_out, zstats = hidden(1)
    u_blocks = near_and_far(u)
    taps = Taps(task_taps, tasks, tasks)
    two.zraw = total_of(zstats, "totalz_1", [splits["b_1 a_1"].go], (u_blocks,))
    two.k, two.yt, stats = task_convs(1, u_blocks, taps)
    two.traw = total_of(stats, "totalt_1")

    task_out, d, stats = run(
        functools.partial(task_last_body, 1, counts[1], widths[1]),
        (two.yt, two.traw, *norms, dq),
        [shape_of((tasks, n1 // 4, 128), LOW), shape_of((tasks, n1, 128)), stats_of(6)],
        scratch=[pltpu.VMEM((n1, 128), F32)],
        name="tasklast_1",
    )
    taps = Taps(task_taps, tasks, tasks)
    two.dtraw = total_of(
        stats,
        "dtotalt_1",
    )
    two.dtrow = 0

    def back_outs(n, lead=()):
        return [
            shape_of(lead + (n, 128), LOW),
            shape_of((2,) + lead + (n, 128), LOW),
            shape_of(lead + (n, 128)),
            shape_of(lead + (n, 128)),
        ]

    def back_scratch(n):
        return [pltpu.VMEM((n, 1152), LOW), pltpu.VMEM((n, 512), F32)]

    def scatter_ch(send, keep, far, name, away=()):
        near, part = run(
            pair_second_body,
            (keep, far, lax.ppermute(send, "ch", CORE)),
            [shape_of(far.shape, LOW), shape_of(far.shape)],
            name=name,
            away=away,
        )
        return (part, lax.ppermute(near, "ch", CHIP))

    def steps(weigh="", halve="", split="", put=""):
        kinds = ((jobs, weigh, "weigh"), (jobs, halve, "halve"))
        kinds += ((splits, split, "go"), (jobs, put, "put"))
        return [
            getattr(table[name], kind)
            for table, names, kind in kinds
            for name in names.split(", ")
            if name
        ]

    flat = []

    def flatten():
        rows = run(
            flat_body,
            [part for k in kept for part in k.both],
            [shape_of((images, layers * 2 * tasks * 128 // images, 128), LOW)],
            name="flat",
        )[0]
        flat.append(swap_img(rows))

    plan = {
        "gate_1": [functools.partial(task_weights, 1)],
        "bottle_1": (),
        "first_1": steps("b_1"),
        "gate_0": steps("", "b_1"),
        "bottle_0": steps("a_1"),
        "first_0": steps("b_0", "a_1") + [flatten],
    }
    unfinished = None

    for l in range(layers - 1, -1, -1):
        k, n, w, count = kept[l], sizes[l], widths[l], counts[l]
        dys, send, keep, far = run(
            functools.partial(task_back_body, l, count, w, k.dtrow),
            (own, d, k.yt, k.traw, k.dtraw, gains, taps),
            back_outs(n, (tasks,)),
            scratch=back_scratch(n),
            name=f"taskback_{l}",
            away=(0,),
        )
        k.dys = dys
        if unfinished is None:
            parts = scatter_ch(send, keep, far, f"pairr_{l}")
            rest_dx = dx
        else:
            send_x, keep_x, far_x = unfinished
            near, part, rest_dx = run(
                pair_tasks_body,
                (
                    keep,
                    far,
                    lax.ppermute(send, "ch", CORE),
                    keep_x,
                    far_x,
                    lax.ppermute(send_x, "ch", CORE),
                ),
                [
                    shape_of((tasks * n + sizes[l + 1], 128), LOW),
                    shape_of((tasks, n, 128)),
                    shape_of((sizes[l + 1], 128)),
                ],
                name=f"pairr_{l}",
            )
            parts = (part, lax.ppermute(near, "ch", CHIP))
        if l == 0:
            task_weights(0)

        def gate_grad(ch, part, far, s, up, zraw, y, raw, gain, shift, dx, *rest, first=unfinished, l=l, w=w):
            more = (dx,) if first is None else (dx, far)
            gate_grad_body(l, counts[l], w, ch, part, far, s, up, zraw, y, raw, gain, shift, more, *rest)

        d, d2, stats = run(
            gate_grad,
            (own, *parts, k.s, up_w, k.zraw, k.y2, k.raw2, *norms, rest_dx),
            [shape_of((tasks, n, 128)), shape_of((n, 128)), stats_of(8)],
            scratch=[pltpu.VMEM((n, 128), F32)],
            name=f"gategrad_{l}",
        )
        k.draw2 = total_of(
            stats, f"dtotal2_{l}", plan[f"gate_{l}"], ahead=[k.s, up_w, k.zraw, params]
        )
        d2 = Long(d2)
        ds, dup = run(
            functools.partial(hidden_grad_body, l, count),
            (own, d, k.s, up_w, k.zraw, k.draw2, gains),
            [shape_of((tasks, n, 128), LOW), shape_of((tasks, 128, 128), LOW)],
            name=f"hiddengrad_{l}",
            away=(1,),
            save=(d2,),
        )
        k.dup = dup
        got = lax.ppermute(ds, "ch", CORE)
        near = run(pair_body, (ds, got), [shape_of(ds.shape, LOW)], name=f"pairs_{l}")[0]
        halves = near, lax.ppermute(near, "ch", CHIP)

        def conv2_back(ch, d, y, raw, draw, gain, taps, *rest, l=l, count=count, w=w):
            conv_back_body(l, 1, count, w, ch, d, y, raw, 0, draw, gain, taps, *rest)

        dys, send, keep, far = run(
            conv2_back,
            (own, d2, k.y2, k.raw2, k.draw2, gains, Taps(shared_taps, 2 * l + 1, 1)),
            back_outs(n),
            scratch=back_scratch(n),
            name=f"conv2back_{l}",
            away=(0,),
        )
        meet([f"b_{l}"], dys)
        parts = scatter_ch(send, keep, far, f"pairv_{l}", (1,))
        gap(plan.get(f"hidden_{l}", ()))
        d, stats = run(
            functools.partial(bottle_grad_body, l, count),
            (*halves, k.p, k.raw2, *bottles),
            [shape_of((tasks, n, 128)), stats_of(6)],
            name=f"bottlegrad_{l}",
        )
        wanted = [k.p, k.raw2, bottles[0], k.g, down_w, k.y1, k.raw1, params]
        if l > 0:
            wanted += [kept[l - 1].yt, kept[l - 1].traw]
        k.draw3 = total_of(stats, f"dtotal3_{l}", plan[f"bottle_{l}"], ahead=wanted if l == 0 else ())
        args = (d, k.p, k.raw2, k.draw3, bottles[0], k.g, down_w, *parts, k.y1, k.raw1, *norms)
        outs = [shape_of((tasks, 128, 128), LOW), shape_of((n, 128))]
        if l > 0:
            ddown, d1, stats, d = run(
                functools.partial(
                    attend_grad_first_body, l, count, k.row1, counts[l - 1], widths[l - 1]
                ),
                args + (kept[l - 1].yt, kept[l - 1].traw),
                outs + [stats_of(8), shape_of((tasks, sizes[l - 1], 128))],
                scratch=[pltpu.VMEM((sizes[l - 1], 128), F32)],
                name=f"attendgrad_{l}",
                away=(0,),
            )
        else:
            ddown, d1, stats = run(
                functools.partial(attend_grad_last_body, l, count, k.row1),
                args,
                outs + [stats_of(2)],
                name=f"attendgrad_{l}",
                away=(0,),
            )
        k.both = [ddown, k.dup]
        last_taps = Taps(shared_taps, 2 * l, 1)
        wanted = [k.y1, k.raw1, params, last_taps]
        if l > 0:
            taps = Taps(task_taps, tasks * (l - 1), tasks)
            wanted.append(taps)
        k.draw1 = total_of(stats, f"dtotal1_{l}", plan[f"first_{l}"], ahead=wanted if l == 0 else ())
        if l > 0:
            kept[l - 1].dtraw, kept[l - 1].dtrow = k.draw1, 2
            d1 = Long(d1)

        def conv1_back(ch, d, y, raw, draw, gain, taps, *rest, l=l, count=count, w=w, row=k.row1):
            conv_back_body(l, 0, count, w, ch, d, y, raw, row, draw, gain, taps, *rest)

        dys, send, keep, far = run(
            conv1_back,
            (own, d1, k.y1, k.raw1, k.draw1, gains, last_taps),
            back_outs(n),
            scratch=back_scratch(n),
            name=f"conv1back_{l}",
            away=(0,),
        )
        meet([f"a_{l}"], dys)

        unfinished = (send, keep, far)

    parts = scatter_ch(*unfinished, "pairx_0")
    every = ["b_1", "a_1", "b_0", "a_0"]

    def put_ready(names):
        for name in names:
            if jobs[name].step == len(rest) and not jobs[name].placed:
                jobs[name].put()

    put_ready(every[:2])
    gap(steps("a_0"))
    gap(steps("", "b_0"))
    dx = run(mixed_body, parts, [shape_of((n0, 128))], name="dx_0", away=(0,))[0].home
    gap(steps("", "a_0"))
    flat = run(spread_sum_body, flat, [shape_of(flat[0].shape, LOW)], name="spread")[0]
    flat = swap_img(flat)
    tw = run(
        widen_body,
        [Long(None, k.task_w) for k in kept],
        [shape_of((tasks * layers, 9, share, 128))],
        name="tasksout",
        away=(0,),
    )[0].home

    order, places = [], []
    for k in kept:
        base = len(places)
        places += [k.draw1, k.draw2, k.dtraw, k.draw3]
        rows = [(base, 0), (base + 1, 0)]
        rows += [(base + 2, k.dtrow + 2 * t) for t in range(3)]
        rows += [(base + 1, 2 + 2 * t) for t in range(3)]
        rows += [(base + 3, 2 * t) for t in range(3)]
        order.append(rows)

    def norms_body(*refs):
        finish_body(order, refs[: len(places)], *refs[len(places) :])

    gains = run(
        norms_body,
        places,
        [shape_of((layers, 8, 128))] * 2 + [shape_of((layers, tasks, 128))] * 2,
        name="norms",
    )
    while any(jobs[name].step < len(rest) for name in every):
        for name in every:
            if jobs[name].step < len(rest):
                gap([jobs[name].halve])
    put_ready(every[:3])
    flat = hold(flat, TURN[0])
    put_ready(every)
    flat = flat.reshape(layers, 2, tasks, 128, 128).astype(F32)
    down, up = flat[:, 0], flat[:, 1]
    (sw,) = buffers
    return (
        shared_out.reshape(1, widths[1] // 2, widths[1] // 2, 128),
        task_out.reshape(tasks, 1, widths[1] // 2, widths[1] // 2, 128),
        dx.reshape(1, widths[0], widths[0], 128),
        sw.reshape(layers, 2, 3, 3, share, 128),
        tw.reshape(layers, tasks, 3, 3, share, 128),
        down,
        up,
        *gains,
    )


def solution(mesh):
    placed = (
        P("img", None, None, "ch"),
        P(None, None, None, None, None, "ch"),
        P(None, None, None, None, None, "ch"),
        P(None, None, "ch", None),
        P(None, None, None, "ch"),
        P(None, None, "ch"),
        P(None, None, "ch"),
        P(),
        P(),
        P("img", None, None),
        P("img", None, None),
        P("img", None, None, "ch"),
        P(None, "img", None, None, "ch"),
    )
    return jax.shard_map(
        on_device,
        mesh=mesh,
        in_specs=placed,
        out_specs=(
            P("img", None, None, "ch"),
            P(None, "img", None, None, "ch"),
            P("img", None, None, "ch"),
            P(None, None, None, None, "img", "ch"),
            P(None, None, None, None, "img", "ch"),
            P(None, None, "ch", None),
            P(None, None, None, "ch"),
            P(None, None, "ch"),
            P(None, None, "ch"),
            P(),
            P(),
        ),
        check_vma=False,
    )
```

```python
import functools

import jax
import jax.numpy as jnp
from jax import lax
from jax.experimental import pallas as pl
from jax.experimental.pallas import tpu as pltpu
from jax.sharding import PartitionSpec as P

EPSILON = 1e-05
F32 = jnp.float32
LOW = jnp.bfloat16
VMEM_LIMIT = 16 * 2**20


def sigmoid(v):
    return 0.5 * jnp.tanh(0.5 * v) + 0.5


def silu_slope(v, s):
    return s * (1.0 + v * (1.0 - s))


def dot(a, b):
    return lax.dot_general(a, b, (((1,), (0,)), ((), ())), preferred_element_type=F32)


def dot_nt(a, b):
    return lax.dot_general(a, b, (((1,), (1,)), ((), ())), preferred_element_type=F32)


def dot_tn(a, b):
    return lax.dot_general(a, b, (((0,), (0,)), ((), ())), preferred_element_type=F32)


def sums(v):
    return jnp.sum(v, axis=0, keepdims=True)


def column_of(shape, width):
    place = lax.broadcasted_iota(jnp.int32, shape, 0)
    row = (place * (2731 if width == 24 else 5462)) >> 16
    return place - row * width


def move_columns(v, step, width):
    if step == 0:
        return v
    column = column_of(v.shape, width)
    keep = column < width - 1 if step == 1 else column > 0
    return jnp.where(keep, pltpu.roll(v, (-step) % v.shape[0], 0), 0.0)


def move_rows(v, step, width):
    if step == 0:
        return v
    size = v.shape[0]
    place = lax.broadcasted_iota(jnp.int32, v.shape, 0)
    keep = place < size - width if step == 1 else place >= width
    return jnp.where(keep, pltpu.roll(v, (-step * width) % size, 0), 0.0)


def centre(total, count):
    mean = total[0:1] / count
    spread = total[1:2] / count - mean * mean
    return mean, lax.rsqrt(spread + EPSILON)


def place_blocks(ch_ref, blocks, full_ref):
    own = ch_ref[0]
    for k, block in enumerate(blocks):
        start = pl.multiple_of((own ^ k) * 128, 128)
        full_ref[:, pl.ds(start, 128)] = block[...]


def conv(values, taps_ref, lead, width):
    total = None
    for col in range(3):
        kernel = jnp.concatenate([taps_ref[lead, 3 * row + col] for row in range(3)], 1)
        part = dot(values, kernel)
        line = part[:, 128:256]
        line = line + move_rows(part[:, 0:128], -1, width)
        line = line + move_rows(part[:, 256:384], 1, width)
        line = move_columns(line, col - 1, width)
        total = line if total is None else total + line
    return total


def spread_taps(grad, width, taps_out):
    for col in range(3):
        line = move_columns(grad, 1 - col, width)
        for row in range(3):
            tap = 3 * row + col
            taps_out[:, tap * 128 : tap * 128 + 128] = move_rows(line, 1 - row, width).astype(LOW)


def conv_back(taps_value, taps_ref, lead):
    kernel = jnp.concatenate([taps_ref[lead, tap] for tap in range(9)], 1)
    return dot_nt(taps_value, kernel)


def pool(v, scratch, width):
    size = v.shape[0]
    if width % 8 == 0:
        pairs = v.reshape(size // (2 * width), 2 * width, 128)
        rows = (pairs[:, :width] + pairs[:, width:]).reshape(size // 2, 128)
        scratch[0 : size // 2] = rows
        return 0.25 * (
            scratch[pl.ds(0, size // 4, stride=2)] + scratch[pl.ds(1, size // 4, stride=2)]
        )
    v = v + pltpu.roll(v, size - width, 0)
    v = v + pltpu.roll(v, size - 1, 0)
    scratch[...] = v
    half = scratch[pl.ds(0, size // 2, stride=2)]
    scratch[0 : size // 2] = half
    parts = [scratch[a * width : a * width + width // 2] for a in range(size // (2 * width))]
    return 0.25 * jnp.concatenate(parts, 0)


def unpool(v, scratch, width):
    size = 4 * v.shape[0]
    v = 0.25 * v
    scratch[pl.ds(0, size // 4, stride=2)] = v
    scratch[pl.ds(1, size // 4, stride=2)] = v
    rows = scratch[0 : size // 2]
    if width % 8 == 0:
        rows = rows.reshape(size // (2 * width), width, 128)
        return jnp.concatenate([rows, rows], 1).reshape(size, 128)
    parts = []
    for a in range(size // (2 * width)):
        part = rows[a * width : a * width + width]
        parts += [part, part]
    return jnp.concatenate(parts, 0)

def bn_of(total, row, count):
    return centre(total[row : row + 2], count)


def spread_stats(out, rows):
    for place, row in enumerate(rows):
        if len(out.shape) == 2:
            out[place : place + 1] = row
        else:
            out[:, place : place + 1] = jnp.broadcast_to(row[None], (out.shape[0],) + row.shape)


def moments(v):
    return [sums(v), sums(v * v)]


def pack_body(down, up, gain, shift, wide, narrow, params):
    for l in range(down.shape[0]):
        wide[l, 0] = down[l]
        wide[l, 1] = up[l]
        narrow[l, 0:3] = gain[l, 5:8]
        narrow[l, 3:6] = shift[l, 5:8]
        params[l, 0:8] = gain[l, 0:8]
        params[l, 8:16] = shift[l, 0:8]


def unpack_body(ch, w0, w1, w2, w3, n0, n1, n2, n3, down, up, gates):
    own = ch[0]
    for k, (wide, narrow) in enumerate(((w0, n0), (w1, n1), (w2, n2), (w3, n3))):
        start = pl.ds(pl.multiple_of((own ^ k) * 128, 128), 128)
        for l in range(down.shape[0]):
            for t in range(3):
                down[l, t, start, :] = wide[l, 0, t]
                up[l, t, :, start] = wide[l, 1, t]
            gates[l, :, start] = narrow[l]


def first_conv_body(width, lead, ch, x0, x1, x2, x3, taps, full, y, stats):
    place_blocks(ch, (x0, x1, x2, x3), full)
    flush(full)
    out = conv(full[...], taps, lead, width)
    y[...] = out
    spread_stats(stats, moments(out))


def next_conv_body(width, lead, skip, ch, x0, x1, x2, x3, taps, full, y, stats):
    own = ch[0]
    for k, block in enumerate((x0, x1, x2, x3)):
        start = pl.multiple_of((own ^ k) * 128, 128)
        full[:, pl.ds(start, 128)] = block[skip:]
    flush(full)
    out = conv(full[...], taps, lead, width)
    y[...] = out
    for place, row in enumerate(moments(out)):
        stats[place : place + 1] = row


def first_act_body(count, y, raw, gain, shift, low, again):
    mean, inverse = bn_of(raw, 0, count)
    v = (y[...] - mean) * inverse * gain[0, 0:1] + shift[0, 0:1]
    act = (v * sigmoid(v)).astype(LOW)
    low[...] = act
    again[...] = act


def second_conv_body(width, lead, ch, x0, x1, x2, x3, taps, down, full, y, p, stats):
    place_blocks(ch, (x0, x1, x2, x3), full)
    flush(full)
    values = full[...]
    out = conv(values, taps, lead, width)
    y[...] = out
    rows = moments(out)
    for t in range(3):
        part = dot(values, down[0, t])
        p[t] = part
        rows += moments(part)
    spread_stats(stats, rows)


def second_conv_next_body(width, lead, ch, x0, x1, x2, x3, taps, near, far, full, y, p, stats):
    place_blocks(ch, (x0, x1, x2, x3), full)
    flush(full)
    out = conv(full[...], taps, lead, width)
    y[...] = out
    rows = moments(out)
    for t in range(3):
        part = near[t].astype(F32) + far[t].astype(F32)
        p[t] = part
        rows += moments(part)
    spread_stats(stats, rows)


def hidden_body(l, count, width, y, p, raw, gain, shift, bgain, bshift, up, s, u, pooled_u, zstats, scratch):
    mean, inverse = bn_of(raw, 0, count)
    v = (y[...] - mean) * inverse * gain[l, 1:2] + shift[l, 1:2]
    act = v * sigmoid(v)
    size = y.shape[0]
    u[0:size] = act.astype(LOW)
    pooled = pool(act, scratch, width).astype(LOW)
    if pooled_u is None:
        u[size:] = pooled
    else:
        pooled_u[...] = pooled
    rows = []
    for t in range(3):
        mean, inverse = bn_of(raw, 2 + 2 * t, count)
        v = (p[t] - mean) * inverse * bgain[l, t : t + 1] + bshift[l, t : t + 1]
        low = (v * sigmoid(v)).astype(LOW)
        s[t] = low
        rows += moments(dot(low, up[l, t]))
    spread_stats(zstats, rows)


def task_conv_body(l, count, width, ch, s, up, u0, u1, u2, u3, zraw, gates, taps, more, k, y, stats, full, acc):
    size = s.shape[1]
    own = ch[0]
    for i, block in enumerate((u0, u1, u2, u3)):
        start = pl.multiple_of((own ^ i) * 128, 128)
        full[:, pl.ds(start, 128)] = block[0:size]
    ztotal = zraw[...]
    for t in range(3):
        mean, inverse = centre(ztotal[2 * t : 2 * t + 2], count)
        scale = inverse * gates[l, t : t + 1]
        v = dot(s[t], up[l, t]) * scale + (gates[l, 3 + t : 4 + t] - mean * scale)
        k[t] = (sigmoid(v) * full[...].astype(F32)).astype(LOW)
    flush(k)
    ready(taps)

    def one(t, carry):
        out = conv(k[t], taps, t, width)
        y[t] = out
        rows = moments(out)
        acc[t, 0:1] = rows[0]
        acc[t, 1:2] = rows[1]
        return carry

    lax.fori_loop(0, 3, one, 0)
    rows = [acc[t, i : i + 1] for t in range(3) for i in range(2)]
    if more is not None:
        rows += [more[0:1], more[1:2]]
    spread_stats(stats, rows)


def attend_body(count, count_next, width, yt, y, raw, gain, shift, down, low, g, part, scratch):
    mean, inverse = bn_of(raw, 6, count_next)
    v = (y[...] - mean) * inverse * gain[1, 0:1] + shift[1, 0:1]
    act = v * sigmoid(v)
    low[...] = act.astype(LOW)
    for t in range(3):
        mean, inverse = bn_of(raw, 2 * t, count)
        v = (yt[t] - mean) * inverse * gain[0, 2 + t : 3 + t] + shift[0, 2 + t : 3 + t]
        attend = (act + pool(v * sigmoid(v), scratch, width)).astype(LOW)
        g[t] = attend
        part[t] = dot(attend, down[1, t]).astype(LOW)


def pair_body(a, b, out):
    out[...] = (a[...].astype(F32) + b[...].astype(F32)).astype(LOW)


def pair_second_body(keep, far, got, out, part):
    out[...] = (far[...] + got[1].astype(F32)).astype(LOW)
    part[...] = keep[...] + got[0].astype(F32)


def pair_tasks_body(keep, far, got, keep_x, far_x, got_x, out, part, part_x):
    size = far.shape[1]
    for t in range(far.shape[0]):
        out[t * size : (t + 1) * size] = (far[t] + got[1, t].astype(F32)).astype(LOW)
        part[t] = keep[t] + got[0, t].astype(F32)
    out[far.shape[0] * size :] = (far_x[...] + got_x[1].astype(F32)).astype(LOW)
    part_x[...] = keep_x[...] + got_x[0].astype(F32)


def mixed_body(a, b, out):
    out[...] = a[...] + b[...].astype(F32)


def stack_body(a, b, out):
    out[0] = a[...]
    out[1] = b[...]


def add_body(a, b, out):
    out[...] = (a[...].astype(F32) + b[...].astype(F32)).astype(out.dtype)


def sum_body(copies, out):
    total = copies[0]
    for i in range(1, copies.shape[0]):
        total = total + copies[i]
    out[...] = total


def sum_all_body(*refs):
    parts = [ref[...] for ref in refs[:-1]]
    while len(parts) > 1:
        parts = [a + b for a, b in zip(parts[::2], parts[1::2])]
    refs[-1][...] = parts[0]


def mark_body(out):
    out[...] = jnp.zeros_like(out)


def task_last_body(l, count, width, y, raw, gain, shift, dq, out, d, stats, scratch):
    rows = []
    for t in range(3):
        mean, inverse = bn_of(raw, 2 * t, count)
        normal = (y[t] - mean) * inverse
        v = normal * gain[l, 2 + t : 3 + t] + shift[l, 2 + t : 3 + t]
        sg = sigmoid(v)
        out[t] = pool(v * sg, scratch, width).astype(LOW)
        grad = unpool(dq[t], scratch, width) * silu_slope(v, sg)
        d[t] = grad
        rows += [sums(grad), sums(grad * normal)]
    spread_stats(stats, rows)


def norm_back(d, y, bn, dtotal, gain, count):
    mean, inverse = bn
    scale = gain * inverse
    normal = (y - mean) * inverse
    return scale * (d - dtotal[0:1] / count - normal * (dtotal[1:2] / count))


def input_grads(width, ch, dy, taps, lead, outs, cat, dv):
    spread_taps(dy, width, cat)
    dv[...] = conv_back(cat[...], taps, lead)
    own = ch[0]
    blocks = []
    for k in range(4):
        start = pl.multiple_of((own ^ k) * 128, 128)
        blocks.append(dv[:, pl.ds(start, 128)])
    return blocks


def task_back_body(l, count, width, row0, ch, d, y, raw, draw, gain, taps, dys, send, keep, far, cat, dv):
    total = raw[...]
    dtotal = draw[...]
    for t in range(3):
        bn = centre(total[2 * t : 2 * t + 2], count)
        dts = dtotal[row0 + 2 * t : row0 + 2 * t + 2]
        dy = norm_back(d[t], y[t], bn, dts, gain[l, 2 + t : 3 + t], count)
        dys[t] = dy.astype(LOW)
    ready(taps)

    def one(t, carry):
        blocks = input_grads(width, ch, dys[t].astype(F32), taps, t, None, cat, dv)
        send[0, t] = blocks[1].astype(LOW)
        send[1, t] = blocks[3].astype(LOW)
        keep[t] = blocks[0]
        far[t] = blocks[2]
        return carry

    lax.fori_loop(0, 3, one, 0)


def conv_back_body(l, k, count, width, ch, d, y, raw, rawrow, draw, gain, taps, dys, send, keep, far, cat, dv):
    dtotal = draw[0:2]
    dy = norm_back(d[...], y[...], bn_of(raw, rawrow, count), dtotal, gain[l, k : k + 1], count)
    dys[...] = dy.astype(LOW)
    blocks = input_grads(width, ch, dy, taps, 0, None, cat, dv)
    send[0] = blocks[1].astype(LOW)
    send[1] = blocks[3].astype(LOW)
    keep[...] = blocks[0]
    far[...] = blocks[2]


def task_weights_body(width, x, dys, out, cat, total):
    ready(x)
    ready(dys)

    def one(t, carry):
        spread_taps(dys.ref[t].astype(F32), width, cat)
        total[...] = dot_tn(x.ref[t], cat[...])
        for tap in range(9):
            out.ref[t, tap] = total[:, tap * 128 : tap * 128 + 128].astype(LOW)
        return carry

    lax.fori_loop(0, 3, one, 0)


def widen_body(*refs):
    out = refs[-1]
    first = 0
    for ref in refs[:-1]:
        last = first + ref.shape[0]
        out[first:last] = ref[...].astype(F32)
        first = last


def split_body(bit, im, *refs):
    out = refs[-1]
    low = (im[0] >> bit) & 1
    for n, x in enumerate(refs[:-1]):
        ready(x)
        for i in range(2):
            start = pl.multiple_of((2 * i + 1 - low) * 128, 128)
            out[n, i] = x.ref[0, :, pl.ds(start, 128)]


def pair_weight_body(width, bit, rest, picks, im, *refs):
    stay, leave, cat, total = refs[-4:]
    low = (im[0] >> bit) & 1
    half = stay.shape[0]
    share = stay.shape[3]
    for n, (place_x, place_dy) in enumerate(picks):
        x, other_x, dy, other_dy = refs[4 * n : 4 * n + 4]
        ready(x)
        ready(dy)
        mine = [
            x.ref[0, :, pl.ds(pl.multiple_of((2 * i + low) * 128, 128), 128)] for i in range(2)
        ]
        spread_taps(dy[0].astype(F32), width, cat)
        total[...] = dot_tn(jnp.concatenate(mine, 1), cat[...])
        theirs = [other_x[place_x, i] for i in range(2)]
        grad = other_dy[...] if place_dy is None else other_dy[place_dy]
        spread_taps(grad.astype(F32), width, cat)
        total[...] += dot_tn(jnp.concatenate(theirs, 1), cat[...])
        for e in range(2 * half):
            mask = 0
            for s, b in enumerate(rest):
                mask |= ((e >> (len(rest) - 1 - s)) & 1) << b
            block = im[0] ^ mask
            row = ((block >> (bit + 1)) & 1) * 128 + (block & ((1 << bit) - 1)) * share
            rows = pl.ds(pl.multiple_of(row, share), share)
            target = stay if e < half else leave
            for tap in range(9):
                target[e % half, n, tap] = total[rows, tap * 128 : tap * 128 + 128].astype(LOW)


def halve_body(*refs):
    stay, leave = refs[-2:]
    half = stay.shape[0]
    first = 0
    for a, b in zip(refs[:-2:2], refs[1:-2:2]):
        last = first + a.shape[1]
        for i in range(half):
            stay[i, first:last] = a[i].astype(F32) + b[i].astype(F32)
            leave[i, first:last] = (a[half + i].astype(F32) + b[half + i].astype(F32)).astype(LOW)
        first = last


def flat_body(*refs):
    out = refs[-1]
    share = out.shape[1]
    rows = [ref[t] for ref in refs[:-1] for t in range(ref.shape[0])]
    whole = jnp.concatenate(rows, 0)
    for i in range(out.shape[0]):
        out[i] = whole[i * share : (i + 1) * share]


def spread_sum_body(copies, out):
    total = copies[0].astype(F32)
    for i in range(1, copies.shape[0]):
        total = total + copies[i].astype(F32)
    out[...] = jnp.broadcast_to(total.astype(LOW)[None], out.shape)


def gate_grad_body(l, count, width, ch, part, far, s, up, zraw, y, raw, gain, shift, dx, d, d2, stats, scratch):
    size = y.shape[0]
    if len(dx) == 1:
        grad = dx[0][...]
    else:
        grad = dx[0][...] + far[3 * size :].astype(F32)
    mean, inverse = bn_of(raw, 0, count)
    normal = (y[...] - mean) * inverse
    v = normal * gain[l, 1:2] + shift[l, 1:2]
    sg = sigmoid(v)
    act = v * sg
    own = pl.ds(pl.multiple_of(ch[0] * 128, 128), 128)
    ztotal = zraw[:, own]
    upstream = unpool(grad, scratch, width)
    rows = []
    for t in range(3):
        zmean, zinverse = centre(ztotal[2 * t : 2 * t + 2], count)
        znormal = (dot(s[t], up[l, t]) - zmean) * zinverse
        m = sigmoid(znormal * gain[l, 5 + t : 6 + t] + shift[l, 5 + t : 6 + t])
        dr = part[t] + (far[t] if len(dx) == 1 else far[t * size : (t + 1) * size]).astype(F32)
        through = dr * m
        upstream = upstream + through
        grad = through * act * (1.0 - m)
        d[t] = grad
        rows += [sums(grad), sums(grad * znormal)]
    grad = upstream * silu_slope(v, sg)
    d2[...] = grad
    spread_stats(stats, [sums(grad), sums(grad * normal)] + rows)


def hidden_grad_body(l, count, ch, d, s, up, zraw, draw, gain, ds, dup):
    own = pl.ds(pl.multiple_of(ch[0] * 128, 128), 128)
    ztotal = zraw[:, own]
    dtotal = draw[2:8]
    for t in range(3):
        z = dot(s[t], up[l, t])
        rows = slice(2 * t, 2 * t + 2)
        bn = centre(ztotal[rows], count)
        dz = norm_back(d[t], z, bn, dtotal[rows], gain[l, 5 + t : 6 + t], count).astype(LOW)
        dup[t] = dot_tn(s[t], dz).astype(LOW)
        ds[t] = dot_nt(dz, up[l, t]).astype(LOW)


def bottle_grad_body(l, count, ds0, ds1, p, raw, bgain, bshift, d, stats):
    rows = []
    for t in range(3):
        mean, inverse = bn_of(raw, 2 + 2 * t, count)
        normal = (p[t] - mean) * inverse
        v = normal * bgain[l, t : t + 1] + bshift[l, t : t + 1]
        grad = (ds0[t].astype(F32) + ds1[t].astype(F32)) * silu_slope(v, sigmoid(v))
        d[t] = grad
        rows += [sums(grad), sums(grad * normal)]
    spread_stats(stats, rows)


def attend_grad_body(l, count, rawrow, d, p, raw, draw, bgain, g, down, dv, y, raw1, gain, shift, more, ddown, d1, stats, more_out):
    upstream = dv[...]
    dtotal = draw[...]
    rows = []
    for t in range(3):
        bn = bn_of(raw, 2 + 2 * t, count)
        dp = norm_back(d[t], p[t], bn, dtotal[2 * t : 2 * t + 2], bgain[l, t : t + 1], count).astype(LOW)
        ddown[t] = dot_tn(g[...] if more is None else g[t], dp).astype(LOW)
        grad = dot_nt(dp, down[l, t])
        upstream = upstream + grad
        if more is not None:
            yt, traw, tcount, twidth, scratch = more
            mean, inverse = bn_of(traw, 2 * t, tcount)
            normal = (yt[t] - mean) * inverse
            v = normal * gain[l - 1, 2 + t : 3 + t] + shift[l - 1, 2 + t : 3 + t]
            grad = unpool(grad, scratch, twidth) * silu_slope(v, sigmoid(v))
            more_out[t] = grad
            rows += [sums(grad), sums(grad * normal)]
    mean, inverse = bn_of(raw1, rawrow, count)
    normal = (y[...] - mean) * inverse
    v = normal * gain[l, 0:1] + shift[l, 0:1]
    grad = upstream * silu_slope(v, sigmoid(v))
    d1[...] = grad
    spread_stats(stats, [sums(grad), sums(grad * normal)] + rows)


def attend_grad_last_body(l, count, rawrow, d, p, raw, draw, bgain, g, down, dv, y, raw1, gain, shift, ddown, d1, stats):
    attend_grad_body(l, count, rawrow, d, p, raw, draw, bgain, g, down, dv, y, raw1, gain, shift, None, ddown, d1, stats, None)


def attend_grad_first_body(l, count, rawrow, tcount, twidth, d, p, raw, draw, bgain, g, down, dv, y, raw1, gain, shift, yt, traw, ddown, d1, stats, dt, scratch):
    more = (yt, traw, tcount, twidth, scratch)
    attend_grad_body(l, count, rawrow, d, p, raw, draw, bgain, g, down, dv, y, raw1, gain, shift, more, ddown, d1, stats, dt)


def finish_body(order, refs_in, gain, shift, bgain, bshift):
    for l in range(gain.shape[0]):
        for row, (place, start) in enumerate(order[l]):
            total = refs_in[place][start : start + 2]
            if row < 8:
                shift[l, row : row + 1] = total[0:1]
                gain[l, row : row + 1] = total[1:2]
            else:
                bshift[l, row - 8 : row - 7] = total[0:1]
                bgain[l, row - 8 : row - 7] = total[1:2]


def shape_of(shape, dtype=F32):
    return jax.ShapeDtypeStruct(tuple(shape), dtype)


class Long:
    def __init__(self, near, home=None):
        self.near, self.home = near, home
        some = home if near is None else near
        self.shape, self.dtype = some.shape, some.dtype


class Taps:
    def __init__(self, home, first, count):
        self.home, self.first, self.shape = home, first, (count,) + home.shape[1:]
        self.dtype, self.near = home.dtype, None


class Rows:
    def __init__(self, whole, first, last):
        self.whole, self.first, self.last = whole, first, last


class Coming:
    def __init__(self, ref, copy):
        self.ref, self.copy, self.shape, self.dtype = ref, copy, ref.shape, ref.dtype

    def ready(self):
        if self.copy is not None:
            self.copy.wait()
            self.copy = None

    def __getitem__(self, place):
        self.ready()
        return self.ref[place]


class Going:
    def __init__(self, ref, copy):
        self.ref, self.copy, self.shape, self.dtype = ref, copy, ref.shape, ref.dtype
        self.started = False

    def flush(self):
        if not self.started:
            self.copy.start()
            self.started = True

    def __getitem__(self, place):
        return self.ref[place]

    def __setitem__(self, place, value):
        self.ref[place] = value


class SomeRows:
    def __init__(self, ref, first):
        self.ref, self.first = ref, first

    def __getitem__(self, place):
        layer, rows = place
        return self.ref[layer, self.first + rows.start : self.first + rows.stop]


def ready(ref):
    if isinstance(ref, Coming):
        ref.ready()


def flush(ref):
    if isinstance(ref, Going):
        ref.flush()


TURN = []


def run(body, args, outs, scratch=(), name=None, keep=(), away=(), save=(), after=()):
    values, picks = [], []
    for v in list(args) + list(save):
        whole = v.whole if isinstance(v, Rows) else v
        place = next((i for i, other in enumerate(values) if other is whole), None)
        if place is None:
            place = len(values)
            values.append(whole)
        picks.append((place, v))
    picks = picks[: len(args)]
    count = len(values)
    far = [isinstance(v, (Taps, Long)) and v.near is None for v in values]
    saved = [i for i, v in enumerate(values) if isinstance(v, Long) and v.home is None]
    hbm, vmem = pl.BlockSpec(memory_space=pltpu.HBM), pl.BlockSpec(memory_space=pltpu.VMEM)
    operands, specs = [], []
    for v, apart in zip(values, far):
        if apart:
            operands.append(pltpu.with_memory_space_constraint(v.home, pltpu.HBM))
            specs.append(hbm)
        else:
            operands.append(v.near if isinstance(v, (Taps, Long)) else v)
            specs.append(spec_of(operands[-1]))
    after = list(after) + TURN
    TURN.clear()
    outs = list(outs) + [shape_of((8, 128))]
    stage = [pltpu.VMEM(v.shape, v.dtype) for v, apart in zip(values, far) if apart]
    leave = [pltpu.VMEM(outs[i].shape, outs[i].dtype) for i in away]
    moves = len(stage) + len(leave) + len(saved)

    def kernel(*refs):
        ins = list(refs[:count])
        results = list(refs[count + len(after) : count + len(after) + len(outs)])
        homes = refs[count + len(after) + len(outs) :][: len(saved)]
        rest = refs[count + len(after) + len(outs) + len(saved) :]
        own, rest = rest[: len(scratch)], rest[len(scratch) :]
        sems = rest[-1] if moves else None
        wait = []
        slot = 0
        for i in range(count):
            if not far[i]:
                continue
            source = ins[i]
            if isinstance(values[i], Taps):
                source = source.at[values[i].first : values[i].first + values[i].shape[0]]
            copy = pltpu.make_async_copy(source, rest[slot], sems.at[slot])
            copy.start()
            ins[i] = Coming(rest[slot], copy)
            wait.append(ins[i])
            slot += 1
        end = []
        for i, home in zip(saved, homes):
            copy = pltpu.make_async_copy(ins[i], home, sems.at[slot])
            copy.start()
            end.append(copy)
            slot += 1
        for n, i in enumerate(away):
            ref = rest[len(stage) + n]
            copy = pltpu.make_async_copy(ref, results[i], sems.at[slot])
            results[i] = Going(ref, copy)
            end.append(results[i])
            slot += 1
        turn = results.pop()
        turn[...] = jnp.zeros_like(turn)
        views = [SomeRows(ins[i], v.first) if isinstance(v, Rows) else ins[i] for i, v in picks]
        body(*views, *results, *own)
        for item in wait:
            item.ready()
        for item in end:
            if isinstance(item, Going):
                item.flush()
        for item in end:
            (item.copy if isinstance(item, Going) else item).wait()

    out_shape = []
    for i, v in enumerate(outs):
        kind = pltpu.HBM if i in away else pltpu.VMEM
        out_shape.append(kind(v.shape, v.dtype))
    out_shape += [pltpu.HBM(values[i].shape, values[i].dtype) for i in saved]
    results = pl.pallas_call(
        kernel,
        out_shape=out_shape,
        in_specs=specs + [vmem] * len(after),
        out_specs=[hbm if i in away else vmem for i in range(len(outs))] + [hbm] * len(saved),
        scratch_shapes=list(scratch)
        + stage
        + leave
        + ([pltpu.SemaphoreType.DMA((moves,))] if moves else []),
        compiler_params=pltpu.CompilerParams(vmem_limit_bytes=VMEM_LIMIT),
        cost_estimate=pl.CostEstimate(flops=0, bytes_accessed=1, transcendentals=0),
        name=name,
    )(*operands, *after)
    answer = list(results[: len(outs)])
    TURN.append(answer.pop())
    for i, home in zip(saved, results[len(outs) :]):
        values[i].home = home
    for v in values:
        if isinstance(v, (Taps, Long)):
            v.near = None
    for i in keep:
        answer[i] = Long(answer[i])
    for i in away:
        answer[i] = Long(None, answer[i])
    return answer


def bring(items, name):
    items = [v for v in items if v.near is None]
    if not items:
        return
    count = len(items)

    def body(*refs):
        turn, sems = refs[2 * count + 1], refs[-1]
        copies = []
        for i, item in enumerate(items):
            source = refs[i]
            if isinstance(item, Taps):
                source = source.at[item.first : item.first + item.shape[0]]
            copies.append(pltpu.make_async_copy(source, refs[count + 1 + i], sems.at[i]))
            copies[-1].start()
        turn[...] = jnp.zeros_like(turn)
        for copy in copies:
            copy.wait()

    hbm, vmem = pl.BlockSpec(memory_space=pltpu.HBM), pl.BlockSpec(memory_space=pltpu.VMEM)
    results = pl.pallas_call(
        body,
        out_shape=[pltpu.VMEM(v.shape, v.dtype) for v in items] + [pltpu.VMEM((8, 128), F32)],
        in_specs=[hbm] * count + [vmem],
        out_specs=[vmem] * (count + 1),
        scratch_shapes=[pltpu.SemaphoreType.DMA((count,))],
        compiler_params=pltpu.CompilerParams(vmem_limit_bytes=VMEM_LIMIT),
        cost_estimate=pl.CostEstimate(flops=0, bytes_accessed=1, transcendentals=0),
        name=name,
    )(*[pltpu.with_memory_space_constraint(v.home, pltpu.HBM) for v in items], TURN.pop())
    TURN.append(results[count])
    for v, near in zip(items, results):
        v.near = near


def spec_of(value):
    return pl.BlockSpec(memory_space=pltpu.SMEM if value.dtype == jnp.int32 else pltpu.VMEM)


CORE = ((0, 1), (1, 0), (2, 3), (3, 2))
CHIP = ((0, 2), (2, 0), (1, 3), (3, 1))


def near_and_far(value):
    far = lax.ppermute(value, "ch", CHIP)
    return [value, lax.ppermute(value, "ch", CORE), far]


def add_last(blocks, after=None):
    far = blocks[2] if after is None else hold(blocks[2], after)
    blocks.append(lax.ppermute(far, "ch", CORE))


def gather_ch(value):
    blocks = near_and_far(value)
    add_last(blocks)
    return blocks


def hold(value, after):
    return lax.optimization_barrier((value, after))[0]


def swap_img(copies):
    return lax.all_to_all(copies, "img", 0, 0)


class Layer:
    pass


def on_device(
    feats,
    shared_w,
    task_w,
    down_w,
    up_w,
    norm_gain,
    norm_shift,
    bottle_gain,
    bottle_shift,
    seg_mask,
    depth_mask,
    shared_cot,
    task_cot,
):
    images = lax.axis_size("img")
    tasks = task_w.shape[1]
    layers = shared_w.shape[0]
    share = 512 // images
    own = lax.axis_index("ch").astype(jnp.int32).reshape(1)
    img = lax.axis_index("img").astype(jnp.int32).reshape(1)
    shared_taps = shared_w.reshape(2 * layers, 9, 512, 128)
    task_taps = task_w.reshape(tasks * layers, 9, 512, 128)
    widths = [feats.shape[2], feats.shape[2] // 2]
    sizes = [w * w for w in widths]
    counts = [float(images * n) for n in sizes]
    n0, n1 = sizes

    def stats_of(rows, lanes=128):
        return shape_of((images, rows, lanes))

    one, two = Layer(), Layer()
    kept = [one, two]

    TURN.clear()
    pending, held = [], []

    def total_of(copies, name, steps=(), mid=(), ahead=()):
        if pending:
            copies = hold(copies, list(pending))
            pending.clear()
        got = swap_img(copies)
        if mid and not steps:
            run(mark_body, (), [shape_of((8, 128))], name="mark")
        for place, step in enumerate(steps):
            step()
            if place == 0:
                for blocks in mid:
                    add_last(blocks, TURN[0])
        if mid and not steps:
            for blocks in mid:
                add_last(blocks, TURN[0])
        bring(ahead, f"bring{name}")
        total = run(sum_body, (got,), [shape_of(copies.shape[1:])], name=name, keep=(0,))[0]
        for make in held:
            make(total.near)
        held.clear()
        return total

    def total_by_pairs(rows, name, first, second, mid, ahead=()):
        if pending:
            rows = hold(rows, list(pending))
            pending.clear()
        low = min(1, bits - 1)
        groups = [range(low, bits), range(low)] if bits <= 3 else [[b] for b in range(bits)]
        for place, group in enumerate(groups):
            shifts = [0]
            for bit in group:
                shifts += [s | 1 << bit for s in shifts]
            parts = [rows] + [
                lax.ppermute(rows, "img", [(i, i ^ s) for i in range(images)]) for s in shifts[1:]
            ]
            last = place == len(groups) - 1
            for step in (first if place == 0 else []) + (second if last else []):
                step()
            if place == 0:
                bring(ahead, f"bring{name}")
            rows = run(
                sum_all_body,
                parts,
                [shape_of(rows.shape)],
                name=f"{name}_{place}",
                keep=(0,) if last else (),
            )[0]
            for blocks in mid if place == 0 else ():
                add_last(blocks, rows.near if last else rows)
        for make in held:
            make(rows.near)
        held.clear()
        return rows

    def gap(steps):
        waiting = list(held)
        held.clear()
        for step in steps:
            step()
        for make in held:
            make(None)
        held[:] = waiting

    def send_img(value, bit, tie=True):
        got = lax.ppermute(value, "img", [(i, i ^ (1 << bit)) for i in range(images)])
        if tie:
            pending.append(got)
        return got

    bits = images.bit_length() - 1
    pair_bit = 7 - (share.bit_length() - 1)
    rest = [b for b in range(bits) if b != pair_bit]

    def later(owner, field, value, bit, tie=True):
        def make(total):
            setattr(owner, field, send_img(value if total is None else hold(value, total), bit, tie))

        held.append(make)

    class Meeting:
        pass

    class Conv:
        def __init__(self, name):
            self.name, self.l = name, int(name[-1])

        def take(self, x, place):
            self.x = Taps(x.home.reshape((-1,) + x.shape[-2:]), place, 1)

    class Split:
        def __init__(self, names):
            self.names = names
            for place, name in enumerate(names):
                convs[name].split, convs[name].place_x = self, place

        def go(self):
            members = [convs[name] for name in self.names]
            out = run(
                functools.partial(split_body, pair_bit),
                (img, *[c.x for c in members]),
                [shape_of((len(members), 2, sizes[members[0].l], 128), LOW)],
                name="split" + "".join(self.names),
            )[0]
            later(self, "got", out, pair_bit)

    class Weights:
        def __init__(self, names):
            self.members, self.name, self.step = [convs[n] for n in names], "".join(names), 0
            self.parts, self.placed = [self], False

        def weigh(self):
            l = self.members[0].l
            args, picks = [], []
            for c in self.members:
                args += [c.x, c.split.got, c.dy, c.meeting.got]
                picks.append((c.place_x, c.place_dy))
            shape = shape_of((images // 4, len(picks), 9, share, 128), LOW)
            self.stay, leave = run(
                functools.partial(pair_weight_body, widths[l], pair_bit, rest, picks),
                (img, *args),
                [shape] * 2,
                scratch=[pltpu.VMEM((sizes[l], 1152), LOW), pltpu.VMEM((256, 1152), F32)],
                name=f"weigh{self.name}",
                away=(0,),
            )
            self.step = 1
            later(self, "got", leave, rest[0])

        def halve(self):
            args = []
            for part in self.parts:
                args += [part.stay, part.got]
            self.step = self.parts[0].step
            self.parts = [self]
            shape = (args[0].shape[0] // 2, len(self.members)) + args[0].shape[2:]
            self.stay, leave = run(
                halve_body,
                args,
                [shape_of(shape), shape_of(shape, LOW)],
                name=f"halve{self.name}_{self.step}",
                away=(0,),
            )
            later(self, "got", leave, rest[self.step], self.step + 1 < len(rest))
            self.step += 1

        def put(self):
            self.placed = True
            places = [PLACES[c.name] for c in self.members]
            first = list(buffers)
            count = len(places)

            def body(*refs):
                stay, got, _, turn, out, value, other, sems = refs[len(first) :]
                load = pltpu.make_async_copy(stay.at[0], other, sems.at[count])
                load.start()
                turn[...] = jnp.zeros_like(turn)
                load.wait()
                copies = []
                for n, place in enumerate(places):
                    value[n] = other[n].astype(F32) + got[0, n].astype(F32)
                    copies.append(pltpu.make_async_copy(value.at[n], out.at[place], sems.at[n]))
                    copies[-1].start()
                for copy in copies:
                    copy.wait()

            stay = self.stay.home
            turn, *buffers[:] = pl.pallas_call(
                body,
                out_shape=[
                    pltpu.VMEM((8, 128), F32),
                    pltpu.HBM((2 * layers, 9, share, 128), F32),
                ],
                in_specs=[hbm] * len(first) + [hbm, vmem, vmem],
                out_specs=[vmem, hbm],
                input_output_aliases={i: i + 1 for i in range(len(first))},
                scratch_shapes=[
                    pltpu.VMEM((count, 9, share, 128), F32),
                    pltpu.VMEM((count, 9, share, 128), stay.dtype),
                    pltpu.SemaphoreType.DMA((count + 1,)),
                ],
                compiler_params=pltpu.CompilerParams(vmem_limit_bytes=VMEM_LIMIT),
                cost_estimate=pl.CostEstimate(flops=0, bytes_accessed=1, transcendentals=0),
                name=f"put{self.name}",
            )(
                *[pltpu.with_memory_space_constraint(v, pltpu.HBM) for v in first],
                pltpu.with_memory_space_constraint(stay, pltpu.HBM),
                self.got,
                TURN.pop(),
            )
            TURN.append(turn)

    hbm, vmem = pl.BlockSpec(memory_space=pltpu.HBM), pl.BlockSpec(memory_space=pltpu.VMEM)
    buffers = []
    PLACES = {"a_0": 0, "b_0": 1, "a_1": 2, "b_1": 3}
    convs = {name: Conv(name) for name in PLACES}

    jobs = {names: Weights(names.split()) for names in ["b_1", "a_1", "b_0", "a_0"]}
    splits = {names: Split(names.split()) for names in ["b_0", "a_0", "b_1 a_1"]}

    def task_weights(l):
        k = kept[l]
        out = run(
            functools.partial(task_weights_body, widths[l]),
            (k.k, k.dys),
            [shape_of((tasks, 9, 512, 128), LOW)],
            scratch=[pltpu.VMEM((sizes[l], 1152), LOW), pltpu.VMEM((512, 1152), F32)],
            name=f"weight_{l}",
            away=(0,),
        )[0]

        def make(total):
            value = out.home if total is None else hold(out.home, total)
            k.task_w = lax.psum_scatter(value, "img", scatter_dimension=2, tiled=True)

        return make

    def meet(names, dys, wait=False):
        for t, name in enumerate(names):
            c = convs[name]
            c.dy = Taps(dys.home.reshape((-1,) + dys.shape[-2:]), t, 1)
            c.meeting, c.place_dy = Meeting(), t if len(names) > 1 else None
        meeting = convs[names[0]].meeting
        for name in names:
            convs[name].meeting = meeting
        if wait:
            later(meeting, "got", dys.home, pair_bit)
        else:
            meeting.got = send_img(dys.home, pair_bit)

    blocks = near_and_far(feats.reshape(n0, 128))
    down_w, up_w = Long(None, down_w), Long(None, up_w)
    wide, narrow, params = run(
        pack_body,
        (down_w, up_w, Long(None, norm_gain), Long(None, norm_shift)),
        [
            shape_of((layers, 2, tasks, 128, 128), LOW),
            shape_of((layers, 6, 128)),
            shape_of((layers, 16, 128)),
        ],
        name="pack",
        away=(2,),
    )
    gains = Rows(params, 0, 8)
    norms = (gains, Rows(params, 8, 16))
    add_last(blocks, TURN[0])
    blocks[0] = Long(None, blocks[0])
    bottles = (Long(None, bottle_gain), Long(None, bottle_shift))
    one.x, one.y1, stats = run(
        functools.partial(first_conv_body, widths[0], 0),
        (own, *blocks, Taps(shared_taps, 0, 1)),
        [shape_of((n0, 512), LOW), shape_of((n0, 128)), stats_of(2)],
        name="conv1_0",
        keep=(1,),
        away=(0,),
    )
    wides, narrows = near_and_far(hold(wide, stats)), near_and_far(hold(narrow, stats))
    scales = jnp.stack([seg_mask, depth_mask, jnp.ones_like(seg_mask)]).astype(F32)
    dq = (task_cot.astype(F32) * scales[..., None]).reshape(tasks, n1 // 4, 128)
    dq, dx = Long(dq), Long(shared_cot.astype(F32).reshape(n1 // 4, 128))
    convs["a_0"].take(one.x, 0)
    one.raw1 = total_of(
        stats, "total1_0", [splits["a_0"].go], (wides, narrows), [params]
    )
    one.row1 = 0
    low, one.g = run(
        functools.partial(first_act_body, counts[0]),
        (one.y1, one.raw1, *norms),
        [shape_of((n0, 128), LOW)] * 2,
        name="act1_0",
        away=(1,),
    )
    blocks = gather_ch(low)
    down_all, up_all, gates = run(
        unpack_body,
        (own, *wides, *narrows),
        [
            shape_of((layers, tasks, 512, 128), LOW),
            shape_of((layers, tasks, 128, 512), LOW),
            shape_of((layers, 6, 512)),
        ],
        name="unpack",
        keep=(0,),
        away=(1, 2),
        save=(dq, dx),
    )
    one.x2, one.y2, one.p, stats = run(
        functools.partial(second_conv_body, widths[0], 0),
        (own, *blocks, Taps(shared_taps, 1, 1), down_all),
        [shape_of((n0, 512), LOW), shape_of((n0, 128)), shape_of((tasks, n0, 128)), stats_of(8)],
        name="conv2_0",
        keep=(1, 2),
        away=(0,),
    )
    one.raw2 = total_of(stats, "total2_0", ahead=[params, up_all, *bottles])

    def hidden(l):
        k, n = kept[l], sizes[l]
        body = functools.partial(hidden_body, l, counts[l], widths[l])
        outs = [shape_of((tasks, n, 128), LOW)]
        if l == 0:

            def inner(y, p, raw, gain, shift, bgain, bshift, up, s, u, zstats, scratch):
                body(y, p, raw, gain, shift, bgain, bshift, up, s, u, None, zstats, scratch)

            outs += [shape_of((n + n // 4, 128), LOW), shape_of((6, 512))]
        else:
            inner = body
            outs += [shape_of((n, 128), LOW), shape_of((n // 4, 128), LOW), stats_of(6, 512)]
        return run(
            inner,
            (k.y2, k.p, k.raw2, *norms, *bottles, up_all),
            outs,
            scratch=[pltpu.VMEM((n, 128), F32)],
            name=f"hidden_{l}",
            keep=(0,),
        )

    def task_convs(l, u_blocks, taps, more=None):
        k, n = kept[l], sizes[l]
        body = functools.partial(task_conv_body, l, counts[l], widths[l])
        args = (own, k.s, up_all, *u_blocks, k.zraw, gates, taps)
        if more is None:

            def inner(ch, s, up, u0, u1, u2, u3, zraw, gt, taps, kk, y, stats, full, acc):
                body(ch, s, up, u0, u1, u2, u3, zraw, gt, taps, None, kk, y, stats, full, acc)

        else:
            inner = body
            args += (more,)
        return run(
            inner,
            args,
            [
                shape_of((tasks, n, 512), LOW),
                shape_of((tasks, n, 128)),
                stats_of(6 if more is None else 8),
            ],
            scratch=[pltpu.VMEM((n, 512), LOW), pltpu.VMEM((tasks, 2, 128), F32)],
            name=f"taskconv_{l}",
            keep=(1,),
            away=(0,),
        )

    one.s, u, zstats = hidden(0)
    u_blocks = near_and_far(u)

    def next_conv():
        two.x, two.y1, two.more = run(
            functools.partial(next_conv_body, widths[1], 0, n0),
            (own, *u_blocks, Taps(shared_taps, 2, 1)),
            [shape_of((n1, 512), LOW), shape_of((n1, 128)), shape_of((2, 128))],
            name="conv1_1",
            away=(0, 1),
        )

    convs["b_0"].take(one.x2, 0)
    taps = Taps(task_taps, 0, tasks)
    one.zraw = total_by_pairs(
        zstats, "totalz_0", [], [next_conv], (u_blocks,), [up_all, gates, taps]
    )
    one.k, one.yt, stats = task_convs(0, u_blocks, taps, two.more)
    one.traw = total_of(
        stats, "totalt_0", [splits["b_0"].go], ahead=[params, down_w, two.y1]
    )
    two.raw1, two.row1 = one.traw, 6

    low, two.g, part = run(
        functools.partial(attend_body, counts[0], counts[1], widths[0]),
        (one.yt, two.y1, one.traw, *norms, down_w),
        [
            shape_of((n1, 128), LOW),
            shape_of((tasks, n1, 128), LOW),
            shape_of((tasks, n1, 128), LOW),
        ],
        scratch=[pltpu.VMEM((n0, 128), F32)],
        name="attend_1",
        away=(1,),
    )

    def sum_ch(value, name):
        got = lax.ppermute(value, "ch", CORE)
        near = run(pair_body, (value, got), [shape_of(value.shape, LOW)], name=name)[0]
        return near, lax.ppermute(near, "ch", CHIP)

    blocks = gather_ch(low)
    halves = sum_ch(part, "pairp_1")
    two.x2, two.y2, two.p, stats = run(
        functools.partial(second_conv_next_body, widths[1], 0),
        (own, *blocks, Taps(shared_taps, 3, 1), *halves),
        [shape_of((n1, 512), LOW), shape_of((n1, 128)), shape_of((tasks, n1, 128)), stats_of(8)],
        name="conv2_1",
        keep=(1, 2),
        away=(0,),
    )
    two.raw2 = total_of(stats, "total2_1", ahead=[params, up_all, *bottles])
    convs["a_1"].take(two.x, 0)
    convs["b_1"].take(two.x2, 0)
    two.s, u, shared_out, zstats = hidden(1)
    u_blocks = near_and_far(u)
    taps = Taps(task_taps, tasks, tasks)
    two.zraw = total_of(zstats, "totalz_1", mid=(u_blocks,))
    two.k, two.yt, stats = task_convs(1, u_blocks, taps)
    two.traw = total_of(stats, "totalt_1")

    task_out, d, stats = run(
        functools.partial(task_last_body, 1, counts[1], widths[1]),
        (two.yt, two.traw, *norms, dq),
        [shape_of((tasks, n1 // 4, 128), LOW), shape_of((tasks, n1, 128)), stats_of(6)],
        scratch=[pltpu.VMEM((n1, 128), F32)],
        name="tasklast_1",
    )
    taps = Taps(task_taps, tasks, tasks)
    two.dtraw = total_of(
        stats,
        "dtotalt_1",
        [splits["b_1 a_1"].go],
    )
    two.dtrow = 0

    def back_outs(n, lead=()):
        return [
            shape_of(lead + (n, 128), LOW),
            shape_of((2,) + lead + (n, 128), LOW),
            shape_of(lead + (n, 128)),
            shape_of(lead + (n, 128)),
        ]

    def back_scratch(n):
        return [pltpu.VMEM((n, 1152), LOW), pltpu.VMEM((n, 512), F32)]

    def scatter_ch(send, keep, far, name, away=()):
        near, part = run(
            pair_second_body,
            (keep, far, lax.ppermute(send, "ch", CORE)),
            [shape_of(far.shape, LOW), shape_of(far.shape)],
            name=name,
            away=away,
        )
        return (part, lax.ppermute(near, "ch", CHIP))

    def steps(weigh="", halve="", split="", put=""):
        kinds = ((jobs, weigh, "weigh"), (jobs, halve, "halve"))
        kinds += ((splits, split, "go"), (jobs, put, "put"))
        return [
            getattr(table[name], kind)
            for table, names, kind in kinds
            for name in names.split(", ")
            if name
        ]

    def put_ready(names):
        for name in names:
            if jobs[name].step == len(rest) and not jobs[name].placed:
                jobs[name].put()

    flat = []

    def flatten():
        rows = run(
            flat_body,
            [part for k in kept for part in k.both],
            [shape_of((images, layers * 2 * tasks * 128 // images, 128), LOW)],
            name="flat",
        )[0]
        flat.append(swap_img(rows))

    plan = {
        "gate_1": (),
        "bottle_1": (),
        "first_1": steps("b_1"),
        "gate_0": steps("a_1", "b_1"),
        "bottle_0": steps("", "a_1"),
        "first_0": steps("b_0") + [lambda: put_ready(["b_1"]), flatten],
    }
    unfinished = None

    for l in range(layers - 1, -1, -1):
        k, n, w, count = kept[l], sizes[l], widths[l], counts[l]
        dys, send, keep, far = run(
            functools.partial(task_back_body, l, count, w, k.dtrow),
            (own, d, k.yt, k.traw, k.dtraw, gains, taps),
            back_outs(n, (tasks,)),
            scratch=back_scratch(n),
            name=f"taskback_{l}",
            away=(0,),
        )
        k.dys = dys
        if unfinished is None:
            parts = scatter_ch(send, keep, far, f"pairr_{l}")
            rest_dx = dx
        else:
            send_x, keep_x, far_x = unfinished
            near, part, rest_dx = run(
                pair_tasks_body,
                (
                    keep,
                    far,
                    lax.ppermute(send, "ch", CORE),
                    keep_x,
                    far_x,
                    lax.ppermute(send_x, "ch", CORE),
                ),
                [
                    shape_of((tasks * n + sizes[l + 1], 128), LOW),
                    shape_of((tasks, n, 128)),
                    shape_of((sizes[l + 1], 128)),
                ],
                name=f"pairr_{l}",
            )
            parts = (part, lax.ppermute(near, "ch", CHIP))
        make_weights = task_weights(l)

        def gate_grad(ch, part, far, s, up, zraw, y, raw, gain, shift, dx, *rest, first=unfinished, l=l, w=w):
            more = (dx,) if first is None else (dx, far)
            gate_grad_body(l, counts[l], w, ch, part, far, s, up, zraw, y, raw, gain, shift, more, *rest)

        d, d2, stats = run(
            gate_grad,
            (own, *parts, k.s, up_w, k.zraw, k.y2, k.raw2, *norms, rest_dx),
            [shape_of((tasks, n, 128)), shape_of((n, 128)), stats_of(8)],
            scratch=[pltpu.VMEM((n, 128), F32)],
            name=f"gategrad_{l}",
        )
        if l == 0:
            held.append(make_weights)
        else:
            make_weights(stats)
        k.draw2 = total_of(
            stats, f"dtotal2_{l}", plan[f"gate_{l}"], ahead=[k.s, up_w, k.zraw, params]
        )
        d2 = Long(d2)
        ds, dup = run(
            functools.partial(hidden_grad_body, l, count),
            (own, d, k.s, up_w, k.zraw, k.draw2, gains),
            [shape_of((tasks, n, 128), LOW), shape_of((tasks, 128, 128), LOW)],
            name=f"hiddengrad_{l}",
            away=(1,),
            save=(d2,),
        )
        k.dup = dup
        got = lax.ppermute(ds, "ch", CORE)
        near = run(pair_body, (ds, got), [shape_of(ds.shape, LOW)], name=f"pairs_{l}")[0]
        halves = near, lax.ppermute(near, "ch", CHIP)

        def conv2_back(ch, d, y, raw, draw, gain, taps, *rest, l=l, count=count, w=w):
            conv_back_body(l, 1, count, w, ch, d, y, raw, 0, draw, gain, taps, *rest)

        dys, send, keep, far = run(
            conv2_back,
            (own, d2, k.y2, k.raw2, k.draw2, gains, Taps(shared_taps, 2 * l + 1, 1)),
            back_outs(n),
            scratch=back_scratch(n),
            name=f"conv2back_{l}",
            away=(0,),
        )
        meet([f"b_{l}"], dys)
        parts = scatter_ch(send, keep, far, f"pairv_{l}", (1,))

        def make_dv(k=k, parts=parts, n=n, l=l):
            k.dv = run(mixed_body, parts, [shape_of((n, 128))], name=f"dv_{l}")[0]

        gap(plan.get(f"hidden_{l}", ()))
        d, stats = run(
            functools.partial(bottle_grad_body, l, count),
            (*halves, k.p, k.raw2, *bottles),
            [shape_of((tasks, n, 128)), stats_of(6)],
            name=f"bottlegrad_{l}",
        )
        wanted = [k.p, k.raw2, bottles[0], k.g, down_w, k.y1, k.raw1, params]
        if l > 0:
            wanted += [kept[l - 1].yt, kept[l - 1].traw]
        k.draw3 = total_of(stats, f"dtotal3_{l}", [make_dv, *plan[f"bottle_{l}"]])
        args = (d, k.p, k.raw2, k.draw3, bottles[0], k.g, down_w, k.dv, k.y1, k.raw1, *norms)
        outs = [shape_of((tasks, 128, 128), LOW), shape_of((n, 128))]
        if l > 0:
            ddown, d1, stats, d = run(
                functools.partial(
                    attend_grad_first_body, l, count, k.row1, counts[l - 1], widths[l - 1]
                ),
                args + (kept[l - 1].yt, kept[l - 1].traw),
                outs + [stats_of(8), shape_of((tasks, sizes[l - 1], 128))],
                scratch=[pltpu.VMEM((sizes[l - 1], 128), F32)],
                name=f"attendgrad_{l}",
                away=(0,),
            )
        else:
            ddown, d1, stats = run(
                functools.partial(attend_grad_last_body, l, count, k.row1),
                args,
                outs + [stats_of(2)],
                name=f"attendgrad_{l}",
                away=(0,),
            )
        k.both = [ddown, k.dup]
        last_taps = Taps(shared_taps, 2 * l, 1)
        wanted = [k.y1, k.raw1, params, last_taps]
        if l > 0:
            taps = Taps(task_taps, tasks * (l - 1), tasks)
            wanted.append(taps)
        k.draw1 = total_of(stats, f"dtotal1_{l}", plan[f"first_{l}"], ahead=wanted if l == 0 else ())
        if l > 0:
            kept[l - 1].dtraw, kept[l - 1].dtrow = k.draw1, 2
            d1 = Long(d1)

        def conv1_back(ch, d, y, raw, draw, gain, taps, *rest, l=l, count=count, w=w, row=k.row1):
            conv_back_body(l, 0, count, w, ch, d, y, raw, row, draw, gain, taps, *rest)

        dys, send, keep, far = run(
            conv1_back,
            (own, d1, k.y1, k.raw1, k.draw1, gains, last_taps),
            back_outs(n),
            scratch=back_scratch(n),
            name=f"conv1back_{l}",
            away=(0,),
        )
        meet([f"a_{l}"], dys)

        unfinished = (send, keep, far)

    parts = scatter_ch(*unfinished, "pairx_0")
    every = ["b_1", "a_1", "b_0", "a_0"]

    put_ready(every[:2])
    gap(steps("a_0"))
    gap(steps("", "b_0"))
    flat = run(spread_sum_body, flat, [shape_of(flat[0].shape, LOW)], name="spread")[0]
    flat = swap_img(flat)
    dx = run(mixed_body, parts, [shape_of((n0, 128))], name="dx_0", away=(0,))[0].home
    gap(steps("", "a_0"))
    tw = run(
        widen_body,
        [Long(None, k.task_w) for k in kept],
        [shape_of((tasks * layers, 9, share, 128))],
        name="tasksout",
        away=(0,),
    )[0].home

    order, places = [], []
    for k in kept:
        base = len(places)
        places += [k.draw1, k.draw2, k.dtraw, k.draw3]
        rows = [(base, 0), (base + 1, 0)]
        rows += [(base + 2, k.dtrow + 2 * t) for t in range(3)]
        rows += [(base + 1, 2 + 2 * t) for t in range(3)]
        rows += [(base + 3, 2 * t) for t in range(3)]
        order.append(rows)

    def norms_body(*refs):
        finish_body(order, refs[: len(places)], *refs[len(places) :])

    gains = run(
        norms_body,
        places,
        [shape_of((layers, 8, 128))] * 2 + [shape_of((layers, tasks, 128))] * 2,
        name="norms",
    )
    while any(jobs[name].step < len(rest) for name in every):
        for name in every:
            if jobs[name].step < len(rest):
                gap([jobs[name].halve])
    flat = hold(flat, TURN[0])
    put_ready(every)
    flat = flat.reshape(layers, 2, tasks, 128, 128).astype(F32)
    down, up = flat[:, 0], flat[:, 1]
    (sw,) = buffers
    return (
        shared_out.reshape(1, widths[1] // 2, widths[1] // 2, 128),
        task_out.reshape(tasks, 1, widths[1] // 2, widths[1] // 2, 128),
        dx.reshape(1, widths[0], widths[0], 128),
        sw.reshape(layers, 2, 3, 3, share, 128),
        tw.reshape(layers, tasks, 3, 3, share, 128),
        down,
        up,
        *gains,
    )


def solution(mesh):
    placed = (
        P("img", None, None, "ch"),
        P(None, None, None, None, None, "ch"),
        P(None, None, None, None, None, "ch"),
        P(None, None, "ch", None),
        P(None, None, None, "ch"),
        P(None, None, "ch"),
        P(None, None, "ch"),
        P(),
        P(),
        P("img", None, None),
        P("img", None, None),
        P("img", None, None, "ch"),
        P(None, "img", None, None, "ch"),
    )
    return jax.shard_map(
        on_device,
        mesh=mesh,
        in_specs=placed,
        out_specs=(
            P("img", None, None, "ch"),
            P(None, "img", None, None, "ch"),
            P("img", None, None, "ch"),
            P(None, None, None, None, "img", "ch"),
            P(None, None, None, None, "img", "ch"),
            P(None, None, "ch", None),
            P(None, None, None, "ch"),
            P(None, None, "ch"),
            P(None, None, "ch"),
            P(),
            P(),
        ),
        check_vma=False,
    )
```

```python
import functools

import jax
import jax.numpy as jnp
from jax import lax
from jax.experimental import pallas as pl
from jax.experimental.pallas import tpu as pltpu
from jax.sharding import PartitionSpec as P

EPSILON = 1e-05
F32 = jnp.float32
LOW = jnp.bfloat16
VMEM_LIMIT = 16 * 2**20


def sigmoid(v):
    return 0.5 * jnp.tanh(0.5 * v) + 0.5


def silu_slope(v, s):
    return s * (1.0 + v * (1.0 - s))


def dot(a, b):
    return lax.dot_general(a, b, (((1,), (0,)), ((), ())), preferred_element_type=F32)


def dot_nt(a, b):
    return lax.dot_general(a, b, (((1,), (1,)), ((), ())), preferred_element_type=F32)


def dot_tn(a, b):
    return lax.dot_general(a, b, (((0,), (0,)), ((), ())), preferred_element_type=F32)


def sums(v):
    return jnp.sum(v, axis=0, keepdims=True)


def column_of(shape, width):
    place = lax.broadcasted_iota(jnp.int32, shape, 0)
    row = (place * (2731 if width == 24 else 5462)) >> 16
    return place - row * width


def move_columns(v, step, width):
    if step == 0:
        return v
    column = column_of(v.shape, width)
    keep = column < width - 1 if step == 1 else column > 0
    return jnp.where(keep, pltpu.roll(v, (-step) % v.shape[0], 0), 0.0)


def move_rows(v, step, width):
    if step == 0:
        return v
    size = v.shape[0]
    place = lax.broadcasted_iota(jnp.int32, v.shape, 0)
    keep = place < size - width if step == 1 else place >= width
    return jnp.where(keep, pltpu.roll(v, (-step * width) % size, 0), 0.0)


def centre(total, count):
    mean = total[0:1] / count
    spread = total[1:2] / count - mean * mean
    return mean, lax.rsqrt(spread + EPSILON)


def place_blocks(ch_ref, blocks, full_ref):
    own = ch_ref[0]
    for k, block in enumerate(blocks):
        start = pl.multiple_of((own ^ k) * 128, 128)
        full_ref[:, pl.ds(start, 128)] = block[...]


def conv(values, taps_ref, lead, width):
    total = None
    for col in range(3):
        kernel = jnp.concatenate([taps_ref[lead, 3 * row + col] for row in range(3)], 1)
        part = dot(values, kernel)
        line = part[:, 128:256]
        line = line + move_rows(part[:, 0:128], -1, width)
        line = line + move_rows(part[:, 256:384], 1, width)
        line = move_columns(line, col - 1, width)
        total = line if total is None else total + line
    return total


def spread_taps(grad, width, taps_out):
    for col in range(3):
        line = move_columns(grad, 1 - col, width)
        for row in range(3):
            tap = 3 * row + col
            taps_out[:, tap * 128 : tap * 128 + 128] = move_rows(line, 1 - row, width).astype(LOW)


def conv_back(taps_value, taps_ref, lead):
    kernel = jnp.concatenate([taps_ref[lead, tap] for tap in range(9)], 1)
    return dot_nt(taps_value, kernel)


def pool(v, scratch, width):
    size = v.shape[0]
    if width % 8 == 0:
        pairs = v.reshape(size // (2 * width), 2 * width, 128)
        rows = (pairs[:, :width] + pairs[:, width:]).reshape(size // 2, 128)
        scratch[0 : size // 2] = rows
        return 0.25 * (
            scratch[pl.ds(0, size // 4, stride=2)] + scratch[pl.ds(1, size // 4, stride=2)]
        )
    v = v + pltpu.roll(v, size - width, 0)
    v = v + pltpu.roll(v, size - 1, 0)
    scratch[...] = v
    half = scratch[pl.ds(0, size // 2, stride=2)]
    scratch[0 : size // 2] = half
    parts = [scratch[a * width : a * width + width // 2] for a in range(size // (2 * width))]
    return 0.25 * jnp.concatenate(parts, 0)


def unpool(v, scratch, width):
    size = 4 * v.shape[0]
    v = 0.25 * v
    scratch[pl.ds(0, size // 4, stride=2)] = v
    scratch[pl.ds(1, size // 4, stride=2)] = v
    rows = scratch[0 : size // 2]
    if width % 8 == 0:
        rows = rows.reshape(size // (2 * width), width, 128)
        return jnp.concatenate([rows, rows], 1).reshape(size, 128)
    parts = []
    for a in range(size // (2 * width)):
        part = rows[a * width : a * width + width]
        parts += [part, part]
    return jnp.concatenate(parts, 0)

def bn_of(total, row, count):
    return centre(total[row : row + 2], count)


def spread_stats(out, rows):
    for place, row in enumerate(rows):
        if len(out.shape) == 2:
            out[place : place + 1] = row
        else:
            out[:, place : place + 1] = jnp.broadcast_to(row[None], (out.shape[0],) + row.shape)


def moments(v):
    return [sums(v), sums(v * v)]


def pack_body(down, up, gain, shift, wide, narrow, params):
    for l in range(down.shape[0]):
        wide[l, 0] = down[l]
        wide[l, 1] = up[l]
        narrow[l, 0:3] = gain[l, 5:8]
        narrow[l, 3:6] = shift[l, 5:8]
        params[l, 0:8] = gain[l, 0:8]
        params[l, 8:16] = shift[l, 0:8]


def unpack_body(ch, w0, w1, w2, w3, n0, n1, n2, n3, down, up, gates):
    own = ch[0]
    for k, (wide, narrow) in enumerate(((w0, n0), (w1, n1), (w2, n2), (w3, n3))):
        start = pl.ds(pl.multiple_of((own ^ k) * 128, 128), 128)
        for l in range(down.shape[0]):
            for t in range(3):
                down[l, t, start, :] = wide[l, 0, t]
                up[l, t, :, start] = wide[l, 1, t]
            gates[l, :, start] = narrow[l]


def first_conv_body(width, lead, ch, x0, x1, x2, x3, taps, full, y, stats):
    place_blocks(ch, (x0, x1, x2, x3), full)
    flush(full)
    out = conv(full[...], taps, lead, width)
    y[...] = out
    spread_stats(stats, moments(out))


def next_conv_body(width, lead, skip, ch, x0, x1, x2, x3, taps, full, y, stats):
    own = ch[0]
    for k, block in enumerate((x0, x1, x2, x3)):
        start = pl.multiple_of((own ^ k) * 128, 128)
        full[:, pl.ds(start, 128)] = block[skip:]
    flush(full)
    out = conv(full[...], taps, lead, width)
    y[...] = out
    for place, row in enumerate(moments(out)):
        stats[place : place + 1] = row


def first_act_body(count, y, raw, gain, shift, low, again):
    mean, inverse = bn_of(raw, 0, count)
    v = (y[...] - mean) * inverse * gain[0, 0:1] + shift[0, 0:1]
    act = (v * sigmoid(v)).astype(LOW)
    low[...] = act
    again[...] = act


def second_conv_body(width, lead, ch, x0, x1, x2, x3, taps, down, full, y, p, stats):
    place_blocks(ch, (x0, x1, x2, x3), full)
    flush(full)
    values = full[...]
    out = conv(values, taps, lead, width)
    y[...] = out
    rows = moments(out)
    for t in range(3):
        part = dot(values, down[0, t])
        p[t] = part
        rows += moments(part)
    spread_stats(stats, rows)


def second_conv_next_body(width, lead, ch, x0, x1, x2, x3, taps, near, far, full, y, p, stats):
    place_blocks(ch, (x0, x1, x2, x3), full)
    flush(full)
    out = conv(full[...], taps, lead, width)
    y[...] = out
    rows = moments(out)
    for t in range(3):
        part = near[t].astype(F32) + far[t].astype(F32)
        p[t] = part
        rows += moments(part)
    spread_stats(stats, rows)


def hidden_body(l, count, width, y, p, raw, gain, shift, bgain, bshift, up, s, u, pooled_u, zstats, scratch):
    mean, inverse = bn_of(raw, 0, count)
    v = (y[...] - mean) * inverse * gain[l, 1:2] + shift[l, 1:2]
    act = v * sigmoid(v)
    size = y.shape[0]
    u[0:size] = act.astype(LOW)
    pooled = pool(act, scratch, width).astype(LOW)
    if pooled_u is None:
        u[size:] = pooled
    else:
        pooled_u[...] = pooled
    rows = []
    for t in range(3):
        mean, inverse = bn_of(raw, 2 + 2 * t, count)
        v = (p[t] - mean) * inverse * bgain[l, t : t + 1] + bshift[l, t : t + 1]
        low = (v * sigmoid(v)).astype(LOW)
        s[t] = low
        rows += moments(dot(low, up[l, t]))
    spread_stats(zstats, rows)


def task_conv_body(l, count, width, ch, s, up, u0, u1, u2, u3, zraw, gates, taps, more, k, y, stats, full, acc):
    size = s.shape[1]
    own = ch[0]
    for i, block in enumerate((u0, u1, u2, u3)):
        start = pl.multiple_of((own ^ i) * 128, 128)
        full[:, pl.ds(start, 128)] = block[0:size]
    ztotal = zraw[...]
    for t in range(3):
        mean, inverse = centre(ztotal[2 * t : 2 * t + 2], count)
        scale = inverse * gates[l, t : t + 1]
        v = dot(s[t], up[l, t]) * scale + (gates[l, 3 + t : 4 + t] - mean * scale)
        k[t] = (sigmoid(v) * full[...].astype(F32)).astype(LOW)
    flush(k)
    ready(taps)

    def one(t, carry):
        out = conv(k[t], taps, t, width)
        y[t] = out
        rows = moments(out)
        acc[t, 0:1] = rows[0]
        acc[t, 1:2] = rows[1]
        return carry

    lax.fori_loop(0, 3, one, 0)
    rows = [acc[t, i : i + 1] for t in range(3) for i in range(2)]
    if more is not None:
        rows += [more[0:1], more[1:2]]
    spread_stats(stats, rows)


def attend_body(count, count_next, width, yt, y, raw, gain, shift, down, low, g, part, scratch):
    mean, inverse = bn_of(raw, 6, count_next)
    v = (y[...] - mean) * inverse * gain[1, 0:1] + shift[1, 0:1]
    act = v * sigmoid(v)
    low[...] = act.astype(LOW)
    for t in range(3):
        mean, inverse = bn_of(raw, 2 * t, count)
        v = (yt[t] - mean) * inverse * gain[0, 2 + t : 3 + t] + shift[0, 2 + t : 3 + t]
        attend = (act + pool(v * sigmoid(v), scratch, width)).astype(LOW)
        g[t] = attend
        part[t] = dot(attend, down[1, t]).astype(LOW)


def pair_body(a, b, out):
    out[...] = (a[...].astype(F32) + b[...].astype(F32)).astype(LOW)


def pair_second_body(keep, far, got, out, part):
    out[...] = (far[...] + got[1].astype(F32)).astype(LOW)
    part[...] = keep[...] + got[0].astype(F32)


def pair_tasks_body(keep, far, got, keep_x, far_x, got_x, out, part, part_x):
    size = far.shape[1]
    for t in range(far.shape[0]):
        out[t * size : (t + 1) * size] = (far[t] + got[1, t].astype(F32)).astype(LOW)
        part[t] = keep[t] + got[0, t].astype(F32)
    out[far.shape[0] * size :] = (far_x[...] + got_x[1].astype(F32)).astype(LOW)
    part_x[...] = keep_x[...] + got_x[0].astype(F32)


def mixed_body(a, b, out):
    out[...] = a[...] + b[...].astype(F32)


def stack_body(a, b, out):
    out[0] = a[...]
    out[1] = b[...]


def add_body(a, b, out):
    out[...] = (a[...].astype(F32) + b[...].astype(F32)).astype(out.dtype)


def sum_body(copies, out):
    total = copies[0]
    for i in range(1, copies.shape[0]):
        total = total + copies[i]
    out[...] = total


def sum_all_body(*refs):
    parts = [ref[...] for ref in refs[:-1]]
    while len(parts) > 1:
        parts = [a + b for a, b in zip(parts[::2], parts[1::2])]
    refs[-1][...] = parts[0]


def mark_body(out):
    out[...] = jnp.zeros_like(out)


def task_last_body(l, count, width, y, raw, gain, shift, dq, out, d, stats, scratch):
    rows = []
    for t in range(3):
        mean, inverse = bn_of(raw, 2 * t, count)
        normal = (y[t] - mean) * inverse
        v = normal * gain[l, 2 + t : 3 + t] + shift[l, 2 + t : 3 + t]
        sg = sigmoid(v)
        out[t] = pool(v * sg, scratch, width).astype(LOW)
        grad = unpool(dq[t], scratch, width) * silu_slope(v, sg)
        d[t] = grad
        rows += [sums(grad), sums(grad * normal)]
    spread_stats(stats, rows)


def norm_back(d, y, bn, dtotal, gain, count):
    mean, inverse = bn
    scale = gain * inverse
    normal = (y - mean) * inverse
    return scale * (d - dtotal[0:1] / count - normal * (dtotal[1:2] / count))


def input_grads(width, ch, dy, taps, lead, outs, cat, dv):
    spread_taps(dy, width, cat)
    dv[...] = conv_back(cat[...], taps, lead)
    own = ch[0]
    blocks = []
    for k in range(4):
        start = pl.multiple_of((own ^ k) * 128, 128)
        blocks.append(dv[:, pl.ds(start, 128)])
    return blocks


def task_back_body(l, count, width, row0, ch, d, y, raw, draw, gain, taps, dys, send, keep, far, cat, dv):
    total = raw[...]
    dtotal = draw[...]
    for t in range(3):
        bn = centre(total[2 * t : 2 * t + 2], count)
        dts = dtotal[row0 + 2 * t : row0 + 2 * t + 2]
        dy = norm_back(d[t], y[t], bn, dts, gain[l, 2 + t : 3 + t], count)
        dys[t] = dy.astype(LOW)
    ready(taps)

    def one(t, carry):
        blocks = input_grads(width, ch, dys[t].astype(F32), taps, t, None, cat, dv)
        send[0, t] = blocks[1].astype(LOW)
        send[1, t] = blocks[3].astype(LOW)
        keep[t] = blocks[0]
        far[t] = blocks[2]
        return carry

    lax.fori_loop(0, 3, one, 0)


def conv_back_body(l, k, count, width, ch, d, y, raw, rawrow, draw, gain, taps, dys, send, keep, far, cat, dv):
    dtotal = draw[0:2]
    dy = norm_back(d[...], y[...], bn_of(raw, rawrow, count), dtotal, gain[l, k : k + 1], count)
    dys[...] = dy.astype(LOW)
    blocks = input_grads(width, ch, dy, taps, 0, None, cat, dv)
    send[0] = blocks[1].astype(LOW)
    send[1] = blocks[3].astype(LOW)
    keep[...] = blocks[0]
    far[...] = blocks[2]


def task_weights_body(width, x, dys, out, cat, total):
    ready(x)
    ready(dys)

    def one(t, carry):
        spread_taps(dys.ref[t].astype(F32), width, cat)
        total[...] = dot_tn(x.ref[t], cat[...])
        for tap in range(9):
            out.ref[t, tap] = total[:, tap * 128 : tap * 128 + 128].astype(LOW)
        return carry

    lax.fori_loop(0, 3, one, 0)


def widen_body(*refs):
    out = refs[-1]
    first = 0
    for ref in refs[:-1]:
        last = first + ref.shape[0]
        out[first:last] = ref[...].astype(F32)
        first = last


def split_body(bit, im, *refs):
    out = refs[-1]
    low = (im[0] >> bit) & 1
    for n, x in enumerate(refs[:-1]):
        ready(x)
        for i in range(2):
            start = pl.multiple_of((2 * i + 1 - low) * 128, 128)
            out[n, i] = x.ref[0, :, pl.ds(start, 128)]


def pair_weight_body(width, bit, rest, picks, im, *refs):
    stay, leave, cat, total = refs[-4:]
    low = (im[0] >> bit) & 1
    half = stay.shape[0]
    share = stay.shape[3]
    for n, (place_x, place_dy) in enumerate(picks):
        x, other_x, dy, other_dy = refs[4 * n : 4 * n + 4]
        ready(x)
        ready(dy)
        mine = [
            x.ref[0, :, pl.ds(pl.multiple_of((2 * i + low) * 128, 128), 128)] for i in range(2)
        ]
        spread_taps(dy[0].astype(F32), width, cat)
        total[...] = dot_tn(jnp.concatenate(mine, 1), cat[...])
        theirs = [other_x[place_x, i] for i in range(2)]
        grad = other_dy[...] if place_dy is None else other_dy[place_dy]
        spread_taps(grad.astype(F32), width, cat)
        total[...] += dot_tn(jnp.concatenate(theirs, 1), cat[...])
        for e in range(2 * half):
            mask = 0
            for s, b in enumerate(rest):
                mask |= ((e >> (len(rest) - 1 - s)) & 1) << b
            block = im[0] ^ mask
            row = ((block >> (bit + 1)) & 1) * 128 + (block & ((1 << bit) - 1)) * share
            rows = pl.ds(pl.multiple_of(row, share), share)
            target = stay if e < half else leave
            for tap in range(9):
                target[e % half, n, tap] = total[rows, tap * 128 : tap * 128 + 128].astype(LOW)


def halve_body(*refs):
    stay, leave = refs[-2:]
    half = stay.shape[0]
    first = 0
    for a, b in zip(refs[:-2:2], refs[1:-2:2]):
        last = first + a.shape[1]
        for i in range(half):
            stay[i, first:last] = a[i].astype(F32) + b[i].astype(F32)
            leave[i, first:last] = (a[half + i].astype(F32) + b[half + i].astype(F32)).astype(LOW)
        first = last


def flat_body(*refs):
    out = refs[-1]
    share = out.shape[1]
    rows = [ref[t] for ref in refs[:-1] for t in range(ref.shape[0])]
    whole = jnp.concatenate(rows, 0)
    for i in range(out.shape[0]):
        out[i] = whole[i * share : (i + 1) * share]


def spread_sum_body(copies, out):
    total = copies[0].astype(F32)
    for i in range(1, copies.shape[0]):
        total = total + copies[i].astype(F32)
    out[...] = jnp.broadcast_to(total.astype(LOW)[None], out.shape)


def gate_grad_body(l, count, width, ch, part, far, s, up, zraw, y, raw, gain, shift, dx, d, d2, stats, scratch):
    size = y.shape[0]
    if len(dx) == 1:
        grad = dx[0][...]
    else:
        grad = dx[0][...] + far[3 * size :].astype(F32)
    mean, inverse = bn_of(raw, 0, count)
    normal = (y[...] - mean) * inverse
    v = normal * gain[l, 1:2] + shift[l, 1:2]
    sg = sigmoid(v)
    act = v * sg
    own = pl.ds(pl.multiple_of(ch[0] * 128, 128), 128)
    ztotal = zraw[:, own]
    upstream = unpool(grad, scratch, width)
    rows = []
    for t in range(3):
        zmean, zinverse = centre(ztotal[2 * t : 2 * t + 2], count)
        znormal = (dot(s[t], up[l, t]) - zmean) * zinverse
        m = sigmoid(znormal * gain[l, 5 + t : 6 + t] + shift[l, 5 + t : 6 + t])
        dr = part[t] + (far[t] if len(dx) == 1 else far[t * size : (t + 1) * size]).astype(F32)
        through = dr * m
        upstream = upstream + through
        grad = through * act * (1.0 - m)
        d[t] = grad
        rows += [sums(grad), sums(grad * znormal)]
    grad = upstream * silu_slope(v, sg)
    d2[...] = grad
    spread_stats(stats, [sums(grad), sums(grad * normal)] + rows)


def hidden_grad_body(l, count, ch, d, s, up, zraw, draw, gain, ds, dup):
    own = pl.ds(pl.multiple_of(ch[0] * 128, 128), 128)
    ztotal = zraw[:, own]
    dtotal = draw[2:8]
    for t in range(3):
        z = dot(s[t], up[l, t])
        rows = slice(2 * t, 2 * t + 2)
        bn = centre(ztotal[rows], count)
        dz = norm_back(d[t], z, bn, dtotal[rows], gain[l, 5 + t : 6 + t], count).astype(LOW)
        dup[t] = dot_tn(s[t], dz).astype(LOW)
        ds[t] = dot_nt(dz, up[l, t]).astype(LOW)


def bottle_grad_body(l, count, ds0, ds1, p, raw, bgain, bshift, d, stats):
    rows = []
    for t in range(3):
        mean, inverse = bn_of(raw, 2 + 2 * t, count)
        normal = (p[t] - mean) * inverse
        v = normal * bgain[l, t : t + 1] + bshift[l, t : t + 1]
        grad = (ds0[t].astype(F32) + ds1[t].astype(F32)) * silu_slope(v, sigmoid(v))
        d[t] = grad
        rows += [sums(grad), sums(grad * normal)]
    spread_stats(stats, rows)


def attend_grad_body(l, count, rawrow, d, p, raw, draw, bgain, g, down, dv, y, raw1, gain, shift, more, ddown, d1, stats, more_out):
    upstream = dv[...]
    dtotal = draw[...]
    rows = []
    for t in range(3):
        bn = bn_of(raw, 2 + 2 * t, count)
        dp = norm_back(d[t], p[t], bn, dtotal[2 * t : 2 * t + 2], bgain[l, t : t + 1], count).astype(LOW)
        ddown[t] = dot_tn(g[...] if more is None else g[t], dp).astype(LOW)
        grad = dot_nt(dp, down[l, t])
        upstream = upstream + grad
        if more is not None:
            yt, traw, tcount, twidth, scratch = more
            mean, inverse = bn_of(traw, 2 * t, tcount)
            normal = (yt[t] - mean) * inverse
            v = normal * gain[l - 1, 2 + t : 3 + t] + shift[l - 1, 2 + t : 3 + t]
            grad = unpool(grad, scratch, twidth) * silu_slope(v, sigmoid(v))
            more_out[t] = grad
            rows += [sums(grad), sums(grad * normal)]
    mean, inverse = bn_of(raw1, rawrow, count)
    normal = (y[...] - mean) * inverse
    v = normal * gain[l, 0:1] + shift[l, 0:1]
    grad = upstream * silu_slope(v, sigmoid(v))
    d1[...] = grad
    spread_stats(stats, [sums(grad), sums(grad * normal)] + rows)


def attend_grad_last_body(l, count, rawrow, d, p, raw, draw, bgain, g, down, dv, y, raw1, gain, shift, ddown, d1, stats):
    attend_grad_body(l, count, rawrow, d, p, raw, draw, bgain, g, down, dv, y, raw1, gain, shift, None, ddown, d1, stats, None)


def attend_grad_first_body(l, count, rawrow, tcount, twidth, d, p, raw, draw, bgain, g, down, dv, y, raw1, gain, shift, yt, traw, ddown, d1, stats, dt, scratch):
    more = (yt, traw, tcount, twidth, scratch)
    attend_grad_body(l, count, rawrow, d, p, raw, draw, bgain, g, down, dv, y, raw1, gain, shift, more, ddown, d1, stats, dt)


def finish_body(order, refs_in, gain, shift, bgain, bshift):
    for l in range(gain.shape[0]):
        for row, (place, start) in enumerate(order[l]):
            total = refs_in[place][start : start + 2]
            if row < 8:
                shift[l, row : row + 1] = total[0:1]
                gain[l, row : row + 1] = total[1:2]
            else:
                bshift[l, row - 8 : row - 7] = total[0:1]
                bgain[l, row - 8 : row - 7] = total[1:2]


def shape_of(shape, dtype=F32):
    return jax.ShapeDtypeStruct(tuple(shape), dtype)


class Long:
    def __init__(self, near, home=None):
        self.near, self.home = near, home
        some = home if near is None else near
        self.shape, self.dtype = some.shape, some.dtype


class Taps:
    def __init__(self, home, first, count):
        self.home, self.first, self.shape = home, first, (count,) + home.shape[1:]
        self.dtype, self.near = home.dtype, None


class Rows:
    def __init__(self, whole, first, last):
        self.whole, self.first, self.last = whole, first, last


class Coming:
    def __init__(self, ref, copy):
        self.ref, self.copy, self.shape, self.dtype = ref, copy, ref.shape, ref.dtype

    def ready(self):
        if self.copy is not None:
            self.copy.wait()
            self.copy = None

    def __getitem__(self, place):
        self.ready()
        return self.ref[place]


class Going:
    def __init__(self, ref, copy):
        self.ref, self.copy, self.shape, self.dtype = ref, copy, ref.shape, ref.dtype
        self.started = False

    def flush(self):
        if not self.started:
            self.copy.start()
            self.started = True

    def __getitem__(self, place):
        return self.ref[place]

    def __setitem__(self, place, value):
        self.ref[place] = value


class SomeRows:
    def __init__(self, ref, first):
        self.ref, self.first = ref, first

    def __getitem__(self, place):
        layer, rows = place
        return self.ref[layer, self.first + rows.start : self.first + rows.stop]


def ready(ref):
    if isinstance(ref, Coming):
        ref.ready()


def flush(ref):
    if isinstance(ref, Going):
        ref.flush()


TURN = []


def run(body, args, outs, scratch=(), name=None, keep=(), away=(), save=(), after=()):
    values, picks = [], []
    for v in list(args) + list(save):
        whole = v.whole if isinstance(v, Rows) else v
        place = next((i for i, other in enumerate(values) if other is whole), None)
        if place is None:
            place = len(values)
            values.append(whole)
        picks.append((place, v))
    picks = picks[: len(args)]
    count = len(values)
    far = [isinstance(v, (Taps, Long)) and v.near is None for v in values]
    saved = [i for i, v in enumerate(values) if isinstance(v, Long) and v.home is None]
    hbm, vmem = pl.BlockSpec(memory_space=pltpu.HBM), pl.BlockSpec(memory_space=pltpu.VMEM)
    operands, specs = [], []
    for v, apart in zip(values, far):
        if apart:
            operands.append(pltpu.with_memory_space_constraint(v.home, pltpu.HBM))
            specs.append(hbm)
        else:
            operands.append(v.near if isinstance(v, (Taps, Long)) else v)
            specs.append(spec_of(operands[-1]))
    after = list(after) + TURN
    TURN.clear()
    outs = list(outs) + [shape_of((8, 128))]
    stage = [pltpu.VMEM(v.shape, v.dtype) for v, apart in zip(values, far) if apart]
    leave = [pltpu.VMEM(outs[i].shape, outs[i].dtype) for i in away]
    moves = len(stage) + len(leave) + len(saved)

    def kernel(*refs):
        ins = list(refs[:count])
        results = list(refs[count + len(after) : count + len(after) + len(outs)])
        homes = refs[count + len(after) + len(outs) :][: len(saved)]
        rest = refs[count + len(after) + len(outs) + len(saved) :]
        own, rest = rest[: len(scratch)], rest[len(scratch) :]
        sems = rest[-1] if moves else None
        wait = []
        slot = 0
        for i in range(count):
            if not far[i]:
                continue
            source = ins[i]
            if isinstance(values[i], Taps):
                source = source.at[values[i].first : values[i].first + values[i].shape[0]]
            copy = pltpu.make_async_copy(source, rest[slot], sems.at[slot])
            copy.start()
            ins[i] = Coming(rest[slot], copy)
            wait.append(ins[i])
            slot += 1
        end = []
        for i, home in zip(saved, homes):
            copy = pltpu.make_async_copy(ins[i], home, sems.at[slot])
            copy.start()
            end.append(copy)
            slot += 1
        for n, i in enumerate(away):
            ref = rest[len(stage) + n]
            copy = pltpu.make_async_copy(ref, results[i], sems.at[slot])
            results[i] = Going(ref, copy)
            end.append(results[i])
            slot += 1
        turn = results.pop()
        turn[...] = jnp.zeros_like(turn)
        views = [SomeRows(ins[i], v.first) if isinstance(v, Rows) else ins[i] for i, v in picks]
        body(*views, *results, *own)
        for item in wait:
            item.ready()
        for item in end:
            if isinstance(item, Going):
                item.flush()
        for item in end:
            (item.copy if isinstance(item, Going) else item).wait()

    out_shape = []
    for i, v in enumerate(outs):
        kind = pltpu.HBM if i in away else pltpu.VMEM
        out_shape.append(kind(v.shape, v.dtype))
    out_shape += [pltpu.HBM(values[i].shape, values[i].dtype) for i in saved]
    results = pl.pallas_call(
        kernel,
        out_shape=out_shape,
        in_specs=specs + [vmem] * len(after),
        out_specs=[hbm if i in away else vmem for i in range(len(outs))] + [hbm] * len(saved),
        scratch_shapes=list(scratch)
        + stage
        + leave
        + ([pltpu.SemaphoreType.DMA((moves,))] if moves else []),
        compiler_params=pltpu.CompilerParams(vmem_limit_bytes=VMEM_LIMIT),
        cost_estimate=pl.CostEstimate(flops=0, bytes_accessed=1, transcendentals=0),
        name=name,
    )(*operands, *after)
    answer = list(results[: len(outs)])
    TURN.append(answer.pop())
    for i, home in zip(saved, results[len(outs) :]):
        values[i].home = home
    for v in values:
        if isinstance(v, (Taps, Long)):
            v.near = None
    for i in keep:
        answer[i] = Long(answer[i])
    for i in away:
        answer[i] = Long(None, answer[i])
    return answer


def bring(items, name):
    items = [v for v in items if v.near is None]
    if not items:
        return
    count = len(items)

    def body(*refs):
        turn, sems = refs[2 * count + 1], refs[-1]
        copies = []
        for i, item in enumerate(items):
            source = refs[i]
            if isinstance(item, Taps):
                source = source.at[item.first : item.first + item.shape[0]]
            copies.append(pltpu.make_async_copy(source, refs[count + 1 + i], sems.at[i]))
            copies[-1].start()
        turn[...] = jnp.zeros_like(turn)
        for copy in copies:
            copy.wait()

    hbm, vmem = pl.BlockSpec(memory_space=pltpu.HBM), pl.BlockSpec(memory_space=pltpu.VMEM)
    results = pl.pallas_call(
        body,
        out_shape=[pltpu.VMEM(v.shape, v.dtype) for v in items] + [pltpu.VMEM((8, 128), F32)],
        in_specs=[hbm] * count + [vmem],
        out_specs=[vmem] * (count + 1),
        scratch_shapes=[pltpu.SemaphoreType.DMA((count,))],
        compiler_params=pltpu.CompilerParams(vmem_limit_bytes=VMEM_LIMIT),
        cost_estimate=pl.CostEstimate(flops=0, bytes_accessed=1, transcendentals=0),
        name=name,
    )(*[pltpu.with_memory_space_constraint(v.home, pltpu.HBM) for v in items], TURN.pop())
    TURN.append(results[count])
    for v, near in zip(items, results):
        v.near = near


def spec_of(value):
    return pl.BlockSpec(memory_space=pltpu.SMEM if value.dtype == jnp.int32 else pltpu.VMEM)


CORE = ((0, 1), (1, 0), (2, 3), (3, 2))
CHIP = ((0, 2), (2, 0), (1, 3), (3, 1))


def near_and_far(value):
    far = lax.ppermute(value, "ch", CHIP)
    return [value, lax.ppermute(value, "ch", CORE), far]


def add_last(blocks, after=None):
    far = blocks[2] if after is None else hold(blocks[2], after)
    blocks.append(lax.ppermute(far, "ch", CORE))


def gather_ch(value):
    blocks = near_and_far(value)
    add_last(blocks)
    return blocks


def hold(value, after):
    return lax.optimization_barrier((value, after))[0]


def swap_img(copies):
    return lax.all_to_all(copies, "img", 0, 0)


class Layer:
    pass


def on_device(
    feats,
    shared_w,
    task_w,
    down_w,
    up_w,
    norm_gain,
    norm_shift,
    bottle_gain,
    bottle_shift,
    seg_mask,
    depth_mask,
    shared_cot,
    task_cot,
):
    images = lax.axis_size("img")
    tasks = task_w.shape[1]
    layers = shared_w.shape[0]
    share = 512 // images
    own = lax.axis_index("ch").astype(jnp.int32).reshape(1)
    img = lax.axis_index("img").astype(jnp.int32).reshape(1)
    shared_taps = shared_w.reshape(2 * layers, 9, 512, 128)
    task_taps = task_w.reshape(tasks * layers, 9, 512, 128)
    widths = [feats.shape[2], feats.shape[2] // 2]
    sizes = [w * w for w in widths]
    counts = [float(images * n) for n in sizes]
    n0, n1 = sizes

    def stats_of(rows, lanes=128):
        return shape_of((images, rows, lanes))

    one, two = Layer(), Layer()
    kept = [one, two]

    TURN.clear()
    pending, held = [], []

    def total_of(copies, name, steps=(), mid=(), ahead=()):
        if pending:
            copies = hold(copies, list(pending))
            pending.clear()
        got = swap_img(copies)
        if mid and not steps:
            run(mark_body, (), [shape_of((8, 128))], name="mark")
        for place, step in enumerate(steps):
            step()
            if place == 0:
                for blocks in mid:
                    add_last(blocks, TURN[0])
        if mid and not steps:
            for blocks in mid:
                add_last(blocks, TURN[0])
        bring(ahead, f"bring{name}")
        total = run(sum_body, (got,), [shape_of(copies.shape[1:])], name=name, keep=(0,))[0]
        for make in held:
            make(total.near)
        held.clear()
        return total

    def total_by_pairs(rows, name, first, second, mid, ahead=()):
        if pending:
            rows = hold(rows, list(pending))
            pending.clear()
        low = min(1, bits - 1)
        groups = [range(low, bits), range(low)] if bits <= 3 else [[b] for b in range(bits)]
        for place, group in enumerate(groups):
            shifts = [0]
            for bit in group:
                shifts += [s | 1 << bit for s in shifts]
            parts = [rows] + [
                lax.ppermute(rows, "img", [(i, i ^ s) for i in range(images)]) for s in shifts[1:]
            ]
            last = place == len(groups) - 1
            for step in (first if place == 0 else []) + (second if last else []):
                step()
            if place == 0:
                bring(ahead, f"bring{name}")
            rows = run(
                sum_all_body,
                parts,
                [shape_of(rows.shape)],
                name=f"{name}_{place}",
                keep=(0,) if last else (),
            )[0]
            for blocks in mid if place == 0 else ():
                add_last(blocks, rows.near if last else rows)
        for make in held:
            make(rows.near)
        held.clear()
        return rows

    def gap(steps):
        waiting = list(held)
        held.clear()
        for step in steps:
            step()
        for make in held:
            make(None)
        held[:] = waiting

    def send_img(value, bit, tie=True):
        got = lax.ppermute(value, "img", [(i, i ^ (1 << bit)) for i in range(images)])
        if tie:
            pending.append(got)
        return got

    bits = images.bit_length() - 1
    pair_bit = 7 - (share.bit_length() - 1)
    rest = [b for b in range(bits) if b != pair_bit]

    def later(owner, field, value, bit, tie=True):
        def make(total):
            setattr(owner, field, send_img(value if total is None else hold(value, total), bit, tie))

        held.append(make)

    class Meeting:
        pass

    class Conv:
        def __init__(self, name):
            self.name, self.l = name, int(name[-1])

        def take(self, x, place):
            self.x = Taps(x.home.reshape((-1,) + x.shape[-2:]), place, 1)

    class Split:
        def __init__(self, names):
            self.names = names
            for place, name in enumerate(names):
                convs[name].split, convs[name].place_x = self, place

        def go(self):
            members = [convs[name] for name in self.names]
            out = run(
                functools.partial(split_body, pair_bit),
                (img, *[c.x for c in members]),
                [shape_of((len(members), 2, sizes[members[0].l], 128), LOW)],
                name="split" + "".join(self.names),
            )[0]
            later(self, "got", out, pair_bit)

    class Weights:
        def __init__(self, names):
            self.members, self.name, self.step = [convs[n] for n in names], "".join(names), 0
            self.parts, self.placed = [self], False

        def weigh(self):
            l = self.members[0].l
            args, picks = [], []
            for c in self.members:
                args += [c.x, c.split.got, c.dy, c.meeting.got]
                picks.append((c.place_x, c.place_dy))
            shape = shape_of((images // 4, len(picks), 9, share, 128), LOW)
            self.stay, leave = run(
                functools.partial(pair_weight_body, widths[l], pair_bit, rest, picks),
                (img, *args),
                [shape] * 2,
                scratch=[pltpu.VMEM((sizes[l], 1152), LOW), pltpu.VMEM((256, 1152), F32)],
                name=f"weigh{self.name}",
                away=(0,),
            )
            self.step = 1
            later(self, "got", leave, rest[0])

        def halve(self):
            args = []
            for part in self.parts:
                args += [part.stay, part.got]
            self.step = self.parts[0].step
            self.parts = [self]
            shape = (args[0].shape[0] // 2, len(self.members)) + args[0].shape[2:]
            self.stay, leave = run(
                halve_body,
                args,
                [shape_of(shape), shape_of(shape, LOW)],
                name=f"halve{self.name}_{self.step}",
                away=(0,),
            )
            later(self, "got", leave, rest[self.step], self.step + 1 < len(rest))
            self.step += 1

        def put(self):
            self.placed = True
            places = [PLACES[c.name] for c in self.members]
            first = list(buffers)
            count = len(places)

            def body(*refs):
                stay, got, _, turn, out, value, other, sems = refs[len(first) :]
                load = pltpu.make_async_copy(stay.at[0], other, sems.at[count])
                load.start()
                turn[...] = jnp.zeros_like(turn)
                load.wait()
                copies = []
                for n, place in enumerate(places):
                    value[n] = other[n].astype(F32) + got[0, n].astype(F32)
                    copies.append(pltpu.make_async_copy(value.at[n], out.at[place], sems.at[n]))
                    copies[-1].start()
                for copy in copies:
                    copy.wait()

            stay = self.stay.home
            turn, *buffers[:] = pl.pallas_call(
                body,
                out_shape=[
                    pltpu.VMEM((8, 128), F32),
                    pltpu.HBM((2 * layers, 9, share, 128), F32),
                ],
                in_specs=[hbm] * len(first) + [hbm, vmem, vmem],
                out_specs=[vmem, hbm],
                input_output_aliases={i: i + 1 for i in range(len(first))},
                scratch_shapes=[
                    pltpu.VMEM((count, 9, share, 128), F32),
                    pltpu.VMEM((count, 9, share, 128), stay.dtype),
                    pltpu.SemaphoreType.DMA((count + 1,)),
                ],
                compiler_params=pltpu.CompilerParams(vmem_limit_bytes=VMEM_LIMIT),
                cost_estimate=pl.CostEstimate(flops=0, bytes_accessed=1, transcendentals=0),
                name=f"put{self.name}",
            )(
                *[pltpu.with_memory_space_constraint(v, pltpu.HBM) for v in first],
                pltpu.with_memory_space_constraint(stay, pltpu.HBM),
                self.got,
                TURN.pop(),
            )
            TURN.append(turn)

    hbm, vmem = pl.BlockSpec(memory_space=pltpu.HBM), pl.BlockSpec(memory_space=pltpu.VMEM)
    buffers = []
    PLACES = {"a_0": 0, "b_0": 1, "a_1": 2, "b_1": 3}
    convs = {name: Conv(name) for name in PLACES}

    jobs = {names: Weights(names.split()) for names in ["b_1", "a_1", "b_0", "a_0"]}
    splits = {names: Split(names.split()) for names in ["b_0", "a_0", "b_1 a_1"]}

    def task_weights(l):
        k = kept[l]
        out = run(
            functools.partial(task_weights_body, widths[l]),
            (k.k, k.dys),
            [shape_of((tasks, 9, 512, 128), LOW)],
            scratch=[pltpu.VMEM((sizes[l], 1152), LOW), pltpu.VMEM((512, 1152), F32)],
            name=f"weight_{l}",
            away=(0,),
        )[0]

        def make(total):
            value = out.home if total is None else hold(out.home, total)
            k.task_w = lax.psum_scatter(value, "img", scatter_dimension=2, tiled=True)

        return make

    def meet(names, dys, wait=False):
        for t, name in enumerate(names):
            c = convs[name]
            c.dy = Taps(dys.home.reshape((-1,) + dys.shape[-2:]), t, 1)
            c.meeting, c.place_dy = Meeting(), t if len(names) > 1 else None
        meeting = convs[names[0]].meeting
        for name in names:
            convs[name].meeting = meeting
        if wait:
            later(meeting, "got", dys.home, pair_bit)
        else:
            meeting.got = send_img(dys.home, pair_bit)

    blocks = near_and_far(feats.reshape(n0, 128))
    down_w, up_w = Long(None, down_w), Long(None, up_w)
    wide, narrow, params = run(
        pack_body,
        (down_w, up_w, Long(None, norm_gain), Long(None, norm_shift)),
        [
            shape_of((layers, 2, tasks, 128, 128), LOW),
            shape_of((layers, 6, 128)),
            shape_of((layers, 16, 128)),
        ],
        name="pack",
        away=(2,),
    )
    gains = Rows(params, 0, 8)
    norms = (gains, Rows(params, 8, 16))
    add_last(blocks, TURN[0])
    blocks[0] = Long(None, blocks[0])
    bottles = (Long(None, bottle_gain), Long(None, bottle_shift))
    one.x, one.y1, stats = run(
        functools.partial(first_conv_body, widths[0], 0),
        (own, *blocks, Taps(shared_taps, 0, 1)),
        [shape_of((n0, 512), LOW), shape_of((n0, 128)), stats_of(2)],
        name="conv1_0",
        keep=(1,),
        away=(0,),
    )
    wides, narrows = near_and_far(hold(wide, stats)), near_and_far(hold(narrow, stats))
    scales = jnp.stack([seg_mask, depth_mask, jnp.ones_like(seg_mask)]).astype(F32)
    dq = (task_cot.astype(F32) * scales[..., None]).reshape(tasks, n1 // 4, 128)
    dq, dx = Long(dq), Long(shared_cot.astype(F32).reshape(n1 // 4, 128))
    convs["a_0"].take(one.x, 0)
    one.raw1 = total_of(
        stats, "total1_0", [splits["a_0"].go], (wides, narrows), [params]
    )
    one.row1 = 0
    low, one.g = run(
        functools.partial(first_act_body, counts[0]),
        (one.y1, one.raw1, *norms),
        [shape_of((n0, 128), LOW)] * 2,
        name="act1_0",
        away=(1,),
    )
    blocks = gather_ch(low)
    down_all, up_all, gates = run(
        unpack_body,
        (own, *wides, *narrows),
        [
            shape_of((layers, tasks, 512, 128), LOW),
            shape_of((layers, tasks, 128, 512), LOW),
            shape_of((layers, 6, 512)),
        ],
        name="unpack",
        keep=(0,),
        away=(1, 2),
        save=(dq, dx),
    )
    one.x2, one.y2, one.p, stats = run(
        functools.partial(second_conv_body, widths[0], 0),
        (own, *blocks, Taps(shared_taps, 1, 1), down_all),
        [shape_of((n0, 512), LOW), shape_of((n0, 128)), shape_of((tasks, n0, 128)), stats_of(8)],
        name="conv2_0",
        keep=(1, 2),
        away=(0,),
    )
    one.raw2 = total_of(stats, "total2_0", ahead=[params, up_all, *bottles])

    def hidden(l):
        k, n = kept[l], sizes[l]
        body = functools.partial(hidden_body, l, counts[l], widths[l])
        outs = [shape_of((tasks, n, 128), LOW)]
        if l == 0:

            def inner(y, p, raw, gain, shift, bgain, bshift, up, s, u, zstats, scratch):
                body(y, p, raw, gain, shift, bgain, bshift, up, s, u, None, zstats, scratch)

            outs += [shape_of((n + n // 4, 128), LOW), shape_of((6, 512))]
        else:
            inner = body
            outs += [shape_of((n, 128), LOW), shape_of((n // 4, 128), LOW), stats_of(6, 512)]
        return run(
            inner,
            (k.y2, k.p, k.raw2, *norms, *bottles, up_all),
            outs,
            scratch=[pltpu.VMEM((n, 128), F32)],
            name=f"hidden_{l}",
            keep=(0,),
        )

    def task_convs(l, u_blocks, taps, more=None):
        k, n = kept[l], sizes[l]
        body = functools.partial(task_conv_body, l, counts[l], widths[l])
        args = (own, k.s, up_all, *u_blocks, k.zraw, gates, taps)
        if more is None:

            def inner(ch, s, up, u0, u1, u2, u3, zraw, gt, taps, kk, y, stats, full, acc):
                body(ch, s, up, u0, u1, u2, u3, zraw, gt, taps, None, kk, y, stats, full, acc)

        else:
            inner = body
            args += (more,)
        return run(
            inner,
            args,
            [
                shape_of((tasks, n, 512), LOW),
                shape_of((tasks, n, 128)),
                stats_of(6 if more is None else 8),
            ],
            scratch=[pltpu.VMEM((n, 512), LOW), pltpu.VMEM((tasks, 2, 128), F32)],
            name=f"taskconv_{l}",
            keep=(1,),
            away=(0,),
        )

    one.s, u, zstats = hidden(0)
    u_blocks = near_and_far(u)

    def next_conv():
        two.x, two.y1, two.more = run(
            functools.partial(next_conv_body, widths[1], 0, n0),
            (own, *u_blocks, Taps(shared_taps, 2, 1)),
            [shape_of((n1, 512), LOW), shape_of((n1, 128)), shape_of((2, 128))],
            name="conv1_1",
            away=(0, 1),
        )

    convs["b_0"].take(one.x2, 0)
    taps = Taps(task_taps, 0, tasks)
    one.zraw = total_by_pairs(
        zstats, "totalz_0", [], [next_conv], (u_blocks,), [up_all, gates, taps]
    )
    one.k, one.yt, stats = task_convs(0, u_blocks, taps, two.more)
    one.traw = total_of(
        stats, "totalt_0", [splits["b_0"].go], ahead=[params, down_w, two.y1]
    )
    two.raw1, two.row1 = one.traw, 6

    low, two.g, part = run(
        functools.partial(attend_body, counts[0], counts[1], widths[0]),
        (one.yt, two.y1, one.traw, *norms, down_w),
        [
            shape_of((n1, 128), LOW),
            shape_of((tasks, n1, 128), LOW),
            shape_of((tasks, n1, 128), LOW),
        ],
        scratch=[pltpu.VMEM((n0, 128), F32)],
        name="attend_1",
        away=(1,),
    )

    def sum_ch(value, name):
        got = lax.ppermute(value, "ch", CORE)
        near = run(pair_body, (value, got), [shape_of(value.shape, LOW)], name=name)[0]
        return near, lax.ppermute(near, "ch", CHIP)

    blocks = gather_ch(low)
    halves = sum_ch(part, "pairp_1")
    two.x2, two.y2, two.p, stats = run(
        functools.partial(second_conv_next_body, widths[1], 0),
        (own, *blocks, Taps(shared_taps, 3, 1), *halves),
        [shape_of((n1, 512), LOW), shape_of((n1, 128)), shape_of((tasks, n1, 128)), stats_of(8)],
        name="conv2_1",
        keep=(1, 2),
        away=(0,),
    )
    two.raw2 = total_of(stats, "total2_1", ahead=[params, up_all, *bottles])
    convs["a_1"].take(two.x, 0)
    convs["b_1"].take(two.x2, 0)
    two.s, u, shared_out, zstats = hidden(1)
    u_blocks = near_and_far(u)
    taps = Taps(task_taps, tasks, tasks)
    two.zraw = total_of(zstats, "totalz_1", mid=(u_blocks,))
    two.k, two.yt, stats = task_convs(1, u_blocks, taps)
    two.traw = total_of(stats, "totalt_1")

    task_out, d, stats = run(
        functools.partial(task_last_body, 1, counts[1], widths[1]),
        (two.yt, two.traw, *norms, dq),
        [shape_of((tasks, n1 // 4, 128), LOW), shape_of((tasks, n1, 128)), stats_of(6)],
        scratch=[pltpu.VMEM((n1, 128), F32)],
        name="tasklast_1",
    )
    taps = Taps(task_taps, tasks, tasks)
    two.dtraw = total_of(
        stats,
        "dtotalt_1",
        [splits["b_1 a_1"].go],
    )
    two.dtrow = 0

    def back_outs(n, lead=()):
        return [
            shape_of(lead + (n, 128), LOW),
            shape_of((2,) + lead + (n, 128), LOW),
            shape_of(lead + (n, 128)),
            shape_of(lead + (n, 128)),
        ]

    def back_scratch(n):
        return [pltpu.VMEM((n, 1152), LOW), pltpu.VMEM((n, 512), F32)]

    def scatter_ch(send, keep, far, name, away=()):
        near, part = run(
            pair_second_body,
            (keep, far, lax.ppermute(send, "ch", CORE)),
            [shape_of(far.shape, LOW), shape_of(far.shape)],
            name=name,
            away=away,
        )
        return (part, lax.ppermute(near, "ch", CHIP))

    def steps(weigh="", halve="", split="", put=""):
        kinds = ((jobs, weigh, "weigh"), (jobs, halve, "halve"))
        kinds += ((splits, split, "go"), (jobs, put, "put"))
        return [
            getattr(table[name], kind)
            for table, names, kind in kinds
            for name in names.split(", ")
            if name
        ]

    def put_ready(names):
        for name in names:
            if jobs[name].step == len(rest) and not jobs[name].placed:
                jobs[name].put()

    flat = []

    def flatten():
        rows = run(
            flat_body,
            [part for k in kept for part in k.both],
            [shape_of((images, layers * 2 * tasks * 128 // images, 128), LOW)],
            name="flat",
        )[0]
        flat.append(rows)

    plan = {
        "gate_1": (),
        "bottle_1": (),
        "first_1": steps("b_1"),
        "gate_0": steps("a_1", "b_1"),
        "bottle_0": steps("", "a_1"),
        "first_0": steps("b_0") + [lambda: put_ready(["b_1"]), flatten],
    }
    unfinished = None

    for l in range(layers - 1, -1, -1):
        k, n, w, count = kept[l], sizes[l], widths[l], counts[l]
        dys, send, keep, far = run(
            functools.partial(task_back_body, l, count, w, k.dtrow),
            (own, d, k.yt, k.traw, k.dtraw, gains, taps),
            back_outs(n, (tasks,)),
            scratch=back_scratch(n),
            name=f"taskback_{l}",
            away=(0,),
        )
        k.dys = dys
        if unfinished is None:
            parts = scatter_ch(send, keep, far, f"pairr_{l}")
            rest_dx = dx
        else:
            send_x, keep_x, far_x = unfinished
            near, part, rest_dx = run(
                pair_tasks_body,
                (
                    keep,
                    far,
                    lax.ppermute(send, "ch", CORE),
                    keep_x,
                    far_x,
                    lax.ppermute(send_x, "ch", CORE),
                ),
                [
                    shape_of((tasks * n + sizes[l + 1], 128), LOW),
                    shape_of((tasks, n, 128)),
                    shape_of((sizes[l + 1], 128)),
                ],
                name=f"pairr_{l}",
            )
            parts = (part, lax.ppermute(near, "ch", CHIP))
        make_weights = task_weights(l)

        def gate_grad(ch, part, far, s, up, zraw, y, raw, gain, shift, dx, *rest, first=unfinished, l=l, w=w):
            more = (dx,) if first is None else (dx, far)
            gate_grad_body(l, counts[l], w, ch, part, far, s, up, zraw, y, raw, gain, shift, more, *rest)

        d, d2, stats = run(
            gate_grad,
            (own, *parts, k.s, up_w, k.zraw, k.y2, k.raw2, *norms, rest_dx),
            [shape_of((tasks, n, 128)), shape_of((n, 128)), stats_of(8)],
            scratch=[pltpu.VMEM((n, 128), F32)],
            name=f"gategrad_{l}",
        )
        if l == 0:
            held.append(make_weights)
        else:
            make_weights(stats)
        k.draw2 = total_of(
            stats, f"dtotal2_{l}", plan[f"gate_{l}"], ahead=[k.s, up_w, k.zraw, params]
        )
        d2 = Long(d2)
        ds, dup = run(
            functools.partial(hidden_grad_body, l, count),
            (own, d, k.s, up_w, k.zraw, k.draw2, gains),
            [shape_of((tasks, n, 128), LOW), shape_of((tasks, 128, 128), LOW)],
            name=f"hiddengrad_{l}",
            away=(1,),
            save=(d2,),
        )
        k.dup = dup
        got = lax.ppermute(ds, "ch", CORE)
        near = run(pair_body, (ds, got), [shape_of(ds.shape, LOW)], name=f"pairs_{l}")[0]
        halves = near, lax.ppermute(near, "ch", CHIP)

        def conv2_back(ch, d, y, raw, draw, gain, taps, *rest, l=l, count=count, w=w):
            conv_back_body(l, 1, count, w, ch, d, y, raw, 0, draw, gain, taps, *rest)

        dys, send, keep, far = run(
            conv2_back,
            (own, d2, k.y2, k.raw2, k.draw2, gains, Taps(shared_taps, 2 * l + 1, 1)),
            back_outs(n),
            scratch=back_scratch(n),
            name=f"conv2back_{l}",
            away=(0,),
        )
        meet([f"b_{l}"], dys)
        parts = scatter_ch(send, keep, far, f"pairv_{l}", (1,))

        def make_dv(k=k, parts=parts, n=n, l=l):
            k.dv = run(mixed_body, parts, [shape_of((n, 128))], name=f"dv_{l}")[0]

        gap(plan.get(f"hidden_{l}", ()))
        d, stats = run(
            functools.partial(bottle_grad_body, l, count),
            (*halves, k.p, k.raw2, *bottles),
            [shape_of((tasks, n, 128)), stats_of(6)],
            name=f"bottlegrad_{l}",
        )
        wanted = [k.p, k.raw2, bottles[0], k.g, down_w, k.y1, k.raw1, params]
        if l > 0:
            wanted += [kept[l - 1].yt, kept[l - 1].traw]
        k.draw3 = total_of(stats, f"dtotal3_{l}", [make_dv, *plan[f"bottle_{l}"]])
        args = (d, k.p, k.raw2, k.draw3, bottles[0], k.g, down_w, k.dv, k.y1, k.raw1, *norms)
        outs = [shape_of((tasks, 128, 128), LOW), shape_of((n, 128))]
        if l > 0:
            ddown, d1, stats, d = run(
                functools.partial(
                    attend_grad_first_body, l, count, k.row1, counts[l - 1], widths[l - 1]
                ),
                args + (kept[l - 1].yt, kept[l - 1].traw),
                outs + [stats_of(8), shape_of((tasks, sizes[l - 1], 128))],
                scratch=[pltpu.VMEM((sizes[l - 1], 128), F32)],
                name=f"attendgrad_{l}",
                away=(0,),
            )
        else:
            ddown, d1, stats = run(
                functools.partial(attend_grad_last_body, l, count, k.row1),
                args,
                outs + [stats_of(2)],
                name=f"attendgrad_{l}",
                away=(0,),
            )
        k.both = [ddown, k.dup]
        last_taps = Taps(shared_taps, 2 * l, 1)
        wanted = [k.y1, k.raw1, params, last_taps]
        if l > 0:
            taps = Taps(task_taps, tasks * (l - 1), tasks)
            wanted.append(taps)
        k.draw1 = total_of(stats, f"dtotal1_{l}", plan[f"first_{l}"], ahead=wanted if l == 0 else ())
        if l > 0:
            kept[l - 1].dtraw, kept[l - 1].dtrow = k.draw1, 2
            d1 = Long(d1)

        def conv1_back(ch, d, y, raw, draw, gain, taps, *rest, l=l, count=count, w=w, row=k.row1):
            conv_back_body(l, 0, count, w, ch, d, y, raw, row, draw, gain, taps, *rest)

        dys, send, keep, far = run(
            conv1_back,
            (own, d1, k.y1, k.raw1, k.draw1, gains, last_taps),
            back_outs(n),
            scratch=back_scratch(n),
            name=f"conv1back_{l}",
            away=(0,),
        )
        meet([f"a_{l}"], dys)

        unfinished = (send, keep, far)

    parts = scatter_ch(*unfinished, "pairx_0")
    every = ["b_1", "a_1", "b_0", "a_0"]

    flat[0] = swap_img(hold(flat[0], parts[0]))
    put_ready(every[:1])
    gap(steps("a_0"))
    gap(steps("", "b_0"))
    flat = run(spread_sum_body, flat, [shape_of(flat[0].shape, LOW)], name="spread")[0]
    flat = swap_img(flat)
    dx = run(mixed_body, parts, [shape_of((n0, 128))], name="dx_0", away=(0,))[0].home
    put_ready(every[1:2])
    gap(steps("", "a_0"))
    tw = run(
        widen_body,
        [Long(None, k.task_w) for k in kept],
        [shape_of((tasks * layers, 9, share, 128))],
        name="tasksout",
        away=(0,),
    )[0].home

    order, places = [], []
    for k in kept:
        base = len(places)
        places += [k.draw1, k.draw2, k.dtraw, k.draw3]
        rows = [(base, 0), (base + 1, 0)]
        rows += [(base + 2, k.dtrow + 2 * t) for t in range(3)]
        rows += [(base + 1, 2 + 2 * t) for t in range(3)]
        rows += [(base + 3, 2 * t) for t in range(3)]
        order.append(rows)

    def norms_body(*refs):
        finish_body(order, refs[: len(places)], *refs[len(places) :])

    gains = run(
        norms_body,
        places,
        [shape_of((layers, 8, 128))] * 2 + [shape_of((layers, tasks, 128))] * 2,
        name="norms",
    )
    while any(jobs[name].step < len(rest) for name in every):
        for name in every:
            if jobs[name].step < len(rest):
                gap([jobs[name].halve])
    flat = hold(flat, TURN[0])
    put_ready(every)
    flat = flat.reshape(layers, 2, tasks, 128, 128).astype(F32)
    down, up = flat[:, 0], flat[:, 1]
    (sw,) = buffers
    return (
        shared_out.reshape(1, widths[1] // 2, widths[1] // 2, 128),
        task_out.reshape(tasks, 1, widths[1] // 2, widths[1] // 2, 128),
        dx.reshape(1, widths[0], widths[0], 128),
        sw.reshape(layers, 2, 3, 3, share, 128),
        tw.reshape(layers, tasks, 3, 3, share, 128),
        down,
        up,
        *gains,
    )


def solution(mesh):
    placed = (
        P("img", None, None, "ch"),
        P(None, None, None, None, None, "ch"),
        P(None, None, None, None, None, "ch"),
        P(None, None, "ch", None),
        P(None, None, None, "ch"),
        P(None, None, "ch"),
        P(None, None, "ch"),
        P(),
        P(),
        P("img", None, None),
        P("img", None, None),
        P("img", None, None, "ch"),
        P(None, "img", None, None, "ch"),
    )
    return jax.shard_map(
        on_device,
        mesh=mesh,
        in_specs=placed,
        out_specs=(
            P("img", None, None, "ch"),
            P(None, "img", None, None, "ch"),
            P("img", None, None, "ch"),
            P(None, None, None, None, "img", "ch"),
            P(None, None, None, None, "img", "ch"),
            P(None, None, "ch", None),
            P(None, None, None, "ch"),
            P(None, None, "ch"),
            P(None, None, "ch"),
            P(),
            P(),
        ),
        check_vma=False,
    )
```
